32 devices in a mesh: batch: 4 (over z), seq: 8 (over y, x, core).
Axes of the slice: x: 2, y: 2, z: 4, core: 2. Of those that a mesh axis runs over, the one named last changes fastest.
Arguments:
- hidden: bfloat16 [16, 1024, 768], P('batch', 'seq'), may hold values from -6 to 6
- char_ids: int32 [16, 4096], P('batch', 'seq'), may hold values from 0 to 255
- group_ids: int32 [16], P('batch'), may hold values from 0 to 3
- word_lengths: int32 [16, 8, 128], P('batch', 'seq'), may hold values from 1 to 8, 512 in all within a row
- qkv_weight: bfloat16 [768, 2304], P('seq'), may hold values from -0.21875 to 0.21875
- out_weight: bfloat16 [768, 768], P('seq'), may hold values from -6 to 6
- up_weight: bfloat16 [768, 3072], P('seq'), may hold values from -0.21875 to 0.21875
- ffn_bias: bfloat16 [3072], P('seq'), may hold values from -3 to 3
- down_weight: bfloat16 [3072, 768], P('seq'), may hold values from -0.109375 to 0.109375
- gru_weight: bfloat16 [768, 1536], P('seq'), may hold values from -0.21875 to 0.21875
- gate_bias: bfloat16 [768], P('seq'), may hold values from -14 to -3
- candidate_bias: bfloat16 [768], P('seq'), may hold values from -3 to 3
- char_weight: bfloat16 [768, 768], P('seq'), may hold values from -1.25 to 1.25
- conv_weight: bfloat16 [3, 1536, 1536], P(None, 'seq'), may hold values from -0.09375 to 0.09375
- char_table: bfloat16 [1024, 768], P('seq'), may hold values from -6 to 6
- norm_gain: bfloat16 [768, 4], P('seq'), may hold values from 0.099609375 to 1.8984375
- norm_shift: bfloat16 [768, 4], P('seq'), may hold values from -3 to 3
- tok_grad: bfloat16 [16, 1024, 768], P('batch', 'seq'), may hold values from -6 to 6
- char_grad: bfloat16 [16, 1024, 768], P('batch', 'seq'), may hold values from -6 to 6
Outputs:
- tok_out: float32 [16, 1024, 768], P('batch', 'seq')
- char_out: float32 [16, 1024, 768], P('batch', 'seq')
- hidden_grad: float32 [16, 1024, 768], P('batch', 'seq')
- qkv_weight_grad: float32 [768, 2304], P('seq')
- out_weight_grad: float32 [768, 768], P('seq')
- up_weight_grad: float32 [768, 3072], P('seq')
- ffn_bias_grad: float32 [3072], P('seq')
- down_weight_grad: float32 [3072, 768], P('seq')
- gru_weight_grad: float32 [768, 1536], P('seq')
- gate_bias_grad: float32 [768], P('seq')
- candidate_bias_grad: float32 [768], P('seq')
- char_weight_grad: float32 [768, 768], P('seq')
- conv_weight_grad: float32 [3, 1536, 1536], P(None, 'seq')
- char_table_grad: float32 [1024, 768], P('seq')
- norm_gain_grad: float32 [768, 4], P('seq')
- norm_shift_grad: float32 [768, 4], P('seq')
The draws below stay inside these ranges and needn't reach their ends.
Inputs may be any that keep to these rules, and one draw needn't show every extreme that they name: `word_lengths`: within each block of 128 tokens (one sequence on one device) the lengths sum to exactly 512.
All inputs are finite; a program needn't handle non-finite values.
Results may differ from the reference program's by a relative error of at most 0.02.
Values may be sent and summed in bfloat16 or wider, within the bound.
No kernel may reach another device: no remote copies, remote signals or barrier semaphores. Data moves between devices by JAX's collectives and lax.ppermute only.
A program may use at most 320 MiB of HBM per device.

```python
import math
import jax
import jax.numpy as jnp
import numpy as np
from jax import lax

D = 768
HEADS = 12
FF = 3072
NCHAR = 256
GROUPS = 4
TOK_DEV = 128
HEAD_DIM = 64
CH_DEV = 512
SEQS = 16
SEQ_LEN = 1024
CHARS = 4096
N_SEQ = 8


def with_ends(array, rng, least, high):
    spot = [jax.random.randint(jax.random.fold_in(rng, axis), (), 0, length) for axis, length in enumerate(array.shape)]
    longest = array.shape.index(max(array.shape))
    beside = spot[:longest] + [(spot[longest] + 1) % array.shape[longest]] + spot[longest + 1:]
    return array.at[tuple(spot)].set(least).at[tuple(beside)].set(high)


def block_levels(stream_key, shape, cuts, smallest, largest):
    loudness, own = 1.0, jax.random.fold_in(stream_key, 6)
    for axis_at, shards_of in cuts:
        steps = jnp.exp(jax.random.uniform(jax.random.fold_in(own, axis_at), (shards_of,), jnp.float32, smallest / len(cuts), largest / len(cuts)))
        loudness = loudness * jnp.repeat(steps, shape[axis_at] // shards_of).reshape([-1 if axis == axis_at else 1 for axis in range(len(shape))])
    return loudness


def length_profile(count, total, most, lean):
    loads = [(1 << 20) // math.isqrt(rank ** lean) + 1 for rank in range(2, count + 1)]
    spare, counts = total - most - (count - 1), [1] * (count - 1)
    while spare > 0:
        free = [i for i in range(count - 1) if counts[i] < most]
        pool, left = sum([loads[i] for i in free]), spare
        for i in free:
            addition = min(most - counts[i], max(1, left * loads[i] // pool), spare)
            counts[i] = counts[i] + addition
            spare = spare - addition
    return np.array([most] + counts)


def ragged(key, number_of, total, reach, slope):
    if number_of == 2:
        one = jax.random.randint(key, (), max(1, total - reach), min(reach, total - 1) + 1)
        return jnp.stack([one, total - one])
    sizes = jnp.asarray(length_profile(number_of, total, reach, slope), jnp.int32)
    couples = (number_of - 1) // 2
    source_of, taker = sizes[1:1 + 2 * couples:2], sizes[2:2 + 2 * couples:2]
    slack = jnp.minimum(source_of - 1, reach - taker)
    moved = jax.random.randint(jax.random.fold_in(key, 1), (couples,), 0, 1 << 20) % (slack + 1)
    sizes = sizes.at[1:1 + 2 * couples:2].set(source_of - moved).at[2:2 + 2 * couples:2].set(taker + moved)
    return sizes[jax.random.permutation(jax.random.fold_in(key, 2), number_of)]


def noise(key, dims, deviation, bound, split=(), held_as=jnp.bfloat16):
    values = deviation * jax.random.normal(key, dims, jnp.float32)
    if split:
        values = values * block_levels(key, dims, split, -0.22, 0.18)
    return jnp.clip(values, -bound, bound).astype(held_as)


def setup_inputs(seed: int = 0) -> dict:
    key_list = jax.random.split(jax.random.key(seed), 20)
    return {
        "hidden": noise(key_list[0], (SEQS, SEQ_LEN, D), 1.0, 6.0, ((0, 4), (1, 8))),
        "char_ids": with_ends(jax.random.randint(key_list[1], (SEQS, CHARS), 0, NCHAR), jax.random.fold_in(key_list[1], 1), 0, NCHAR - 1).astype(jnp.int32),
        "group_ids": with_ends(jax.random.randint(key_list[2], (SEQS,), 0, GROUPS), jax.random.fold_in(key_list[2], 1), 0, GROUPS - 1).astype(jnp.int32),
        "word_lengths": jax.vmap(lambda own: ragged(own, TOK_DEV, CH_DEV, 8, 1))(jax.random.split(key_list[3], SEQS * N_SEQ)).reshape((SEQS, N_SEQ, TOK_DEV)).astype(jnp.int32),
        "qkv_weight": noise(key_list[4], (D, 3 * D), D ** -0.5, 0.21875, ((0, 8),)),
        "out_weight": noise(key_list[5], (D, D), 1.0, 6.0, ((0, 8),)),
        "up_weight": noise(key_list[6], (D, FF), D ** -0.5, 0.21875, ((0, 8),)),
        "ffn_bias": noise(key_list[7], (FF,), 0.5, 3.0, ((0, 8),)),
        "down_weight": noise(key_list[8], (FF, D), FF ** -0.5, 0.109375, ((0, 8),)),
        "gru_weight": noise(key_list[9], (D, 2 * D), D ** -0.5, 0.21875, ((0, 8),)),
        "gate_bias": jnp.clip(-14.0 + 11.0 * jax.random.uniform(key_list[10], (D,), jnp.float32) ** block_levels(key_list[10], (D,), ((0, 8),), -0.2, 0.2), -14.0, -3.0).astype(jnp.bfloat16),
        "candidate_bias": noise(key_list[11], (D,), 0.5, 3.0, ((0, 8),)),
        "char_weight": noise(key_list[12], (D, D), (D // 32) ** -0.5, 1.25, ((0, 8),)),
        "conv_weight": noise(key_list[13], (3, 2 * D, 2 * D), (6 * D) ** -0.5, 0.09375, ((1, 8),)),
        "char_table": noise(key_list[14], (GROUPS * NCHAR, D), 1.0, 6.0, ((0, 8),)),
        "norm_gain": jnp.clip(1.0 + 0.18 * jax.random.normal(key_list[15], (D, 4), jnp.float32), 0.099609375, 1.8984375).astype(jnp.bfloat16),
        "norm_shift": noise(key_list[16], (D, 4), 0.5, 3.0, ((0, 8),)),
        "tok_grad": noise(key_list[17], (SEQS, SEQ_LEN, D), 1.0, 6.0, ((0, 4), (1, 8))),
        "char_grad": noise(key_list[18], (SEQS, SEQ_LEN, D), 1.0, 6.0, ((0, 4), (1, 8))),
    }


@jax.custom_vjp
def low(v):
    return lax.optimization_barrier(v.astype(jnp.bfloat16)).astype(jnp.float32)

@jax.custom_vjp
def low_back(v):
    return v

def low_keep(v):
    return (low(v), None)

def low_pass(kept, grad):
    return (grad,)

def back_keep(v):
    return (v, None)

def back_low(kept, grad):
    return (low(grad),)
low.defvjp(low_keep, low_pass)
low_back.defvjp(back_keep, back_low)
NORM_EPS = 1e-06
HIGH = lax.Precision.HIGHEST

def product(left, right):
    return jnp.dot(left, right, precision=HIGH)

def layer_norm(values, gains, shifts):
    center = values - lax.optimization_barrier(jnp.mean(values, -1, keepdims=True))
    spread = lax.optimization_barrier(jnp.mean(center * center, -1, keepdims=True))
    return center * lax.rsqrt(spread + NORM_EPS) * gains + shifts

def affine(earlier, latter):
    return (earlier[0] * latter[0], latter[0] * earlier[1] + latter[1])

def layer(params, hidden, table_rows, word_lens):
    qkv_w, out_w, up_w, ffn_b, down_w, gru_w, gate_b, cand_b, char_w, conv_w, table, gains, shifts = params
    half_width = D // 2
    projected = low_back(product(hidden, qkv_w))
    queries = low(projected[:, :D]).reshape(SEQ_LEN, HEADS, HEAD_DIM)
    keys_part = low(projected[:, D:2 * D]).reshape(SEQ_LEN, HEADS, HEAD_DIM)
    values_part = low(projected[:, 2 * D:]).reshape(SEQ_LEN, HEADS, HEAD_DIM)
    block_rows = math.gcd(SEQ_LEN, 512)
    score_scale = HEAD_DIM ** (-0.5)

    def attend(block_index):
        query_block = lax.dynamic_slice_in_dim(queries, block_index * block_rows, block_rows, 0)
        scores = low_back(jnp.einsum('qhe,khe->hqk', query_block, keys_part, precision=HIGH) * score_scale)
        probability = jax.nn.softmax(scores, axis=-1)
        return jnp.einsum('hqk,khe->qhe', low(probability), values_part, precision=HIGH)
    mixture = lax.map(jax.checkpoint(attend), jnp.arange(SEQ_LEN // block_rows, dtype=jnp.int32))
    mixture = low_back(mixture.reshape(SEQ_LEN, D))
    attended = low_back(product(low(mixture), out_w))
    normed_a = layer_norm(hidden + attended, gains[:, 0], shifts[:, 0])
    up_proj = low_back(product(low(normed_a), up_w) + ffn_b)
    ffn_out = low_back(product(low(jax.nn.gelu(up_proj, approximate=False)), down_w))
    ffn_norm = layer_norm(normed_a + ffn_out, gains[:, 1], shifts[:, 1])
    embedded = low_back(jnp.take(table, table_rows, axis=0))
    bias_all = jnp.concatenate([gate_b[:half_width], cand_b[:half_width], gate_b[half_width:], cand_b[half_width:]])
    gate_input = low_back(product(embedded, gru_w) + bias_all)
    update_fwd = jax.nn.sigmoid(gate_input[:, :half_width])
    cand_fwd = jnp.tanh(gate_input[:, half_width:2 * half_width])
    update_rev = jax.nn.sigmoid(gate_input[:, 2 * half_width:3 * half_width])
    cand_rev = jnp.tanh(gate_input[:, 3 * half_width:])
    ignored_f, state_fwd = lax.associative_scan(affine, (1.0 - update_fwd, update_fwd * cand_fwd), axis=0)
    ignored_r, state_rev = lax.associative_scan(affine, (1.0 - update_rev, update_rev * cand_rev), axis=0, reverse=True)
    states = low(jnp.concatenate([state_fwd, state_rev], -1))
    word_ends = jnp.cumsum(word_lens).astype(jnp.int32)
    char_place = jnp.arange(CHARS, dtype=jnp.int32)
    owner_token = lax.optimization_barrier(jnp.sum((word_ends[None, :] <= char_place[:, None]).astype(jnp.int32), 1)).astype(jnp.int32)
    summed = low_back(jax.ops.segment_sum(states, owner_token, num_segments=SEQ_LEN))
    pooled = low(summed / word_lens[:, None].astype(jnp.float32))
    char_proj = low_back(product(pooled, char_w))
    joined = low(jnp.concatenate([ffn_norm, char_proj], -1))
    padded = jnp.pad(joined, ((1, 1), (0, 0)))
    merged = low_back(product(padded[:-2], conv_w[0]) + product(padded[1:-1], conv_w[1]) + product(padded[2:], conv_w[2]))
    tok_out = layer_norm(ffn_norm + merged[:, :D], gains[:, 2], shifts[:, 2])
    char_out = layer_norm(char_proj + merged[:, D:], gains[:, 3], shifts[:, 3])
    return (tok_out, char_out)

def reference(hidden, char_ids, group_ids, word_lengths, qkv_weight, out_weight, up_weight, ffn_bias, down_weight, gru_weight, gate_bias, candidate_bias, char_weight, conv_weight, char_table, norm_gain, norm_shift, tok_grad, char_grad):
    params = tuple((weight.astype(jnp.float32) for weight in (qkv_weight, out_weight, up_weight, ffn_bias, down_weight, gru_weight, gate_bias, candidate_bias, char_weight, conv_weight, char_table, norm_gain, norm_shift)))

    def per_sequence(running, record):
        seq_hidden, seq_chars, seq_group, seq_lengths, seq_tok_grad, seq_char_grad = record
        table_rows = (seq_group * NCHAR + seq_chars).astype(jnp.int32)
        word_lens = seq_lengths.reshape(SEQ_LEN).astype(jnp.int32)

        def forward(weights, inputs):
            return layer(weights, inputs, table_rows, word_lens)
        results, pullback = jax.vjp(forward, params, seq_hidden.astype(jnp.float32))
        weight_grads, input_grad = pullback((seq_tok_grad.astype(jnp.float32), seq_char_grad.astype(jnp.float32)))
        running = jax.tree.map(jnp.add, running, weight_grads)
        return (running, (results[0], results[1], input_grad))
    zeros_init = jax.tree.map(jnp.zeros_like, params)
    totals, outputs = lax.scan(per_sequence, zeros_init, (hidden, char_ids, group_ids, word_lengths, tok_grad, char_grad))
    return (outputs[0], outputs[1], outputs[2], totals[0], totals[1], totals[2], totals[3], totals[4], totals[5], totals[6], totals[7], totals[8], totals[9], totals[10], totals[11], totals[12])
```

```python
import functools

import jax
import jax.numpy as jnp
from jax import lax
from jax.experimental import pallas as pl
from jax.experimental.pallas import tpu as pltpu
from jax.sharding import PartitionSpec as P

HEADS = 12
NCHAR = 256
NORM_EPS = 1e-06
LANES = 128
SMALL_ROWS = 16
RIDE = 32
SCALE = 1000
F32 = jnp.float32
BF16 = jnp.bfloat16
VMEM_BYTES = 60 << 20


def dot(left, right, left_dim, right_dim):
    return lax.dot_general(
        left, right, (((left_dim,), (right_dim,)), ((), ())), preferred_element_type=F32
    )


def params(grid_rank):
    return pltpu.CompilerParams(
        dimension_semantics=("arbitrary",) * grid_rank, vmem_limit_bytes=VMEM_BYTES
    )


def shape(dims, dtype):
    return jax.ShapeDtypeStruct(dims, dtype)


def whole(dims):
    return pl.BlockSpec(dims, lambda *_: (0,) * len(dims))


def cost(flops, nbytes):
    return pl.CostEstimate(flops=int(flops) * SCALE, bytes_accessed=int(nbytes) * SCALE, transcendentals=0)


LATEST = []


def launch(
    body, grid, prefetch, inputs, in_specs, out_specs, out_shape, scratch, price, name, carry=()
):
    deps = LATEST[-1:]
    single = not isinstance(out_shape, (list, tuple))
    outs = [out_shape] if single else list(out_shape)
    specs = [out_specs] if single else list(out_specs)
    lead = len(prefetch) + len(inputs)
    extra = len(carry) + len(deps)
    anywhere = pl.BlockSpec(memory_space=pl.ANY)

    def kernel(*refs):
        own = refs[lead + extra :]
        body(*refs[:lead], *own[: len(outs)], *own[len(outs) + len(carry) :])

    results = pl.pallas_call(
        kernel,
        grid_spec=pltpu.PrefetchScalarGridSpec(
            num_scalar_prefetch=len(prefetch),
            grid=grid,
            in_specs=list(in_specs) + [anywhere] * extra,
            out_specs=specs + [anywhere] * len(carry),
            scratch_shapes=scratch,
        ),
        out_shape=outs + [shape(v.shape, v.dtype) for v in carry],
        input_output_aliases={lead + i: len(outs) + i for i in range(len(carry))},
        compiler_params=params(len(grid)),
        cost_estimate=price,
        name=name,
    )(*prefetch, *inputs, *carry, *deps)
    LATEST[:] = results[len(outs) - 1 : len(outs)]
    return results[0] if len(results) == 1 else results


def flat_block(ref):
    block = ref[...]
    return block.reshape(block.shape[0] * block.shape[1], block.shape[2])


def norm_forward(values):
    center = values - jnp.mean(values, -1, keepdims=True)
    rstd = lax.rsqrt(jnp.mean(center * center, -1, keepdims=True) + NORM_EPS)
    return center * rstd, rstd


def norm_backward(normal, rstd, gain, gradient):
    scaled = gradient * gain
    first = jnp.mean(scaled, -1, keepdims=True)
    second = jnp.mean(scaled * normal, -1, keepdims=True)
    return rstd * (scaled - first - normal * second)


def column_sum(values):
    return jnp.sum(values, 0, keepdims=True)


def gelu_parts(values):
    size = jnp.abs(values) * 0.7071067811865476
    bell = jnp.exp(-size * size)
    t = 1.0 / (1.0 + 0.3275911 * size)
    series = t * (
        0.254829592
        + t * (-0.284496736 + t * (1.421413741 + t * (-1.453152027 + t * 1.061405429)))
    )
    tail = 0.5 * series * bell
    phi_sum = jnp.where(values < 0, tail, 1.0 - tail)
    return values * phi_sum, phi_sum + values * (bell * 0.3989422804014327)


def qkv_kernel(seqs, toks, per, x_ref, w_ref, o_ref):
    acc = dot(x_ref[...], flat_block(w_ref), 1, 0)
    turned = acc.T.astype(BF16)
    width = turned.shape[0] // HEADS
    for s in range(seqs):
        for h in range(HEADS):
            pair = s * HEADS + h
            o_ref[pair // per, pair % per, 0] = turned[
                h * width : (h + 1) * width, s * toks : (s + 1) * toks
            ]


def qkv_call(rows, packed, base, seqs, count):
    total, width = rows.shape
    toks = total // seqs
    per = seqs * HEADS // count
    head = width // HEADS
    blk = width // count
    return launch(
        functools.partial(qkv_kernel, seqs, toks, per),
        (3,),
        [],
        [rows, packed],
        [ whole(rows.shape), pl.BlockSpec((count, blk, width), lambda j: (0, base + j, 0)), ],
        pl.BlockSpec((count, per, 1, head, toks), lambda j: (0, 0, j, 0, 0)),
        shape((count, per, 3, head, toks), BF16),
        [],
        cost(6 * total * width * width, 6 * width * width + 8 * total * width),
        "qkv",
    )


def spread(ref, index):
    return jnp.concatenate([ref[(i, *index)] for i in range(ref.shape[0])], axis=1)


def attend_kernel(step, scale, x_ref, o_ref, total_ref):
    queries = spread(x_ref, (0, 0)) * scale
    keys = spread(x_ref, (0, 1)).T
    values = spread(x_ref, (0, 2))
    toks = x_ref.shape[-1]
    for begin in range(0, queries.shape[1], step):
        scores = dot(keys, queries[:, begin : begin + step], 1, 0)
        highest = jnp.max(scores, 0, keepdims=True)
        expo = jnp.exp(scores - highest)
        totals = jnp.sum(expo, 0, keepdims=True)
        mixture = (dot(values, expo.astype(BF16), 1, 0) / totals).astype(BF16)
        total_ref[0, :, begin : begin + step] = highest + jnp.log(totals)
        for at in range(0, step, toks):
            o_ref[(begin + at) // toks, 0] = mixture[:, at : at + toks]


def attend_call(qkv, step):
    count, per, _, head, toks = qkv.shape
    length = count * toks
    scale = head**-0.5
    return launch(
        functools.partial(attend_kernel, step, scale),
        (per,),
        [],
        [qkv],
        [pl.BlockSpec((count, 1, 3, head, toks), lambda p: (0, p, 0, 0, 0))],
        [ pl.BlockSpec((count, 1, head, toks), lambda p: (0, p, 0, 0)), pl.BlockSpec((1, 1, length), lambda p: (p, 0, 0)), ],
        [shape((count, per, head, toks), BF16), shape((per, 1, length), F32)],
        [],
        cost(16 * per * length * length * head, 8 * per * length * head),
        "attend",
    )


def attend_back_kernel(step, scale, x_ref, g_ref, total_ref, o_ref):
    queries = spread(x_ref, (0, 0)) * scale
    keys_t = spread(x_ref, (0, 1))
    keys = keys_t.T
    values = spread(x_ref, (0, 2)).T
    grads = spread(g_ref, ())
    toks = x_ref.shape[-1]
    length = queries.shape[1]
    d_keys = jnp.zeros(queries.shape, F32)
    d_values = jnp.zeros(queries.shape, F32)
    for begin in range(0, length, step):
        query = queries[:, begin : begin + step]
        grad = grads[:, begin : begin + step]
        scores = dot(keys, query, 1, 0)
        probability = jnp.exp(scores - total_ref[0, :, begin : begin + step])
        d_prob = dot(values, grad, 1, 0)
        centered = jnp.sum(probability * d_prob, 0, keepdims=True)
        d_scores = (probability * (d_prob - centered)).astype(BF16)
        d_values += dot(grad, probability.astype(BF16), 1, 1)
        d_keys += dot(query, d_scores, 1, 1)
        d_query = (dot(keys_t, d_scores, 1, 0) * scale).astype(BF16)
        for at in range(0, step, toks):
            o_ref[(begin + at) // toks, 0, 0] = d_query[:, at : at + toks]
    d_keys = d_keys.astype(BF16)
    d_values = d_values.astype(BF16)
    for i in range(length // toks):
        o_ref[i, 0, 1] = d_keys[:, i * toks : (i + 1) * toks]
        o_ref[i, 0, 2] = d_values[:, i * toks : (i + 1) * toks]


def attend_back_call(qkv, grads, totals, step):
    count, per, _, head, toks = qkv.shape
    length = count * toks
    scale = head**-0.5
    return launch(
        functools.partial(attend_back_kernel, step, scale),
        (per,),
        [],
        [qkv, grads, totals],
        [ pl.BlockSpec((count, 1, 3, head, toks), lambda p: (0, p, 0, 0, 0)), pl.BlockSpec((count, head, toks), lambda p: (0, p, 0)), pl.BlockSpec((1, 1, length), lambda p: (p, 0, 0)), ],
        pl.BlockSpec((count, 1, 3, head, toks), lambda p: (0, p, 0, 0, 0)),
        shape(qkv.shape, BF16),
        [],
        cost(40 * per * length * length * head, 14 * per * length * head),
        "attend_back",
    )


def ffn_kernel(
    seqs,
    o_ref,
    x_ref,
    w_out_ref,
    w_up_ref,
    w_down_ref,
    bias_ref,
    norms_ref,
    mix_ref,
    normal0_ref,
    rstd0_ref,
    a_ref,
    g_ref,
    slope_ref,
    normal1_ref,
    rstd1_ref,
    f_ref,
    acc_ref,
):
    j = pl.program_id(0)
    per = o_ref.shape[1]
    head, toks = o_ref.shape[2:]

    @pl.when(j == 0)
    def _():
        for s in range(seqs):
            for h in range(HEADS):
                pair = s * HEADS + h
                mix_ref[h * head : (h + 1) * head, s * toks : (s + 1) * toks] = o_ref[
                    pair // per, pair % per
                ]
        attended = dot(mix_ref[...].T, flat_block(w_out_ref), 1, 0)
        normal, rstd = norm_forward(x_ref[...].astype(F32) + attended)
        normal0_ref[...] = normal
        rstd0_ref[...] = rstd
        normed = normal * norms_ref[0:1] + norms_ref[4:5]
        a_ref[...] = normed.astype(BF16)
        acc_ref[...] = normed

    up = dot(a_ref[...], flat_block(w_up_ref), 1, 0) + bias_ref[...]
    active, slope = gelu_parts(up)
    active = active.astype(BF16)
    g_ref[...] = active
    slope_ref[...] = slope
    acc_ref[...] += dot(active, flat_block(w_down_ref), 1, 0)

    @pl.when(j == pl.num_programs(0) - 1)
    def _():
        normal, rstd = norm_forward(acc_ref[...])
        normal1_ref[...] = normal
        rstd1_ref[...] = rstd
        f_ref[...] = (normal * norms_ref[1:2] + norms_ref[5:6]).astype(BF16)


def ffn_call(mixture, rows, packed, at_out, at_up, at_down, bias, norms, seqs):
    count, per, head, toks = mixture.shape
    total, width = rows.shape
    hidden = bias.shape[1]
    chunks = hidden // width
    blk = width // count
    owners = count // chunks
    return launch(
        functools.partial(ffn_kernel, seqs),
        (chunks,),
        [],
        [mixture, rows, packed, packed, packed, bias, norms],
        [ whole(mixture.shape), whole(rows.shape), pl.BlockSpec((count, blk, width), lambda j: (0, at_out, 0)), pl.BlockSpec((count, blk, width), lambda j: (0, at_up + j, 0)), pl.BlockSpec((owners, hidden // count, width), lambda j: (j, at_down, 0)), pl.BlockSpec((1, width), lambda j: (0, j)), whole(norms.shape), ],
        [ whole((width, total)), whole((total, width)), whole((total, 1)), whole((total, width)), pl.BlockSpec((total, width), lambda j: (0, j)), pl.BlockSpec((total, width), lambda j: (0, j)), whole((total, width)), whole((total, 1)), whole((total, width)), ],
        [ shape((width, total), BF16), shape((total, width), F32), shape((total, 1), F32), shape((total, width), BF16), shape((total, hidden), BF16), shape((total, hidden), F32), shape((total, width), F32), shape((total, 1), F32), shape((total, width), BF16), ],
        [pltpu.VMEM((total, width), F32)],
        cost( 2 * total * width * (width + 2 * hidden), 4 * hidden * width + 10 * total * hidden ),
        "ffn",
    )


def ffn_back_kernel(
    seqs,
    slot_ref,
    order_ref,
    d_ref,
    g_ref,
    slope_ref,
    a_ref,
    normal_ref,
    rstd_ref,
    norms_ref,
    w_out_ref,
    w_up_ref,
    w_down_ref,
    total_ref,
    *refs,
):
    j = pl.program_id(0)
    count, blk, width = w_up_ref.shape
    owners, share, _ = w_down_ref.shape
    half = count // 2
    send_refs, refs = refs[:half], refs[half:]
    keep_ref, bias_ref, d_attn_ref, d_attended_ref, sums_ref, d_mix_ref = refs[:6]
    db_ref, at_ref, acc_ref, part_ref = refs[6:]

    @pl.when(j == 0)
    def _():
        db_ref[...] = d_ref[...].astype(BF16)
        at_ref[...] = a_ref[...].T
        acc_ref[...] = d_ref[...]

    part_ref[...] = dot(g_ref[...].T, db_ref[...], 1, 0)
    for i in range(owners):
        slot = slot_ref[j * owners + i]
        piece = part_ref[i * share : (i + 1) * share, :].astype(BF16)

        @pl.when(slot < half)
        def _():
            keep_ref[slot, 0:share, :] = piece

        for at, send_ref in enumerate(send_refs):

            @pl.when(slot == half + at)
            def _():
                send_ref[0:share, :] = piece

    d_up = (dot(db_ref[...], flat_block(w_down_ref), 1, 1) * slope_ref[...]).astype(BF16)
    bias_ref[...] = column_sum(d_up.astype(F32))
    part_ref[...] = dot(at_ref[...], d_up, 1, 0)
    place = pl.ds(pl.multiple_of(share + j * blk, 16), blk)
    for pos in range(count):
        piece = part_ref[pl.ds(pl.multiple_of(order_ref[pos] * blk, 16), blk), :].astype(BF16)
        if pos < half:
            keep_ref[pos, place, :] = piece
        else:
            send_refs[pos - half][place, :] = piece
    acc_ref[...] += dot(d_up, flat_block(w_up_ref), 1, 1)

    @pl.when(j == pl.num_programs(0) - 1)
    def _():
        gradient = acc_ref[...]
        normal = normal_ref[...]
        sums_ref[0:1, :] = column_sum(gradient * normal)
        sums_ref[1:2, :] = column_sum(gradient)
        d_sum = norm_backward(normal, rstd_ref[...], norms_ref[0:1], gradient)
        d_attn_ref[...] = d_sum
        low = d_sum.astype(BF16)
        d_attended_ref[...] = low
        turned = dot(flat_block(w_out_ref), low, 1, 1).astype(BF16)
        per = seqs * HEADS // count
        head, toks = width // HEADS, d_mix_ref.shape[2]
        for s in range(seqs):
            for h in range(HEADS):
                pair = s * HEADS + h
                row = pair % per * head
                d_mix_ref[pair // per, row : row + head] = turned[
                    h * head : (h + 1) * head, s * toks : (s + 1) * toks
                ]
        rest = jnp.concatenate([total_ref[j] for j in range(total_ref.shape[0])], 0)
        rest = jnp.concatenate([rest, jnp.zeros((RIDE - rest.shape[0], LANES), F32)], 0)
        for part in range(3):
            low = rest.astype(BF16)
            rest = rest - low.astype(F32)
            row = per * head + part * RIDE
            for device in range(count):
                d_mix_ref[device, row : row + RIDE] = low


def ffn_back_call(
    slot, order, d_ffn, active, slope, normed, normal, rstd, norms, packed, at_out, at_up, at_down, totals, seqs):
    total, width = d_ffn.shape
    hidden = active.shape[1]
    count = packed.shape[0]
    chunks = hidden // width
    blk = width // count
    share = hidden // count
    owners = count // chunks
    per = seqs * HEADS // count
    head = width // HEADS
    toks = total // seqs
    rows_out = share + chunks * blk
    wide = pl.BlockSpec((total, width), lambda j, *_: (0, j))
    results = launch(
        functools.partial(ffn_back_kernel, seqs),
        (chunks,),
        [slot, order],
        [d_ffn, active, slope, normed, normal, rstd, norms, packed, packed, packed, totals],
        [ whole(d_ffn.shape), wide, wide, whole(normed.shape), whole(normal.shape), whole(rstd.shape), whole(norms.shape), pl.BlockSpec((count, blk, width), lambda j, *_: (0, at_out, 0)), pl.BlockSpec((count, blk, width), lambda j, *_: (0, at_up + j, 0)), pl.BlockSpec((owners, share, width), lambda j, *_: (j, at_down, 0)), whole(totals.shape), ],
        [ *[whole((rows_out, width))] * (count // 2), whole((count // 2, rows_out, width)), pl.BlockSpec((1, width), lambda j, *_: (0, j)), whole((total, width)), whole((total, width)), whole((2, width)), whole((count, per * head + 3 * RIDE, toks)), ],
        [ *[shape((rows_out, width), BF16)] * (count // 2), shape((count // 2, rows_out, width), BF16), shape((1, hidden), F32), shape((total, width), F32), shape((total, width), BF16), shape((2, width), F32), shape((count, per * head + 3 * RIDE, toks), BF16), ],
        [ pltpu.VMEM((total, width), BF16), pltpu.VMEM((width, total), BF16), pltpu.VMEM((total, width), F32), pltpu.VMEM((width, width), F32), ],
        cost( 8 * total * width * hidden + 2 * total * width * width, 8 * hidden * width + 10 * total * hidden, ),
        "ffn_back",
    )
    return results[: count // 2], *results[count // 2 :]


def gates_kernel(
    seqs, groups_ref, ids_ref, back_ids_ref, table_ref, w_fwd_ref, w_rev_ref, bias_ref,
    z_ref, c_ref, totals_ref,
):
    s = pl.program_id(0)
    steps = ids_ref.shape[1]
    rows = 2 * seqs
    table = flat_block(table_ref)
    vocabulary = lax.broadcasted_iota(jnp.int32, (steps, NCHAR), 1)
    chunks = z_ref.shape[0]
    half = chunks * LANES
    for direction, (source, weight) in enumerate(((ids_ref, w_fwd_ref), (back_ids_ref, w_rev_ref))):
        onehot = jnp.where(source[0] == vocabulary, 1.0, 0.0).astype(BF16)
        embedded = dot(onehot, table, 1, 0).astype(BF16)
        gate_input = dot(embedded, flat_block(weight), 1, 0)
        own = slice(direction * half, (direction + 1) * half)
        update = jax.nn.sigmoid(gate_input[:, :half] + bias_ref[8:9, own])
        candidate = jnp.tanh(gate_input[:, half:] + bias_ref[9:10, own])
        place = pl.ds(s + direction * seqs, steps, stride=rows)
        for j in range(chunks):
            z_ref[j, place, :] = update[:, j * LANES : (j + 1) * LANES]
            c_ref[j, place, :] = candidate[:, j * LANES : (j + 1) * LANES]

    @pl.when(s == pl.num_programs(0) - 1)
    def _():
        def one(t, carry):
            states, products = carry
            place = pl.ds(pl.multiple_of(t * rows, rows), rows)
            new_states, new_products = [], []
            for j in range(chunks):
                update = z_ref[j, place, :]
                decay = 1.0 - update
                new_states.append(decay * states[j] + update * c_ref[j, place, :])
                new_products.append(products[j] * decay)
            return tuple(new_states), tuple(new_products)

        zero = jnp.zeros((rows, LANES), F32)
        states, products = lax.fori_loop(
            0, steps, one, ((zero,) * chunks, (zero + 1.0,) * chunks), unroll=8
        )
        for j in range(chunks):
            totals_ref[0, j] = products[j]
            totals_ref[1, j] = states[j]


def gates_call(groups, ids, packed, at_gru, at_table, bias):
    seqs, steps = ids.shape
    count, _, width = packed.shape
    blk = width // count
    table_rows = 4 * NCHAR // count
    per_group = NCHAR // table_rows
    chunks = width // 2 // LANES
    laid = (chunks, steps * 2 * seqs, LANES)
    return launch(
        functools.partial(gates_kernel, seqs),
        (seqs,),
        [groups],
        [ids[..., None], ids[:, ::-1, None], packed, packed, packed, bias],
        [ pl.BlockSpec((1, steps, 1), lambda s, g: (s, 0, 0)), pl.BlockSpec((1, steps, 1), lambda s, g: (s, 0, 0)), pl.BlockSpec((per_group, table_rows, width), lambda s, g: (g[s], at_table, 0)), pl.BlockSpec((count, blk, width), lambda s, g: (0, at_gru, 0)), pl.BlockSpec((count, blk, width), lambda s, g: (0, at_gru + 1, 0)), whole(bias.shape), ],
        [whole(laid), whole(laid), whole((2, chunks, 2 * seqs, LANES))],
        [shape(laid, F32), shape(laid, F32), shape((2, chunks, 2 * seqs, LANES), F32)],
        [],
        cost( 2 * seqs * steps * width * (2 * NCHAR + 2 * width), 16 * seqs * steps * width ),
        "gates",
    )


def entry_state(me, totals, products, rows, seqs, forward):
    count, chunks = products.shape[0], products.shape[1]
    first = lax.broadcasted_iota(jnp.int32, (rows, LANES), 0) < seqs
    result = []
    for j in range(chunks):
        state = jnp.zeros((rows, LANES), F32)
        for lap in range(count):
            up, down = lap, count - 1 - lap
            one, other = (up, down) if forward else (down, up)
            product = jnp.where(first, products[one, j], products[other, j])
            total = jnp.where(first, totals[one, j], totals[other, j])
            up_in, down_in = (up < me).astype(F32), (down > me).astype(F32)
            ahead = jnp.where(first, up_in, down_in) if forward else jnp.where(first, down_in, up_in)
            state = jnp.where(ahead > 0.5, product * state + total, state)
        result.append(state)
    return result


def states_kernel(
    seqs, me_ref, z_ref, c_ref, all_ref, starts_ref, ends_ref, lens_ref, w_ref,
    prior_ref, pooled_ref, proj_ref, proj_low_ref, hold_ref, state_ref, acc_ref,
):
    i = pl.program_id(0)
    last = pl.num_programs(0) - 1
    rows = 2 * seqs
    chunks = z_ref.shape[0]
    span = z_ref.shape[1] // rows
    toks = starts_ref.shape[1]
    half = chunks * LANES

    @pl.when(i == 0)
    def _():
        entry = entry_state(me_ref[0], all_ref[:, 1], all_ref[:, 0], rows, seqs, True)
        for j in range(chunks):
            state_ref[j] = entry[j]
        acc_ref[...] = jnp.zeros_like(acc_ref)

    def one(t, states):
        place = pl.ds(pl.multiple_of(t * rows, rows), rows)
        result = []
        for j in range(chunks):
            prior_ref[j, place, :] = states[j]
            update = z_ref[j, place, :]
            state = (1.0 - update) * states[j] + update * c_ref[j, place, :]
            hold_ref[j, place, :] = state
            result.append(state)
        return tuple(result)

    states = lax.fori_loop(0, span, one, tuple(state_ref[j] for j in range(chunks)), unroll=8)
    for j in range(chunks):
        state_ref[j] = states[j]
    count = lax.broadcasted_iota(jnp.int32, (toks, span), 1) + i * span
    for direction in range(2):
        place_of = count if direction == 0 else (last + 1) * span - 1 - count
        for s in range(seqs):
            member = jnp.where(
                (place_of >= starts_ref[s]) & (place_of < ends_ref[s]), 1.0, 0.0
            ).astype(BF16)
            held = jnp.concatenate(
                [
                    hold_ref[j, pl.ds(s + direction * seqs, span, stride=rows), :]
                    for j in range(chunks)
                ],
                axis=1,
            ).astype(BF16)
            acc_ref[s * toks : (s + 1) * toks, direction * half : (direction + 1) * half] += dot(
                member, held, 1, 0
            )

    @pl.when(i == last)
    def _():
        for s in range(seqs):
            rows_of = slice(s * toks, (s + 1) * toks)
            pooled_ref[rows_of, :] = (acc_ref[rows_of, :] / lens_ref[s]).astype(BF16)
        proj = dot(pooled_ref[...], flat_block(w_ref), 1, 0)
        proj_ref[...] = proj
        proj_low_ref[...] = proj.astype(BF16)


def collect_kernel(me_ref, *refs):
    for mask, ref in enumerate(refs[:-1]):
        refs[-1][me_ref[0] ^ mask] = ref[...]


def collect(me, parts):
    out = (len(parts), *parts[0].shape)
    return launch(
        collect_kernel,
        (1,),
        [me],
        parts,
        [whole(v.shape) for v in parts],
        whole(out),
        shape(out, parts[0].dtype),
        [],
        cost(0, 8 * len(parts) * parts[0].size),
        "collect",
    )


def states_call(me, z, c, gathered, starts, ends, lens, packed, at_char, parts):
    chunks, length, _ = z.shape
    seqs, toks, _ = starts.shape
    count, _, width = packed.shape
    blk = width // count
    span = length // parts
    total = seqs * toks
    stream = pl.BlockSpec((chunks, span, LANES), lambda i, *_: (0, i, 0))
    return launch(
        functools.partial(states_kernel, seqs),
        (parts,),
        [me],
        [z, c, gathered, starts, ends, lens, packed],
        [ stream, stream, whole(gathered.shape), whole(starts.shape), whole(ends.shape), whole(lens.shape), pl.BlockSpec((count, blk, width), lambda i, *_: (0, at_char, 0)), ],
        [stream] + [whole((total, width))] * 3,
        [shape(z.shape, F32), shape((total, width), BF16), shape((total, width), F32), shape((total, width), BF16), ],
        [ pltpu.VMEM((chunks, span, LANES), F32), pltpu.VMEM((chunks, 2 * seqs, LANES), F32), pltpu.VMEM((total, width), F32), ],
        cost(2 * total * width * (width + length // 8), 12 * chunks * length * LANES),
        "states",
    )


def states_back_kernel(
    seqs, d_ref, w_ref, lens_ref, starts_ref, ends_ref, z_ref, ds_ref, total_ref,
):
    rows = 2 * seqs
    chunks = z_ref.shape[0]
    steps = z_ref.shape[1] // rows
    toks = starts_ref.shape[2]
    half = chunks * LANES
    d_pooled = dot(d_ref[...], flat_block(w_ref), 1, 1)
    count = lax.broadcasted_iota(jnp.int32, (steps, toks), 0)
    for s in range(seqs):
        d_summed = (d_pooled[s * toks : (s + 1) * toks] / lens_ref[s]).astype(BF16)
        for direction in range(2):
            place_of = count if direction == 0 else steps - 1 - count
            member = jnp.where(
                (place_of >= starts_ref[s]) & (place_of < ends_ref[s]), 1.0, 0.0
            ).astype(BF16)
            d_states = dot(member, d_summed[:, direction * half : (direction + 1) * half], 1, 0)
            for j in range(chunks):
                ds_ref[j, pl.ds(s + direction * seqs, steps, stride=rows), :] = d_states[
                    :, j * LANES : (j + 1) * LANES
                ]

    def one(lap, carried):
        place = pl.ds(pl.multiple_of((steps - 1 - lap) * rows, rows), rows)
        return tuple(
            (1.0 - z_ref[j, place, :]) * (ds_ref[j, place, :] + carried[j]) for j in range(chunks)
        )

    zero = jnp.zeros((rows, LANES), F32)
    carried = lax.fori_loop(0, steps, one, (zero,) * chunks, unroll=8)
    for j in range(chunks):
        total_ref[j] = carried[j]


def states_back_call(d_proj, packed, at_char, lens, starts, ends, z):
    chunks, length, _ = z.shape
    seqs = starts.shape[0]
    count, _, width = packed.shape
    blk = width // count
    return launch(
        functools.partial(states_back_kernel, seqs),
        (1,),
        [],
        [d_proj, packed, lens, starts, ends, z],
        [ whole(d_proj.shape), pl.BlockSpec((count, blk, width), lambda i: (0, at_char, 0)), whole(lens.shape), whole(starts.shape), whole(ends.shape), whole(z.shape), ],
        [whole(z.shape), whole((chunks, 2 * seqs, LANES))],
        [shape(z.shape, F32), shape((chunks, 2 * seqs, LANES), F32)],
        [],
        cost( 2 * d_proj.shape[0] * width * (width + length // 8), 8 * chunks * length * LANES ),
        "states_back",
    )


def gates_back_kernel(
    seqs, me_ref, groups_ref, z_ref, c_ref, prior_ref, ds_ref, all_ref, back_ref, ids_ref,
    back_ids_ref, s_ref, bias_ref, du_ref, dc_ref, carried_ref, acc_ref,
):
    i = pl.program_id(0)
    rows = 2 * seqs
    chunks = z_ref.shape[0]
    span = z_ref.shape[1] // rows
    half = chunks * LANES

    @pl.when(i == 0)
    def _():
        parts = back_ref[...].astype(F32)
        summed = parts[:, :RIDE] + parts[:, RIDE : 2 * RIDE] + parts[:, 2 * RIDE :]
        totals = summed[:, : chunks * rows].reshape(-1, chunks, rows, LANES)
        entry = entry_state(me_ref[0], totals, all_ref[:, 0], rows, seqs, False)
        for j in range(chunks):
            carried_ref[j] = entry[j]
        acc_ref[...] = jnp.zeros_like(acc_ref)

    def one(lap, carried):
        place = pl.ds(pl.multiple_of((span - 1 - lap) * rows, rows), rows)
        result = []
        for j in range(chunks):
            update = z_ref[j, place, :]
            candidate = c_ref[j, place, :]
            total = ds_ref[j, place, :] + carried[j]
            decay = 1.0 - update
            gated = total * update
            du_ref[j, place, :] = gated * decay * (candidate - prior_ref[j, place, :])
            dc_ref[j, place, :] = gated * (1.0 - candidate * candidate)
            result.append(decay * total)
        return tuple(result)

    carried = lax.fori_loop(0, span, one, tuple(carried_ref[j] for j in range(chunks)), unroll=8)
    for j in range(chunks):
        carried_ref[j] = carried[j]
    vocabulary = lax.broadcasted_iota(jnp.int32, (NCHAR, span), 0)
    for direction in range(2):
        source = ids_ref if direction == 0 else back_ids_ref
        for s in range(seqs):
            place = pl.ds(s + direction * seqs, span, stride=rows)
            gradient = jnp.concatenate(
                [part[j, place, :] for part in (du_ref, dc_ref) for j in range(chunks)], axis=1
            ).astype(BF16)
            onehot = jnp.where(source[s] == vocabulary, 1.0, 0.0).astype(BF16)
            acc_ref[groups_ref[s], :, direction * 2 * half : (direction + 1) * 2 * half] += dot(
                onehot, gradient, 1, 0
            )

    @pl.when(i == pl.num_programs(0) - 1)
    def _():
        total = jnp.zeros((1, 4 * half), F32)
        for g in range(acc_ref.shape[0]):
            total += column_sum(acc_ref[g])
            s_ref[g] = acc_ref[g].astype(BF16)
        bias_ref[...] = total


def gates_back_call(me, groups, z, c, prior, ds, gathered, gathered_back, ids, n_groups, parts):
    chunks, length, _ = z.shape
    seqs, steps = ids.shape
    span = length // parts
    width = 2 * chunks * LANES
    stream = pl.BlockSpec((chunks, span, LANES), lambda i, *_: (0, parts - 1 - i, 0))
    lanes = pl.BlockSpec((seqs, 1, steps // parts), lambda i, *_: (0, 0, parts - 1 - i))
    return launch(
        functools.partial(gates_back_kernel, seqs),
        (parts,),
        [me, groups],
        [z, c, prior, ds, gathered, gathered_back, ids[:, None, :], ids[:, None, ::-1]],
        [stream] * 4 + [whole(gathered.shape), pl.BlockSpec((gathered_back.shape[0], 3 * RIDE, LANES), lambda i, *_: (0, gathered_back.shape[1] // (3 * RIDE) - 1, 0)), lanes, lanes],
        [whole((n_groups, NCHAR, 2 * width)), whole((1, 2 * width))],
        [shape((n_groups, NCHAR, 2 * width), BF16), shape((1, 2 * width), F32)],
        [ pltpu.VMEM((chunks, span, LANES), F32), pltpu.VMEM((chunks, span, LANES), F32), pltpu.VMEM((chunks, 2 * seqs, LANES), F32), pltpu.VMEM((n_groups, NCHAR, 2 * width), F32), ],
        cost(4 * seqs * steps * NCHAR * width, 16 * chunks * length * LANES),
        "gates_back",
    )


def shifted(values, toks, low, high):
    total = values.shape[0]
    row = lax.broadcasted_iota(jnp.int32, (total, 1), 0)
    before = pltpu.roll(values, 1, 0)
    after = pltpu.roll(values, total - 1, 0)
    for s in range(total // toks):
        before = jnp.where(row == s * toks, low[s], before)
        after = jnp.where(row == (s + 1) * toks - 1, high[s], after)
    return before.astype(BF16), after.astype(BF16)


def conv_kernel(
    toks, f_ref, p_ref, normal_ref, proj_ref, norms_ref, low_ref, high_ref, w_ref, tok_g_ref,
    char_g_ref, tok_ref, char_ref, d_tok_ref, d_char_ref, dm_ref, sums_ref, begin_ref, end_ref,
    acc_ref, x_ref,
):
    half, k = pl.program_id(0), pl.program_id(1)
    width = f_ref.shape[1]

    @pl.when((half == 0) & (k == 0))
    def _():
        for part, source in enumerate((f_ref, p_ref)):
            columns = slice(part * width, (part + 1) * width)
            before, after = shifted(
                source[...].astype(F32),
                toks,
                low_ref[:, :, columns].astype(F32),
                high_ref[:, :, columns].astype(F32),
            )
            x_ref[0, :, columns] = before
            x_ref[1, :, columns] = source[...]
            x_ref[2, :, columns] = after

    product = dot(x_ref[k], flat_block(w_ref), 1, 0)

    @pl.when(k == 0)
    def _():
        acc_ref[...] = product

    @pl.when(k > 0)
    def _():
        acc_ref[...] += product

    def finish(which, base, grad_ref, out_ref, d_ref):
        normal, rstd = norm_forward(base + acc_ref[...])
        gain = norms_ref[2 + which : 3 + which]
        out_ref[...] = normal * gain + norms_ref[6 + which : 7 + which]
        gradient = grad_ref[...].astype(F32)
        sums_ref[0, 0:1, :] = column_sum(gradient * normal)
        sums_ref[0, 1:2, :] = column_sum(gradient)
        d_sum = norm_backward(normal, rstd, gain, gradient)
        d_ref[...] = d_sum
        low_sum = d_sum.astype(BF16)
        dm_ref[...] = low_sum
        for s in range(begin_ref.shape[0]):
            begin_ref[s] = low_sum[s * toks : s * toks + 1]
            end_ref[s] = low_sum[(s + 1) * toks - 1 : (s + 1) * toks]

    @pl.when((half == 0) & (k == 2))
    def _():
        finish(
            0, normal_ref[...] * norms_ref[1:2] + norms_ref[5:6], tok_g_ref, tok_ref, d_tok_ref
        )

    @pl.when((half == 1) & (k == 2))
    def _():
        finish(1, proj_ref[...], char_g_ref, char_ref, d_char_ref)


def conv_call(f_low, proj_low, normal1, proj, norms, low, high, packed, tok_grad, char_grad, seqs, carry):
    total, width = f_low.shape
    count = packed.shape[0]
    blk = 2 * width // count
    rows = (total, width)
    return launch(
        functools.partial(conv_kernel, total // seqs),
        (2, 3),
        [],
        [f_low, proj_low, normal1, proj, norms, low, high, packed, tok_grad, char_grad],
        [ whole(rows), whole(rows), whole(rows), whole(rows), whole(norms.shape), whole(low.shape), whole(high.shape), pl.BlockSpec((count, blk, width), lambda h, k: (0, 2 * k + h, 0)), whole(rows), whole(rows), ],
        [ whole(rows), whole(rows), whole(rows), whole(rows), pl.BlockSpec(rows, lambda h, k: (0, h)), pl.BlockSpec((1, 2, width), lambda h, k: (h, 0, 0)), pl.BlockSpec((seqs, 1, width), lambda h, k: (0, 0, h)), pl.BlockSpec((seqs, 1, width), lambda h, k: (0, 0, h)), ],
        [ shape(rows, F32), shape(rows, F32), shape(rows, F32), shape(rows, F32), shape((total, 2 * width), BF16), shape((2, 2, width), F32), shape((seqs, 1, 2 * width), BF16), shape((seqs, 1, 2 * width), BF16), ],
        [pltpu.VMEM(rows, F32), pltpu.VMEM((3, total, 2 * width), BF16)],
        cost(24 * total * width * width, 24 * width * width + 40 * total * width),
        "conv",
        carry,
    )


def place_blocks(part_ref, order_ref, send_ref, keep_ref, blk, row=0):
    count = part_ref.shape[0] // blk
    for pos in range(count):
        start = pl.multiple_of(order_ref[pos] * blk, 16)
        piece = part_ref[pl.ds(start, blk), :].astype(BF16)
        if pos < count // 2:
            keep_ref[pos, row : row + blk, :] = piece
        else:
            send_ref[pos - count // 2, row : row + blk, :] = piece


def conv_weight_kernel(
    toks, order_ref, f_ref, p_ref, other_f_ref, other_p_ref, dm_ref, low_ref, high_ref,
    other_dm_ref, begin_ref, end_ref, far_low_ref, far_high_ref, keep_a_ref, sent_a_ref, keep_b_ref, sent_b_ref,
    turned_ref, whole_ref, shift_ref, part_ref,
):
    k, half = pl.program_id(0), pl.program_id(1)
    total, width = f_ref.shape
    pieces = 2 * keep_a_ref.shape[0]
    blk = keep_a_ref.shape[1]

    @pl.when((k == 0) & (half == 0))
    def _():
        for core, pair in enumerate(((f_ref, p_ref), (other_f_ref, other_p_ref))):
            for part, source in enumerate(pair):
                whole_ref[part * width : (part + 1) * width, :] = source[...].T
            for pos in range(pieces):
                start = pl.multiple_of(order_ref[pos] * blk, 16)
                turned_ref[pos * blk : (pos + 1) * blk, core * total : (core + 1) * total] = (
                    whole_ref[pl.ds(start, blk), :]
                )
        odd = (order_ref[0] & 1) == 1
        edges = (
            (low_ref[...], high_ref[...]),
            (
                jnp.where(odd, far_low_ref[...], end_ref[...]),
                jnp.where(odd, begin_ref[...], far_high_ref[...]),
            ),
        )
        for core, (source, (low, high)) in enumerate(zip((dm_ref, other_dm_ref), edges)):
            rows = slice(core * total, (core + 1) * total)
            for part in range(2):
                columns = slice(part * width, (part + 1) * width)
                middle = source[:, columns]
                before, after = shifted(
                    middle.astype(F32),
                    toks,
                    low[:, :, columns].astype(F32),
                    high[:, :, columns].astype(F32),
                )
                shift_ref[part, rows, :] = after
                shift_ref[2 + part, rows, :] = middle
                shift_ref[4 + part, rows, :] = before

    at = 2 * k + half
    part_ref[...] = dot(turned_ref[...], shift_ref[at], 1, 0)

    def put(keep_ref, sent_ref, kept, sent):
        for index, (one, other) in enumerate(zip(kept, sent)):
            keep_ref[index] = part_ref[one * blk : (one + 1) * blk, :].astype(BF16)
            sent_ref[index] = part_ref[other * blk : (other + 1) * blk, :].astype(BF16)

    @pl.when(at < 3)
    def _():
        put(keep_a_ref, sent_a_ref, range(pieces // 2), range(pieces // 2, pieces))

    @pl.when(at >= 3)
    def _():
        put(keep_b_ref, sent_b_ref, range(0, pieces, 2), range(1, pieces, 2))


def conv_weight_call(order, own, other, dm, low, high, other_dm, begin, end, far_low, far_high, count):
    total, width = own[0].shape
    toks = total // low.shape[0]
    blk = 2 * width // count
    out = (count // 4, 3 * blk, width)
    first = pl.BlockSpec((count // 4, blk, width), lambda k, h, *_: (0, jnp.minimum(2 * k + h, 2), 0))
    second = pl.BlockSpec(
        (count // 4, blk, width), lambda k, h, *_: (0, jnp.maximum(2 * k + h - 3, 0), 0)
    )
    inputs = [*own, *other, dm, low, high, other_dm, begin, end, far_low, far_high]
    keep_a, sent_a, keep_b, sent_b = launch(
        functools.partial(conv_weight_kernel, toks),
        (3, 2),
        [order],
        inputs,
        [whole(v.shape) for v in inputs],
        [first, first, second, second],
        [shape(out, BF16)] * 4,
        [
            pltpu.VMEM((width, 2 * total), BF16),
            pltpu.VMEM((2 * width, total), BF16),
            pltpu.VMEM((6, 2 * total, width), BF16),
            pltpu.VMEM((width, width), F32),
        ],
        cost(24 * total * width * width, 12 * width * width),
        "conv_weight",
    )
    return [[keep_a, sent_a], [keep_b, sent_b]]


def conv_back_kernel(
    toks, dm_ref, low_ref, high_ref, w_ref, d_tok_ref, d_char_ref, normal_ref, rstd_ref,
    norms_ref, d_proj_ref, d_ffn_ref, sums_ref, shift_ref, acc_ref,
):
    k, half = pl.program_id(0), pl.program_id(1)
    width = d_tok_ref.shape[1]

    @pl.when((half == 0) & (k == 0))
    def _():
        for part in range(2):
            columns = slice(part * width, (part + 1) * width)
            source = dm_ref[:, columns]
            before, after = shifted(
                source.astype(F32),
                toks,
                low_ref[:, :, columns].astype(F32),
                high_ref[:, :, columns].astype(F32),
            )
            shift_ref[part] = after
            shift_ref[2 + part] = source
            shift_ref[4 + part] = before

    product = dot(shift_ref[2 * k + half], flat_block(w_ref), 1, 1)

    @pl.when((k == 0) & (half == 0))
    def _():
        acc_ref[...] = product

    @pl.when((k > 0) | (half > 0))
    def _():
        acc_ref[...] += product

    @pl.when((k == 2) & (half == 1))
    def _():
        d_proj_ref[...] = (d_char_ref[...] + acc_ref[:, width:]).astype(BF16)
        gradient = d_tok_ref[...] + acc_ref[:, :width]
        normal = normal_ref[...]
        sums_ref[0:1, :] = column_sum(gradient * normal)
        sums_ref[1:2, :] = column_sum(gradient)
        d_ffn_ref[...] = norm_backward(normal, rstd_ref[...], norms_ref[1:2], gradient)


def conv_back_call(d_merged, low, high, packed, d_tok, d_char, normal1, rstd1, norms, seqs, carry):
    total, width = d_tok.shape
    count = packed.shape[0]
    blk = 2 * width // count
    rows = (total, width)
    return launch(
        functools.partial(conv_back_kernel, total // seqs),
        (3, 2),
        [],
        [d_merged, low, high, packed, d_tok, d_char, normal1, rstd1, norms],
        [ whole(d_merged.shape), whole(low.shape), whole(high.shape), pl.BlockSpec((count, blk, width), lambda k, h: (0, 2 * k + h, 0)), whole(rows), whole(rows), whole(rows), whole(rstd1.shape), whole(norms.shape), ],
        [whole(rows), whole(rows), whole((2, width))],
        [shape(rows, BF16), shape(rows, F32), shape((2, width), F32)],
        [ pltpu.VMEM((6, total, width), BF16), pltpu.VMEM((total, 2 * width), F32), ],
        cost(24 * total * width * width, 24 * width * width + 20 * total * width),
        "conv_back",
        carry,
    )


def rest_kernel(
    order_ref, table_ref, s_ref, w0_ref, w1_ref, mix_ref, d_att_ref, send_ref, keep_ref, part_ref,
):
    count, blk, width = w0_ref.shape
    rows = part_ref.shape[0]
    turned = flat_block(table_ref).T
    sums = s_ref[...].reshape(rows, 2 * width)
    for part in range(2):
        part_ref[0:width, :] = dot(turned, sums[:, part * width : (part + 1) * width], 1, 0)
        place_blocks(part_ref.at[0:width], order_ref, send_ref, keep_ref, blk, part * blk)
    part_ref[...] = dot(sums[:, :width], flat_block(w0_ref), 1, 1) + dot(
        sums[:, width:], flat_block(w1_ref), 1, 1
    )
    place_blocks(part_ref, order_ref, send_ref, keep_ref, rows // count, 2 * blk)
    part_ref[0:width, :] = dot(mix_ref[...], d_att_ref[...], 1, 0)
    place_blocks(
        part_ref.at[0:width], order_ref, send_ref, keep_ref, blk, 2 * blk + rows // count
    )


def rest_call(order, packed, at_table, at_gru, sums, mixture, d_att, height):
    count, _, width = packed.shape
    blk = width // count
    rows = sums.shape[0] * sums.shape[1]
    table_rows = rows // count
    out = (count // 2, height, width)
    return launch(
        rest_kernel,
        (1,),
        [order],
        [packed, sums, packed, packed, mixture, d_att],
        [
            pl.BlockSpec((count, table_rows, width), lambda i, *_: (0, at_table, 0)),
            whole(sums.shape),
            pl.BlockSpec((count, blk, width), lambda i, *_: (0, at_gru, 0)),
            pl.BlockSpec((count, blk, width), lambda i, *_: (0, at_gru + 1, 0)),
            whole(mixture.shape),
            whole(d_att.shape),
        ],
        [whole(out), whole(out)],
        [shape(out, BF16), shape(out, BF16)],
        [pltpu.VMEM((rows, width), F32)],
        cost(8 * rows * width * width, 20 * width * width),
        "rest",
    )


def qkv_back_kernel(
    seqs, order_ref, d_ref, x_ref, w_ref, d_attn_ref, pooled_ref, d_proj_ref,
    sums0_ref, sums1_ref, sums23_ref, bias_ref, bias_up_ref, out_ref, send_ref, keep_ref, xt_ref,
    dt_ref, part_ref, small_ref,
):
    j = pl.program_id(0)
    per = d_ref.shape[1]
    head, toks = d_ref.shape[3:]
    pieces, _, width = send_ref.shape
    blk = width // (2 * pieces)
    half = width // 2

    def put(row):
        for pos in range(2 * pieces):
            start = pl.multiple_of(order_ref[pos] * blk, 16)
            piece = part_ref[pl.ds(start, blk), :].astype(BF16)
            if pos < pieces:
                keep_ref[pos, row, :] = piece
            else:
                send_ref[pos - pieces, row, :] = piece

    @pl.when(j == 0)
    def _():
        xt_ref[...] = x_ref[...].T
        out_ref[...] = d_attn_ref[...]
        small_ref[...] = jnp.zeros_like(small_ref)
        for row, ref in enumerate((sums0_ref, sums1_ref)):
            small_ref[row : row + 1] = ref[0:1]
            small_ref[4 + row : 5 + row] = ref[1:2]
        for which in range(2):
            small_ref[2 + which : 3 + which] = sums23_ref[which, 0:1]
            small_ref[6 + which : 7 + which] = sums23_ref[which, 1:2]
        for part in range(2):
            own = slice(part * half, (part + 1) * half)
            small_ref[8:9, own] = bias_ref[:, part * width : part * width + half]
            small_ref[9:10, own] = bias_ref[:, part * width + half : (part + 1) * width]
        for part in range(bias_up_ref.shape[1] // width):
            small_ref[10 + part : 11 + part] = bias_up_ref[:, part * width : (part + 1) * width]
        small = small_ref[...].astype(BF16)
        for pos in range(pieces):
            keep_ref[pos, 4 * blk : 4 * blk + SMALL_ROWS, :] = small
            send_ref[pos, 4 * blk : 4 * blk + SMALL_ROWS, :] = small
        part_ref[...] = dot(pooled_ref[...].T, d_proj_ref[...], 1, 0)
        put(slice(3 * blk, 4 * blk))

    for s in range(seqs):
        for h in range(HEADS):
            pair = s * HEADS + h
            dt_ref[h * head : (h + 1) * head, s * toks : (s + 1) * toks] = d_ref[
                pair // per, pair % per, 0
            ]
    gradient = dt_ref[...].T
    part_ref[...] = dot(xt_ref[...], gradient, 1, 0)
    put(pl.ds(pl.multiple_of(j * blk, 16), blk))
    out_ref[...] += dot(gradient, flat_block(w_ref), 1, 1)


def qkv_back_call(
    order, d_qkv, rows, packed, base, d_attn, pooled, d_proj, small, seqs, height
):
    count, per, _, head, toks = d_qkv.shape
    total, width = rows.shape
    blk = width // count
    out = (count // 2, height, width)
    rest = [d_attn, pooled, d_proj, *small]
    return launch(
        functools.partial(qkv_back_kernel, seqs),
        (3,),
        [order],
        [d_qkv, rows, packed, *rest],
        [
            pl.BlockSpec((count, per, 1, head, toks), lambda j, *_: (0, 0, j, 0, 0)),
            whole(rows.shape),
            pl.BlockSpec((count, blk, width), lambda j, *_: (0, base + j, 0)),
            *[whole(v.shape) for v in rest],
        ],
        [whole((total, width)), whole(out), whole(out)],
        [shape((total, width), F32), shape(out, BF16), shape(out, BF16)],
        [
            pltpu.VMEM((width, total), BF16),
            pltpu.VMEM((width, total), BF16),
            pltpu.VMEM((width, width), F32),
            pltpu.VMEM((SMALL_ROWS, width), F32),
        ],
        cost(16 * total * width * width, 20 * width * width + 16 * total * width),
        "qkv_back",
    )


def pack_kernel(layout, *refs):
    ins, out_ref = refs[:-1], refs[-1]
    at = 0
    out_ref[...] = jnp.zeros_like(out_ref)
    width = out_ref.shape[1]
    for ref, row in zip(ins, layout):
        height, columns = ref.shape
        if columns < width:
            out_ref[row : row + height, :columns] = ref[...]
        else:
            for block in range(columns // width):
                out_ref[row + block * height : row + (block + 1) * height, :] = ref[
                    :, block * width : (block + 1) * width
                ]


def pack(arrays, layout, rows, width):
    return launch(
        functools.partial(pack_kernel, layout),
        (1,),
        [],
        arrays,
        [whole(v.shape) for v in arrays],
        whole((rows, width)),
        shape((rows, width), BF16),
        [],
        cost(0, 4 * rows * width),
        "pack",
    )


def swap(value, axis, bit):
    size = lax.axis_size(axis)
    return lax.ppermute(value, axis, [(i, i ^ (1 << bit)) for i in range(size)])


def add_low(kept, arrived):
    return (kept.astype(F32) + arrived.astype(F32)).astype(BF16)


def fold_kernel(keep_top, keep_bottom, came_top, came_bottom, ka_ref, sa_ref, kb_ref, sb_ref):
    half = ka_ref.shape[0]
    for index in range(half):
        ka_ref[index] = add_low(keep_top[index], came_top[index])
        sa_ref[index] = add_low(keep_top[half + index], came_top[half + index])
        kb_ref[index] = add_low(keep_bottom[2 * index], came_bottom[2 * index])
        sb_ref[index] = add_low(keep_bottom[2 * index + 1], came_bottom[2 * index + 1])


def tiles(rows):
    return 3 if rows % 48 == 0 else 1


def fold_pieces_kernel(keep_top, keep_bottom, *refs):
    pieces = keep_top.shape[0]
    top, bottom, outs = refs[:pieces], refs[pieces : 2 * pieces], refs[2 * pieces :]
    ka_ref, sa_ref, kb_ref, sb_ref = outs
    half = pieces // 2
    for index in range(half):
        ka_ref[index] = add_low(keep_top[index], top[index][...])
        sa_ref[index] = add_low(keep_top[half + index], top[half + index][...])
        kb_ref[index] = add_low(keep_bottom[2 * index], bottom[2 * index][...])
        sb_ref[index] = add_low(keep_bottom[2 * index + 1], bottom[2 * index + 1][...])


def fold(keep, arrived):
    pieces, rows, width = keep.shape
    steps = tiles(rows // 2)
    tile = rows // 2 // steps
    top = pl.BlockSpec((pieces, tile, width), lambda i: (0, i, 0))
    bottom = pl.BlockSpec((pieces, tile, width), lambda i: (0, steps + i, 0))
    one_top = pl.BlockSpec((tile, width), lambda i: (i, 0))
    one_bottom = pl.BlockSpec((tile, width), lambda i: (steps + i, 0))
    ka, sa, kb, sb = launch(
        fold_pieces_kernel,
        (steps,),
        [],
        [keep, keep, *arrived, *arrived],
        [top, bottom] + [one_top] * pieces + [one_bottom] * pieces,
        [pl.BlockSpec((pieces // 2, tile, width), lambda i: (0, i, 0))] * 4,
        [shape((pieces // 2, rows // 2, width), BF16)] * 4,
        [],
        cost(pieces * rows * width, 6 * pieces * rows * width),
        "fold",
    )
    return [[ka, sa], [kb, sb]]


def send_links(state, step):
    bits = lax.axis_size("seq").bit_length() - 1
    return [
        [kept, swap(sent, "seq", bit)] for (kept, sent), bit in zip(state, (step, bits - step))
    ]


def split(state, carry=()):
    pieces, rows, width = state[0][0].shape
    steps = tiles(rows)
    spec = pl.BlockSpec((pieces, rows // steps, width), lambda i: (0, i, 0))
    out = pl.BlockSpec((pieces // 2, rows // steps, width), lambda i: (0, i, 0))
    ka, sa, kb, sb, *carried = launch(
        fold_kernel,
        (steps,),
        [],
        [state[0][0], state[1][0], state[0][1], state[1][1]],
        [spec] * 4,
        [out] * 4,
        [shape((pieces // 2, rows, width), BF16)] * 4,
        [],
        cost(pieces * rows * width, 12 * pieces * rows * width),
        "split",
        carry,
    )
    return [[ka, sa], [kb, sb]], carried


def cross_kernel(place_ref, ka_ref, kb_ref, ca_ref, cb_ref, kept_ref, sent_ref):
    high = (place_ref[0] & 1) == 1
    first = add_low(ka_ref[0], ca_ref[0])
    second = add_low(kb_ref[0], cb_ref[0])
    kept_ref[...] = jnp.where(high, second, first)
    sent_ref[...] = jnp.where(high, first, second)


def cross(place, state, carry=()):
    _, rows, width = state[0][0].shape
    steps = tiles(rows)
    spec = pl.BlockSpec((1, rows // steps, width), lambda i, *_: (0, i, 0))
    return launch(
        cross_kernel,
        (steps,),
        [place],
        [state[0][0], state[1][0], state[0][1], state[1][1]],
        [spec] * 4,
        [pl.BlockSpec((rows // steps, width), lambda i, *_: (i, 0))] * 2,
        [shape((rows, width), BF16)] * 2,
        [],
        cost(rows * width, 12 * rows * width),
        "cross",
        carry,
    )


def halve_kernel(bit, place_ref, kept_ref, came_ref, next_ref, sent_ref):
    high = ((place_ref[0] >> bit) & 1) == 1
    rows = next_ref.shape[0]
    first = add_low(kept_ref[:rows], came_ref[:rows])
    second = add_low(kept_ref[rows:], came_ref[rows:])
    next_ref[...] = jnp.where(high, second, first)
    sent_ref[...] = jnp.where(high, first, second)


def halve(place, bit, kept, came, carry):
    rows, width = kept.shape
    return launch(
        functools.partial(halve_kernel, bit),
        (1,),
        [place],
        [kept, came],
        [whole(kept.shape)] * 2,
        [whole((rows // 2, width))] * 2,
        [shape((rows // 2, width), BF16)] * 2,
        [],
        cost(rows * width, 6 * rows * width),
        "halve",
        carry,
    )


def add_kernel(kept_ref, came_ref, out_ref):
    out_ref[...] = add_low(kept_ref[...], came_ref[...])


def add(kept, came):
    return launch(
        add_kernel,
        (1,),
        [],
        [kept, came],
        [whole(kept.shape)] * 2,
        whole(kept.shape),
        shape(kept.shape, BF16),
        [],
        cost(kept.size, 6 * kept.size),
        "add",
    )


def assemble_kernel(bit, place_ref, held_ref, came_ref, out_ref):
    high = ((place_ref[0] >> bit) & 1) == 1
    rows = held_ref.shape[0]
    held, came = held_ref[...], came_ref[...]
    out_ref[:rows] = jnp.where(high, came, held)
    out_ref[rows:] = jnp.where(high, held, came)


def assemble(place, bit, held, came):
    rows, width = held.shape
    return launch(
        functools.partial(assemble_kernel, bit),
        (1,),
        [place],
        [held, came],
        [whole(held.shape)] * 2,
        whole((2 * rows, width)),
        shape((2 * rows, width), BF16),
        [],
        cost(rows * width, 8 * rows * width),
        "assemble",
    )


def finish_kernel(layout, place_ref, held_ref, came_ref, *out_refs):
    high = (place_ref[0] & 1) == 1
    rows = held_ref.shape[0]
    for begin, size, out, index in layout:
        part = slice(begin % rows, begin % rows + size)
        held, came = held_ref[part].astype(F32), came_ref[part].astype(F32)
        out_refs[out][index] = jnp.where(high == (begin < rows), came, held)


def cut(layout, rows):
    for begin, size, out, index in layout:
        edges = [begin, begin + size]
        if begin < rows < begin + size:
            edges.insert(1, rows)
        for low, high in zip(edges, edges[1:]):
            yield low, high - low, out, index[:-2] + (slice(low - begin, high - begin), index[-1])


def finish(place, held, came, layout, outs):
    layout = list(cut(layout, held.shape[0]))
    return launch(
        functools.partial(finish_kernel, layout),
        (1,),
        [place],
        [held, came],
        [whole(held.shape)] * 2,
        [whole(dims) for dims in outs],
        [shape(dims, F32) for dims in outs],
        [],
        cost(held.size, 16 * held.size),
        "finish",
    )


def across_halves(place, kept, sent, layout, outs):
    bits = lax.axis_size("batch").bit_length() - 1
    came = swap(sent, "batch", 0)
    carry = yield
    for bit in range(1, bits):
        kept, sent, *carry = halve(place, bit, kept, came, carry or ())
        came = swap(sent, "batch", bit)
        carry = yield carry
    held = add(kept, came)
    for bit in reversed(range(bits)):
        came = swap(held, "batch", bit)
        yield
        if bit:
            held = assemble(place, bit, held, came)
    yield finish(place, held, came, layout, outs)


def deal_kernel(place_ref, ka_ref, kb_ref, ca_ref, cb_ref, *refs):
    outs, sum_ref = refs[:-1], refs[-1]
    rows, part = ka_ref.shape[1], outs[0].shape[0]
    sum_ref[:rows] = add_low(ka_ref[0], ca_ref[0])
    sum_ref[rows:] = add_low(kb_ref[0], cb_ref[0])
    for mask, out_ref in enumerate(outs):
        start = pl.multiple_of((place_ref[0] ^ mask) * part, 16)
        out_ref[...] = sum_ref[pl.ds(start, part), :]


def total_kernel(*refs):
    total = refs[0][...].astype(F32)
    for ref in refs[1:-1]:
        total += ref[...].astype(F32)
    refs[-1][...] = total.astype(BF16)


def spread_kernel(layout, parts, place_ref, *refs):
    ins, outs, all_ref = refs[:parts], refs[parts:-1], refs[-1]
    rows = ins[0].shape[0]
    for mask, ref in enumerate(ins):
        start = pl.multiple_of((place_ref[0] ^ mask) * rows, 16)
        all_ref[pl.ds(start, rows), :] = ref[...]
    for begin, size, out, index in layout:
        outs[out][index] = all_ref[begin : begin + size].astype(F32)


def across_direct(place, state, layout, outs):
    parts = lax.axis_size("batch")
    _, rows, width = state[0][0].shape
    part = (2 * rows // parts, width)
    ends = [(mask, [(i, i ^ mask) for i in range(parts)]) for mask in range(1, parts)]
    pieces = launch(
        deal_kernel,
        (1,),
        [place],
        [state[0][0], state[1][0], state[0][1], state[1][1]],
        [whole(state[0][0].shape)] * 4,
        [whole(part)] * parts,
        [shape(part, BF16)] * parts,
        [pltpu.VMEM((2 * rows, width), BF16)],
        cost(rows * width, 12 * rows * width),
        "deal",
    )
    came = [lax.ppermute(pieces[mask], "batch", pairs) for mask, pairs in ends]
    yield
    held = launch(
        total_kernel,
        (1,),
        [],
        [pieces[0], *came],
        [whole(part)] * parts,
        whole(part),
        shape(part, BF16),
        [],
        cost(rows * width, 5 * rows * width),
        "total",
    )
    came = [lax.ppermute(held, "batch", pairs) for _, pairs in ends]
    yield
    yield launch(
        functools.partial(spread_kernel, layout, parts),
        (1,),
        [place],
        [held, *came],
        [whole(part)] * parts,
        [whole(dims) for dims in outs],
        [shape(dims, F32) for dims in outs],
        [pltpu.VMEM((2 * rows, width), BF16)],
        cost(rows * width, 12 * rows * width),
        "spread",
    )


def last(steps):
    result = None
    for result in steps:
        pass
    return result if isinstance(result, (list, tuple)) else [result]


def neighbours(first, last):
    count = lax.axis_size("seq")
    up = [(i, i + 1) for i in range(count - 1)]
    down = [(target, source) for source, target in up]
    return lax.ppermute(last, "seq", up), lax.ppermute(first, "seq", down)


def local(
    hidden, char_ids, group_ids, word_lengths, qkv_weight, out_weight, up_weight, ffn_bias,
    down_weight, gru_weight, gate_bias, candidate_bias, char_weight, conv_weight, char_table,
    norm_gain, norm_shift, tok_grad, char_grad,
):
    count = lax.axis_size("seq")
    bits = count.bit_length() - 1
    me = lax.axis_index("seq").astype(jnp.int32)
    seqs, toks, width = hidden.shape
    total = seqs * toks
    half = width // 2
    blk = width // count
    share = ffn_bias.shape[0]
    table_rows = char_table.shape[0]
    chars = char_ids.shape[1]
    reverse = [int(format(i, f"0{bits}b")[::-1], 2) for i in range(count)]
    order = jnp.asarray(reverse, jnp.int32) ^ me
    slot = sum(
        (((jnp.arange(count, dtype=jnp.int32) ^ me) >> b) & 1) << (bits - 1 - b) for b in range(bits)
    )
    me_one = me.reshape(1)

    place = lax.axis_index("batch").astype(jnp.int32).reshape(1)
    LATEST.clear()

    table_at = share
    small_at = table_at + table_rows
    block_at = small_at + 16
    block_at += -block_at % blk
    pack_rows = block_at + 11 * blk
    small = jnp.concatenate(
        [norm_gain.T, norm_shift.T, gate_bias[None], candidate_bias[None]], 0
    )
    small = jnp.pad(small, ((0, 6), (0, width - blk)))
    small = small.at[10, :share].set(ffn_bias)
    arrays = [
        down_weight, char_table, small, gru_weight, qkv_weight, char_weight, out_weight, up_weight
    ]
    at_block = block_at // blk
    at_gru, at_qkv, at_char, at_out, at_up = (at_block + i for i in (0, 2, 5, 6, 7))
    layout = [0, table_at, small_at] + [i * blk for i in (at_gru, at_qkv, at_char, at_out, at_up)]
    at_table, at_down = table_at // table_rows, 0
    first = pack(arrays, layout, pack_rows, width)
    third = pack(
        [conv_weight[k] for k in range(3)], [k * 4 * blk for k in range(3)], 12 * blk, width
    )
    first = lax.all_gather(first, "seq", axis=0)
    third = lax.all_gather(third, "seq", axis=0)
    vectors = (
        first[:, small_at : small_at + 10, :blk].astype(F32).transpose(1, 0, 2).reshape(10, width)
    )
    bias_up = first[:, small_at + 10, :share].astype(F32).reshape(1, -1)
    norms = vectors

    rows = hidden.reshape(total, width)
    words = word_lengths.reshape(seqs, toks)
    ends = jnp.cumsum(words, axis=1)
    starts = ends - words
    lens = words.astype(F32)[..., None]

    qkv = qkv_call(rows, first, at_qkv, seqs, count)
    qkv = lax.all_to_all(qkv, "seq", 0, 0, tiled=True)
    z, c, block_totals = gates_call(group_ids, char_ids, first, at_gru, at_table, vectors)
    gathered = [block_totals] + [
        lax.ppermute(block_totals, "seq", [(i, i ^ mask) for i in range(count)])
        for mask in range(1, count)
    ]
    step = 512
    mixture, totals = attend_call(qkv, step)
    mixture = lax.all_to_all(mixture, "seq", 0, 0, tiled=True)
    gathered = collect(me_one, gathered)
    prior, pooled, proj, proj_low = states_call(
        me_one, z, c, gathered, starts[..., None], ends[..., None], lens, first, at_char, 2
    )
    mix_t, normal0, rstd0, normed, active, slope, normal1, rstd1, f_low = ffn_call(
        mixture, rows, first, at_out, at_up, at_down, bias_up, norms, seqs
    )

    def edges(left, right):
        joined = [v.reshape(seqs, toks, width) for v in (left, right)]
        return (
            jnp.concatenate([v[:, :1] for v in joined], -1),
            jnp.concatenate([v[:, -1:] for v in joined], -1),
        )

    low, high = neighbours(*edges(f_low, proj_low))
    other = [swap(v, "seq", 0) for v in (f_low, proj_low)]
    tok_out, char_out, d_tok, d_char, d_merged, sums23, begin, end, *other = conv_call(
        f_low, proj_low, normal1, proj, norms, low, high, third,
        tok_grad.reshape(total, width), char_grad.reshape(total, width), seqs, other,
    )

    low, high = neighbours(begin, end)
    other_dm = swap(d_merged, "seq", 0)

    def onward(state, first_link, carry=()):
        for link in range(first_link + 1, bits):
            state, carry = split(state, carry)
            state = send_links(state, link)
        return state, carry

    def columns_of(begin, blocks, out):
        return [
            (begin + j * blk, blk, out, (slice(None), slice(j * width, (j + 1) * width)))
            for j in range(blocks)
        ]

    everything = (slice(None), slice(None))
    double = 2 * blk
    unit = 8 * lax.axis_size("batch")
    height = max(3 * blk + table_rows, 4 * blk + SMALL_ROWS)
    height += -height % unit
    d_proj, d_ffn, sums1, begin, end = conv_back_call(
        d_merged, low, high, third, d_tok, d_char, normal1, rstd1, norms, seqs, [begin, end]
    )
    far_high = lax.ppermute(begin, "seq", [(i, i - 2) for i in range(2, count)])
    far_low = lax.ppermute(end, "seq", [(i, i + 2) for i in range(count - 2)])
    conv_state = conv_weight_call(
        order, (f_low, proj_low), other, d_merged, low, high, other_dm, begin, end, far_low,
        far_high, count,
    )
    conv_state = send_links(conv_state, 1)
    ds, back_totals = states_back_call(
        d_proj, first, at_char, lens, starts[:, None, :], ends[:, None, :], z
    )
    send, keep, d_bias_up, d_attn, d_attended, sums0, d_mix = ffn_back_call(
        slot, order, d_ffn, active, slope, normed, normal0, rstd0, norms, first, at_out, at_up,
        at_down, back_totals, seqs,
    )
    d_mix = lax.all_to_all(d_mix, "seq", 0, 0, tiled=True)
    ffn_came = [swap(piece, "seq", 0) for piece in send]
    conv_state, _ = onward(conv_state, 1)
    ffn_state = fold(keep, ffn_came)
    ffn_state = send_links(ffn_state, 1)
    d_qkv = attend_back_call(qkv, d_mix, totals, step)
    d_qkv = lax.all_to_all(d_qkv, "seq", 0, 0, tiled=True)
    conv_steps = across_halves(
        place, *cross(place, conv_state),
        [
            (r * double, double, 0, (r // 2, slice(None), slice(r % 2 * width, (r % 2 + 1) * width)))
            for r in range(6)
        ],
        [(3, double, 2 * width)],
    )
    next(conv_steps)
    sums, d_bias = gates_back_call(
        me_one, group_ids, z, c, prior, ds, gathered, d_mix, char_ids,
        count * table_rows // NCHAR, 2,
    )
    ffn_state, _ = onward(ffn_state, 1)
    rest_send, rest_keep = rest_call(
        order, first, at_table, at_gru, sums, mix_t, d_attended, height
    )
    next(conv_steps)
    hidden_grad, qkv_send, qkv_keep = qkv_back_call(
        order, d_qkv, rows, first, at_qkv, d_attn, pooled, d_proj,
        [sums0, sums1, sums23, d_bias, d_bias_up], seqs, height,
    )
    kept, sent, *both = cross(place, ffn_state, (rest_send, qkv_send))
    rest_came, qkv_came = (swap(send, "seq", 0) for send in both)
    ffn_steps = across_halves(
        place, kept, sent,
        [(0, share, 0, everything), *columns_of(share, 4, 1)],
        [(share, width), (blk, 4 * width)],
    )
    next(ffn_steps)
    next(conv_steps)
    last_state, _ = split([[rest_keep, rest_came], [qkv_keep, qkv_came]])
    last_state = send_links(last_state, 1)
    next(ffn_steps)
    next(conv_steps)
    last_state, _ = onward(last_state, 1)
    next(ffn_steps)
    (conv_grad,) = last(conv_steps)
    last_steps = across_direct(
        place, last_state,
        [
            *columns_of(0, 2, 0),
            (2 * blk, table_rows, 1, everything),
            (2 * blk + table_rows, blk, 2, everything),
            *columns_of(height, 3, 3),
            (height + 3 * blk, blk, 4, everything),
            (height + 4 * blk, SMALL_ROWS, 5, everything),
        ],
        [
            (blk, 2 * width), (table_rows, width), (blk, width), (blk, 3 * width), (blk, width),
            (SMALL_ROWS, width),
        ],
    )
    next(last_steps)
    next(ffn_steps)
    next(last_steps)
    down_grad, up_grad = last(ffn_steps)
    gru_grad, table_grad, out_grad, qkv_grad, char_grad_w, small_sum = last(last_steps)

    mine = lax.dynamic_slice(small_sum, (0, me * blk), (10, blk))
    d_gain, d_shift, d_gate_b, d_cand_b = mine[:4].T, mine[4:8].T, mine[8], mine[9]
    d_ffn_b = lax.dynamic_slice(small_sum[10:14].reshape(-1), (me * share,), (share,))
    shape_out = (seqs, toks, width)
    return (
        tok_out.reshape(shape_out),
        char_out.reshape(shape_out),
        hidden_grad.reshape(shape_out),
        qkv_grad,
        out_grad,
        up_grad,
        d_ffn_b,
        down_grad,
        gru_grad,
        d_gate_b,
        d_cand_b,
        char_grad_w,
        conv_grad,
        table_grad,
        d_gain,
        d_shift,
    )


def solution(mesh):
    rows, columns = P("seq", None), P("batch", "seq", None)
    return jax.shard_map(
        local,
        mesh=mesh,
        in_specs=(
            columns, P("batch", "seq"), P("batch"), columns, rows, rows, rows, P("seq"), rows,
            rows, P("seq"), P("seq"), rows, P(None, "seq", None), rows, rows, rows, columns,
            columns,
        ),
        out_specs=(
            columns, columns, columns, rows, rows, rows, P("seq"), rows, rows, P("seq"), P("seq"),
            rows, P(None, "seq", None), rows, rows, rows,
        ),
        check_vma=False,
    )
```

```python
import functools

import jax
import jax.numpy as jnp
from jax import lax
from jax.experimental import pallas as pl
from jax.experimental.pallas import tpu as pltpu
from jax.sharding import PartitionSpec as P

HEADS = 12
NCHAR = 256
NORM_EPS = 1e-06
LANES = 128
SMALL_ROWS = 16
RIDE = 32
SCALE = 1000
F32 = jnp.float32
BF16 = jnp.bfloat16
VMEM_BYTES = 40 << 20


def dot(left, right, left_dim, right_dim):
    return lax.dot_general(
        left, right, (((left_dim,), (right_dim,)), ((), ())), preferred_element_type=F32
    )


def params(grid_rank):
    return pltpu.CompilerParams(
        dimension_semantics=("arbitrary",) * grid_rank, vmem_limit_bytes=VMEM_BYTES
    )


def shape(dims, dtype):
    return jax.ShapeDtypeStruct(dims, dtype)


def stored(dims, dtype):
    return pltpu.HBM(dims, dtype) if PLACED else shape(dims, dtype)


def whole(dims):
    return pl.BlockSpec(dims, lambda *_: (0,) * len(dims))


def cost(flops, nbytes):
    return pl.CostEstimate(flops=int(flops) * SCALE, bytes_accessed=int(nbytes) * SCALE, transcendentals=0)


NEAR = []
LATEST = []
PLACED = []
TOKEN = jax.ShapeDtypeStruct((8, LANES), F32)


def launch(
    body, grid, prefetch, inputs, in_specs, out_specs, out_shape, scratch, price, name, carry=()
):
    deps = [pltpu.with_memory_space_constraint(v, pltpu.HBM) for v in LATEST]
    single = not isinstance(out_shape, (list, tuple))
    outs = [out_shape] if single else list(out_shape)
    specs = [out_specs] if single else list(out_specs)
    lead = len(prefetch) + len(inputs)
    extra = len(carry) + len(deps)
    anywhere = pl.BlockSpec(memory_space=pl.ANY)

    def kernel(*refs):
        own = refs[lead + extra :]
        body(*refs[:lead], *own[: len(outs)], *own[len(outs) + len(carry) + 1 :])

    inputs = [
        v
        if not PLACED or v.size < 1 << 16 or any(v is near for near in NEAR)
        else pltpu.with_memory_space_constraint(v, pltpu.HBM)
        for v in inputs
    ]
    results = pl.pallas_call(
        kernel,
        grid_spec=pltpu.PrefetchScalarGridSpec(
            num_scalar_prefetch=len(prefetch),
            grid=grid,
            in_specs=list(in_specs) + [anywhere] * extra,
            out_specs=specs + [anywhere] * (len(carry) + 1),
            scratch_shapes=scratch,
        ),
        out_shape=outs + [stored(v.shape, v.dtype) for v in (*carry, TOKEN)],
        input_output_aliases={lead + i: len(outs) + i for i in range(len(carry))},
        compiler_params=params(len(grid)),
        cost_estimate=price,
        name=name,
    )(*prefetch, *inputs, *carry, *deps)
    NEAR.extend(v for v, out in zip(results, outs) if isinstance(out, jax.ShapeDtypeStruct))
    *results, LATEST[:] = *results[:-1], results[-1:]
    return results[0] if len(results) == 1 else results


def flat_block(ref):
    block = ref[...]
    return block.reshape(block.shape[0] * block.shape[1], block.shape[2])


def norm_forward(values):
    center = values - jnp.mean(values, -1, keepdims=True)
    rstd = lax.rsqrt(jnp.mean(center * center, -1, keepdims=True) + NORM_EPS)
    return center * rstd, rstd


def norm_backward(normal, rstd, gain, gradient):
    scaled = gradient * gain
    first = jnp.mean(scaled, -1, keepdims=True)
    second = jnp.mean(scaled * normal, -1, keepdims=True)
    return rstd * (scaled - first - normal * second)


def column_sum(values):
    return jnp.sum(values, 0, keepdims=True)


def gelu_parts(values):
    size = jnp.abs(values) * 0.7071067811865476
    bell = jnp.exp(-size * size)
    t = 1.0 / (1.0 + 0.3275911 * size)
    series = t * (
        0.254829592
        + t * (-0.284496736 + t * (1.421413741 + t * (-1.453152027 + t * 1.061405429)))
    )
    tail = 0.5 * series * bell
    phi_sum = jnp.where(values < 0, tail, 1.0 - tail)
    return values * phi_sum, phi_sum + values * (bell * 0.3989422804014327)


def qkv_kernel(seqs, toks, per, x_ref, w_ref, o_ref):
    acc = dot(x_ref[...], flat_block(w_ref), 1, 0)
    turned = acc.T.astype(BF16)
    width = turned.shape[0] // HEADS
    for s in range(seqs):
        for h in range(HEADS):
            pair = s * HEADS + h
            o_ref[pair // per, pair % per, 0] = turned[
                h * width : (h + 1) * width, s * toks : (s + 1) * toks
            ]


def qkv_call(rows, packed, base, seqs, count):
    total, width = rows.shape
    toks = total // seqs
    per = seqs * HEADS // count
    head = width // HEADS
    blk = width // count
    return launch(
        functools.partial(qkv_kernel, seqs, toks, per),
        (3,),
        [],
        [rows, packed],
        [ whole(rows.shape), pl.BlockSpec((count, blk, width), lambda j: (0, base + j, 0)), ],
        pl.BlockSpec((count, per, 1, head, toks), lambda j: (0, 0, j, 0, 0)),
        stored((count, per, 3, head, toks), BF16),
        [],
        cost(6 * total * width * width, 6 * width * width + 8 * total * width),
        "qkv",
    )


def spread(ref, index):
    return jnp.concatenate([ref[(i, *index)] for i in range(ref.shape[0])], axis=1)


def attend_kernel(step, scale, x_ref, o_ref, total_ref):
    queries = spread(x_ref, (0, 0)) * scale
    keys = spread(x_ref, (0, 1)).T
    values = spread(x_ref, (0, 2))
    toks = x_ref.shape[-1]
    for begin in range(0, queries.shape[1], step):
        scores = dot(keys, queries[:, begin : begin + step], 1, 0)
        highest = jnp.max(scores, 0, keepdims=True)
        expo = jnp.exp(scores - highest)
        totals = jnp.sum(expo, 0, keepdims=True)
        mixture = (dot(values, expo.astype(BF16), 1, 0) / totals).astype(BF16)
        total_ref[0, :, begin : begin + step] = highest + jnp.log(totals)
        for at in range(0, step, toks):
            o_ref[(begin + at) // toks, 0] = mixture[:, at : at + toks]


def attend_call(qkv, step):
    count, per, _, head, toks = qkv.shape
    length = count * toks
    scale = head**-0.5
    return launch(
        functools.partial(attend_kernel, step, scale),
        (per,),
        [],
        [qkv],
        [pl.BlockSpec((count, 1, 3, head, toks), lambda p: (0, p, 0, 0, 0))],
        [ pl.BlockSpec((count, 1, head, toks), lambda p: (0, p, 0, 0)), pl.BlockSpec((1, 1, length), lambda p: (p, 0, 0)), ],
        [stored((count, per, head, toks), BF16), shape((per, 1, length), F32)],
        [],
        cost(16 * per * length * length * head, 8 * per * length * head),
        "attend",
    )


def attend_back_kernel(step, scale, x_ref, g_ref, total_ref, o_ref):
    queries = spread(x_ref, (0, 0)) * scale
    keys_t = spread(x_ref, (0, 1))
    keys = keys_t.T
    values = spread(x_ref, (0, 2)).T
    grads = spread(g_ref, ())
    toks = x_ref.shape[-1]
    length = queries.shape[1]
    d_keys = jnp.zeros(queries.shape, F32)
    d_values = jnp.zeros(queries.shape, F32)
    for begin in range(0, length, step):
        query = queries[:, begin : begin + step]
        grad = grads[:, begin : begin + step]
        scores = dot(keys, query, 1, 0)
        probability = jnp.exp(scores - total_ref[0, :, begin : begin + step])
        d_prob = dot(values, grad, 1, 0)
        centered = jnp.sum(probability * d_prob, 0, keepdims=True)
        d_scores = (probability * (d_prob - centered)).astype(BF16)
        d_values += dot(grad, probability.astype(BF16), 1, 1)
        d_keys += dot(query, d_scores, 1, 1)
        d_query = (dot(keys_t, d_scores, 1, 0) * scale).astype(BF16)
        for at in range(0, step, toks):
            o_ref[(begin + at) // toks, 0, 0] = d_query[:, at : at + toks]
    d_keys = d_keys.astype(BF16)
    d_values = d_values.astype(BF16)
    for i in range(length // toks):
        o_ref[i, 0, 1] = d_keys[:, i * toks : (i + 1) * toks]
        o_ref[i, 0, 2] = d_values[:, i * toks : (i + 1) * toks]


def attend_back_call(qkv, grads, totals, step):
    count, per, _, head, toks = qkv.shape
    length = count * toks
    scale = head**-0.5
    return launch(
        functools.partial(attend_back_kernel, step, scale),
        (per,),
        [],
        [qkv, grads, totals],
        [ pl.BlockSpec((count, 1, 3, head, toks), lambda p: (0, p, 0, 0, 0)), pl.BlockSpec((count, head, toks), lambda p: (0, p, 0)), pl.BlockSpec((1, 1, length), lambda p: (p, 0, 0)), ],
        pl.BlockSpec((count, 1, 3, head, toks), lambda p: (0, p, 0, 0, 0)),
        stored(qkv.shape, BF16),
        [],
        cost(40 * per * length * length * head, 14 * per * length * head),
        "attend_back",
    )


def ffn_kernel(
    seqs,
    o_ref,
    x_ref,
    w_out_ref,
    w_up_ref,
    w_down_ref,
    bias_ref,
    norms_ref,
    mix_ref,
    normal0_ref,
    rstd0_ref,
    a_ref,
    g_ref,
    slope_ref,
    normal1_ref,
    rstd1_ref,
    f_ref,
    acc_ref,
):
    j = pl.program_id(0)
    per = o_ref.shape[1]
    head, toks = o_ref.shape[2:]

    @pl.when(j == 0)
    def _():
        for s in range(seqs):
            for h in range(HEADS):
                pair = s * HEADS + h
                mix_ref[h * head : (h + 1) * head, s * toks : (s + 1) * toks] = o_ref[
                    pair // per, pair % per
                ]
        attended = dot(mix_ref[...].T, flat_block(w_out_ref), 1, 0)
        normal, rstd = norm_forward(x_ref[...].astype(F32) + attended)
        normal0_ref[...] = normal
        rstd0_ref[...] = rstd
        normed = normal * norms_ref[0:1] + norms_ref[4:5]
        a_ref[...] = normed.astype(BF16)
        acc_ref[...] = normed

    up = dot(a_ref[...], flat_block(w_up_ref), 1, 0) + bias_ref[...]
    active, slope = gelu_parts(up)
    active = active.astype(BF16)
    g_ref[...] = active
    slope_ref[...] = slope
    acc_ref[...] += dot(active, flat_block(w_down_ref), 1, 0)

    @pl.when(j == pl.num_programs(0) - 1)
    def _():
        normal, rstd = norm_forward(acc_ref[...])
        normal1_ref[...] = normal
        rstd1_ref[...] = rstd
        f_ref[...] = (normal * norms_ref[1:2] + norms_ref[5:6]).astype(BF16)


def ffn_call(mixture, rows, packed, at_out, at_up, at_down, bias, norms, seqs):
    count, per, head, toks = mixture.shape
    total, width = rows.shape
    hidden = bias.shape[1]
    chunks = hidden // width
    blk = width // count
    owners = count // chunks
    return launch(
        functools.partial(ffn_kernel, seqs),
        (chunks,),
        [],
        [mixture, rows, packed, packed, packed, bias, norms],
        [ whole(mixture.shape), whole(rows.shape), pl.BlockSpec((count, blk, width), lambda j: (0, at_out, 0)), pl.BlockSpec((count, blk, width), lambda j: (0, at_up + j, 0)), pl.BlockSpec((owners, hidden // count, width), lambda j: (j, at_down, 0)), pl.BlockSpec((1, width), lambda j: (0, j)), whole(norms.shape), ],
        [ whole((width, total)), whole((total, width)), whole((total, 1)), whole((total, width)), pl.BlockSpec((total, width), lambda j: (0, j)), pl.BlockSpec((total, width), lambda j: (0, j)), whole((total, width)), whole((total, 1)), whole((total, width)), ],
        [ stored((width, total), BF16), stored((total, width), F32), stored((total, 1), F32), stored((total, width), BF16), stored((total, hidden), BF16), stored((total, hidden), F32), shape((total, width), F32), shape((total, 1), F32), shape((total, width), BF16)],
        [pltpu.VMEM((total, width), F32)],
        cost( 2 * total * width * (width + 2 * hidden), 4 * hidden * width + 10 * total * hidden ),
        "ffn",
    )


def ffn_back_kernel(
    seqs,
    slot_ref,
    order_ref,
    d_ref,
    g_ref,
    slope_ref,
    a_ref,
    normal_ref,
    rstd_ref,
    norms_ref,
    w_out_ref,
    w_up_ref,
    w_down_ref,
    total_ref,
    mix_ref,
    pooled_ref,
    d_proj_ref,
    *refs,
):
    j = pl.program_id(0)
    count, blk, width = w_up_ref.shape
    owners, share, _ = w_down_ref.shape
    half = count // 2
    send_refs, refs = refs[:half], refs[half:]
    keep_ref, bias_ref, d_attn_ref, sums_ref, d_mix_ref = refs[:5]
    db_ref, at_ref, acc_ref, part_ref = refs[5:]

    @pl.when(j == 0)
    def _():
        db_ref[...] = d_ref[...].astype(BF16)
        at_ref[...] = a_ref[...].T
        acc_ref[...] = d_ref[...]

    part_ref[...] = dot(g_ref[...].T, db_ref[...], 1, 0)
    for i in range(owners):
        slot = slot_ref[j * owners + i]
        piece = part_ref[i * share : (i + 1) * share, :].astype(BF16)

        @pl.when(slot < half)
        def _():
            keep_ref[slot, 0:share, :] = piece

        for at, send_ref in enumerate(send_refs):

            @pl.when(slot == half + at)
            def _():
                send_ref[0:share, :] = piece

    d_up = (dot(db_ref[...], flat_block(w_down_ref), 1, 1) * slope_ref[...]).astype(BF16)
    bias_ref[...] = column_sum(d_up.astype(F32))
    part_ref[...] = dot(at_ref[...], d_up, 1, 0)
    place = pl.ds(pl.multiple_of(share + j * blk, 16), blk)
    for pos in range(count):
        piece = part_ref[pl.ds(pl.multiple_of(order_ref[pos] * blk, 16), blk), :].astype(BF16)
        if pos < half:
            keep_ref[pos, place, :] = piece
        else:
            send_refs[pos - half][place, :] = piece
    acc_ref[...] += dot(d_up, flat_block(w_up_ref), 1, 1)

    @pl.when(j == pl.num_programs(0) - 1)
    def _():
        gradient = acc_ref[...]
        normal = normal_ref[...]
        sums_ref[0:1, :] = column_sum(gradient * normal)
        sums_ref[1:2, :] = column_sum(gradient)
        d_sum = norm_backward(normal, rstd_ref[...], norms_ref[0:1], gradient)
        d_attn_ref[...] = d_sum
        low = d_sum.astype(BF16)

        def put(row):
            for pos in range(count):
                start = pl.multiple_of(order_ref[pos] * blk, 16)
                piece = part_ref[pl.ds(start, blk), :].astype(BF16)
                if pos < half:
                    keep_ref[pos, row : row + blk, :] = piece
                else:
                    send_refs[pos - half][row : row + blk, :] = piece

        base = keep_ref.shape[1] - 2 * blk
        part_ref[...] = dot(mix_ref[...], low, 1, 0)
        put(base)
        part_ref[...] = dot(pooled_ref[...].T, d_proj_ref[...], 1, 0)
        put(base + blk)
        turned = dot(flat_block(w_out_ref), low, 1, 1).astype(BF16)
        per = seqs * HEADS // count
        head, toks = width // HEADS, d_mix_ref.shape[2]
        for s in range(seqs):
            for h in range(HEADS):
                pair = s * HEADS + h
                row = pair % per * head
                d_mix_ref[pair // per, row : row + head] = turned[
                    h * head : (h + 1) * head, s * toks : (s + 1) * toks
                ]
        rest = jnp.concatenate([total_ref[j] for j in range(total_ref.shape[0])], 0)
        rest = jnp.concatenate([rest, jnp.zeros((RIDE - rest.shape[0], LANES), F32)], 0)
        for part in range(3):
            low = rest.astype(BF16)
            rest = rest - low.astype(F32)
            row = per * head + part * RIDE
            for device in range(count):
                d_mix_ref[device, row : row + RIDE] = low


def ffn_back_call(
    slot, order, d_ffn, active, slope, normed, normal, rstd, norms, packed, at_out, at_up, at_down, totals, mixture, pooled, d_proj, seqs):
    total, width = d_ffn.shape
    hidden = active.shape[1]
    count = packed.shape[0]
    chunks = hidden // width
    blk = width // count
    share = hidden // count
    owners = count // chunks
    per = seqs * HEADS // count
    head = width // HEADS
    toks = total // seqs
    rows_out = share + (chunks + 2) * blk
    wide = pl.BlockSpec((total, width), lambda j, *_: (0, j))
    results = launch(
        functools.partial(ffn_back_kernel, seqs),
        (chunks,),
        [slot, order],
        [d_ffn, active, slope, normed, normal, rstd, norms, packed, packed, packed, totals, mixture, pooled, d_proj],
        [ whole(d_ffn.shape), wide, wide, whole(normed.shape), whole(normal.shape), whole(rstd.shape), whole(norms.shape), pl.BlockSpec((count, blk, width), lambda j, *_: (0, at_out, 0)), pl.BlockSpec((count, blk, width), lambda j, *_: (0, at_up + j, 0)), pl.BlockSpec((owners, share, width), lambda j, *_: (j, at_down, 0)), whole(totals.shape), whole(mixture.shape), whole(pooled.shape), whole(d_proj.shape), ],
        [ *[whole((rows_out, width))] * (count // 2), whole((count // 2, rows_out, width)), pl.BlockSpec((1, width), lambda j, *_: (0, j)), whole((total, width)), whole((2, width)), whole((count, per * head + 3 * RIDE, toks)), ],
        [ *[stored((rows_out, width), BF16)] * (count // 2), stored((count // 2, rows_out, width), BF16), stored((1, hidden), F32), stored((total, width), F32), stored((2, width), F32), stored((count, per * head + 3 * RIDE, toks), BF16), ],
        [ pltpu.VMEM((total, width), BF16), pltpu.VMEM((width, total), BF16), pltpu.VMEM((total, width), F32), pltpu.VMEM((width, width), F32), ],
        cost( 8 * total * width * hidden + 2 * total * width * width, 8 * hidden * width + 10 * total * hidden, ),
        "ffn_back",
    )
    return results[: count // 2], *results[count // 2 :]


def gates_kernel(
    seqs, groups_ref, ids_ref, back_ids_ref, table_ref, w_fwd_ref, w_rev_ref, bias_ref,
    z_ref, c_ref, totals_ref,
):
    s = pl.program_id(0)
    steps = ids_ref.shape[1]
    rows = 2 * seqs
    table = flat_block(table_ref)
    vocabulary = lax.broadcasted_iota(jnp.int32, (steps, NCHAR), 1)
    chunks = z_ref.shape[0]
    half = chunks * LANES
    for direction, (source, weight) in enumerate(((ids_ref, w_fwd_ref), (back_ids_ref, w_rev_ref))):
        onehot = jnp.where(source[0] == vocabulary, 1.0, 0.0).astype(BF16)
        embedded = dot(onehot, table, 1, 0).astype(BF16)
        gate_input = dot(embedded, flat_block(weight), 1, 0)
        own = slice(direction * half, (direction + 1) * half)
        update = jax.nn.sigmoid(gate_input[:, :half] + bias_ref[8:9, own])
        candidate = jnp.tanh(gate_input[:, half:] + bias_ref[9:10, own])
        place = pl.ds(s + direction * seqs, steps, stride=rows)
        for j in range(chunks):
            z_ref[j, place, :] = update[:, j * LANES : (j + 1) * LANES]
            c_ref[j, place, :] = candidate[:, j * LANES : (j + 1) * LANES]

    @pl.when(s == pl.num_programs(0) - 1)
    def _():
        def one(t, carry):
            states, products = carry
            place = pl.ds(pl.multiple_of(t * rows, rows), rows)
            new_states, new_products = [], []
            for j in range(chunks):
                update = z_ref[j, place, :]
                decay = 1.0 - update
                new_states.append(decay * states[j] + update * c_ref[j, place, :])
                new_products.append(products[j] * decay)
            return tuple(new_states), tuple(new_products)

        zero = jnp.zeros((rows, LANES), F32)
        states, products = lax.fori_loop(
            0, steps, one, ((zero,) * chunks, (zero + 1.0,) * chunks), unroll=8
        )
        for j in range(chunks):
            totals_ref[0, j] = products[j]
            totals_ref[1, j] = states[j]


def gates_call(groups, ids, packed, at_gru, at_table, bias):
    seqs, steps = ids.shape
    count, _, width = packed.shape
    blk = width // count
    table_rows = 4 * NCHAR // count
    per_group = NCHAR // table_rows
    chunks = width // 2 // LANES
    laid = (chunks, steps * 2 * seqs, LANES)
    return launch(
        functools.partial(gates_kernel, seqs),
        (seqs,),
        [groups],
        [ids[..., None], ids[:, ::-1, None], packed, packed, packed, bias],
        [ pl.BlockSpec((1, steps, 1), lambda s, g: (s, 0, 0)), pl.BlockSpec((1, steps, 1), lambda s, g: (s, 0, 0)), pl.BlockSpec((per_group, table_rows, width), lambda s, g: (g[s], at_table, 0)), pl.BlockSpec((count, blk, width), lambda s, g: (0, at_gru, 0)), pl.BlockSpec((count, blk, width), lambda s, g: (0, at_gru + 1, 0)), whole(bias.shape), ],
        [whole(laid), whole(laid), whole((2, chunks, 2 * seqs, LANES))],
        [stored(laid, F32), stored(laid, F32), stored((2, chunks, 2 * seqs, LANES), F32)],
        [],
        cost( 2 * seqs * steps * width * (2 * NCHAR + 2 * width), 16 * seqs * steps * width ),
        "gates",
    )


def entry_state(me, totals, products, rows, seqs, forward):
    count, chunks = products.shape[0], products.shape[1]
    first = lax.broadcasted_iota(jnp.int32, (rows, LANES), 0) < seqs
    result = []
    for j in range(chunks):
        state = jnp.zeros((rows, LANES), F32)
        for lap in range(count):
            up, down = lap, count - 1 - lap
            one, other = (up, down) if forward else (down, up)
            product = jnp.where(first, products[one, j], products[other, j])
            total = jnp.where(first, totals[one, j], totals[other, j])
            up_in, down_in = (up < me).astype(F32), (down > me).astype(F32)
            ahead = jnp.where(first, up_in, down_in) if forward else jnp.where(first, down_in, up_in)
            state = jnp.where(ahead > 0.5, product * state + total, state)
        result.append(state)
    return result


def states_kernel(
    seqs, me_ref, z_ref, c_ref, all_ref, starts_ref, ends_ref, lens_ref, w_ref,
    prior_ref, pooled_ref, proj_ref, proj_low_ref, hold_ref, state_ref, acc_ref,
):
    i = pl.program_id(0)
    last = pl.num_programs(0) - 1
    rows = 2 * seqs
    chunks = z_ref.shape[0]
    span = z_ref.shape[1] // rows
    toks = starts_ref.shape[1]
    half = chunks * LANES

    @pl.when(i == 0)
    def _():
        entry = entry_state(me_ref[0], all_ref[:, 1], all_ref[:, 0], rows, seqs, True)
        for j in range(chunks):
            state_ref[j] = entry[j]
        acc_ref[...] = jnp.zeros_like(acc_ref)

    def one(t, states):
        place = pl.ds(pl.multiple_of(t * rows, rows), rows)
        result = []
        for j in range(chunks):
            prior_ref[j, place, :] = states[j]
            update = z_ref[j, place, :]
            state = (1.0 - update) * states[j] + update * c_ref[j, place, :]
            hold_ref[j, place, :] = state
            result.append(state)
        return tuple(result)

    states = lax.fori_loop(0, span, one, tuple(state_ref[j] for j in range(chunks)), unroll=8)
    for j in range(chunks):
        state_ref[j] = states[j]
    count = lax.broadcasted_iota(jnp.int32, (toks, span), 1) + i * span
    for direction in range(2):
        place_of = count if direction == 0 else (last + 1) * span - 1 - count
        for s in range(seqs):
            member = jnp.where(
                (place_of >= starts_ref[s]) & (place_of < ends_ref[s]), 1.0, 0.0
            ).astype(BF16)
            held = jnp.concatenate(
                [
                    hold_ref[j, pl.ds(s + direction * seqs, span, stride=rows), :]
                    for j in range(chunks)
                ],
                axis=1,
            ).astype(BF16)
            acc_ref[s * toks : (s + 1) * toks, direction * half : (direction + 1) * half] += dot(
                member, held, 1, 0
            )

    @pl.when(i == last)
    def _():
        for s in range(seqs):
            rows_of = slice(s * toks, (s + 1) * toks)
            pooled_ref[rows_of, :] = (acc_ref[rows_of, :] / lens_ref[s]).astype(BF16)
        proj = dot(pooled_ref[...], flat_block(w_ref), 1, 0)
        proj_ref[...] = proj
        proj_low_ref[...] = proj.astype(BF16)


def collect_kernel(me_ref, *refs):
    for mask, ref in enumerate(refs[:-1]):
        refs[-1][me_ref[0] ^ mask] = ref[...]


def collect(me, parts):
    out = (len(parts), *parts[0].shape)
    return launch(
        collect_kernel,
        (1,),
        [me],
        parts,
        [whole(v.shape) for v in parts],
        whole(out),
        shape(out, parts[0].dtype),
        [],
        cost(0, 8 * len(parts) * parts[0].size),
        "collect",
    )


def states_call(me, z, c, gathered, starts, ends, lens, packed, at_char, parts):
    chunks, length, _ = z.shape
    seqs, toks, _ = starts.shape
    count, _, width = packed.shape
    blk = width // count
    span = length // parts
    total = seqs * toks
    stream = pl.BlockSpec((chunks, span, LANES), lambda i, *_: (0, i, 0))
    return launch(
        functools.partial(states_kernel, seqs),
        (parts,),
        [me],
        [z, c, gathered, starts, ends, lens, packed],
        [ stream, stream, whole(gathered.shape), whole(starts.shape), whole(ends.shape), whole(lens.shape), pl.BlockSpec((count, blk, width), lambda i, *_: (0, at_char, 0)), ],
        [stream] + [whole((total, width))] * 3,
        [stored(z.shape, F32), stored((total, width), BF16), stored((total, width), F32), shape((total, width), BF16), ],
        [ pltpu.VMEM((chunks, span, LANES), F32), pltpu.VMEM((chunks, 2 * seqs, LANES), F32), pltpu.VMEM((total, width), F32), ],
        cost(2 * total * width * (width + length // 8), 12 * chunks * length * LANES),
        "states",
    )


def states_back_kernel(
    seqs, d_ref, w_ref, lens_ref, starts_ref, ends_ref, z_ref, ds_ref, total_ref,
):
    rows = 2 * seqs
    chunks = z_ref.shape[0]
    steps = z_ref.shape[1] // rows
    toks = starts_ref.shape[2]
    half = chunks * LANES
    d_pooled = dot(d_ref[...], flat_block(w_ref), 1, 1)
    count = lax.broadcasted_iota(jnp.int32, (steps, toks), 0)
    for s in range(seqs):
        d_summed = (d_pooled[s * toks : (s + 1) * toks] / lens_ref[s]).astype(BF16)
        for direction in range(2):
            place_of = count if direction == 0 else steps - 1 - count
            member = jnp.where(
                (place_of >= starts_ref[s]) & (place_of < ends_ref[s]), 1.0, 0.0
            ).astype(BF16)
            d_states = dot(member, d_summed[:, direction * half : (direction + 1) * half], 1, 0)
            for j in range(chunks):
                ds_ref[j, pl.ds(s + direction * seqs, steps, stride=rows), :] = d_states[
                    :, j * LANES : (j + 1) * LANES
                ]

    def one(lap, carried):
        place = pl.ds(pl.multiple_of((steps - 1 - lap) * rows, rows), rows)
        return tuple(
            (1.0 - z_ref[j, place, :]) * (ds_ref[j, place, :] + carried[j]) for j in range(chunks)
        )

    zero = jnp.zeros((rows, LANES), F32)
    carried = lax.fori_loop(0, steps, one, (zero,) * chunks, unroll=8)
    for j in range(chunks):
        total_ref[j] = carried[j]


def states_back_call(d_proj, packed, at_char, lens, starts, ends, z):
    chunks, length, _ = z.shape
    seqs = starts.shape[0]
    count, _, width = packed.shape
    blk = width // count
    return launch(
        functools.partial(states_back_kernel, seqs),
        (1,),
        [],
        [d_proj, packed, lens, starts, ends, z],
        [ whole(d_proj.shape), pl.BlockSpec((count, blk, width), lambda i: (0, at_char, 0)), whole(lens.shape), whole(starts.shape), whole(ends.shape), whole(z.shape), ],
        [whole(z.shape), whole((chunks, 2 * seqs, LANES))],
        [stored(z.shape, F32), shape((chunks, 2 * seqs, LANES), F32)],
        [],
        cost( 2 * d_proj.shape[0] * width * (width + length // 8), 8 * chunks * length * LANES ),
        "states_back",
    )


def gates_back_kernel(
    seqs, me_ref, groups_ref, z_ref, c_ref, prior_ref, ds_ref, all_ref, back_ref, ids_ref,
    back_ids_ref, s_ref, bias_ref, du_ref, dc_ref, carried_ref, acc_ref,
):
    i = pl.program_id(0)
    rows = 2 * seqs
    chunks = z_ref.shape[0]
    span = z_ref.shape[1] // rows
    half = chunks * LANES

    @pl.when(i == 0)
    def _():
        parts = back_ref[...].astype(F32)
        summed = parts[:, :RIDE] + parts[:, RIDE : 2 * RIDE] + parts[:, 2 * RIDE :]
        totals = summed[:, : chunks * rows].reshape(-1, chunks, rows, LANES)
        entry = entry_state(me_ref[0], totals, all_ref[:, 0], rows, seqs, False)
        for j in range(chunks):
            carried_ref[j] = entry[j]
        acc_ref[...] = jnp.zeros_like(acc_ref)

    def one(lap, carried):
        place = pl.ds(pl.multiple_of((span - 1 - lap) * rows, rows), rows)
        result = []
        for j in range(chunks):
            update = z_ref[j, place, :]
            candidate = c_ref[j, place, :]
            total = ds_ref[j, place, :] + carried[j]
            decay = 1.0 - update
            gated = total * update
            du_ref[j, place, :] = gated * decay * (candidate - prior_ref[j, place, :])
            dc_ref[j, place, :] = gated * (1.0 - candidate * candidate)
            result.append(decay * total)
        return tuple(result)

    carried = lax.fori_loop(0, span, one, tuple(carried_ref[j] for j in range(chunks)), unroll=8)
    for j in range(chunks):
        carried_ref[j] = carried[j]
    vocabulary = lax.broadcasted_iota(jnp.int32, (NCHAR, span), 0)
    for direction in range(2):
        source = ids_ref if direction == 0 else back_ids_ref
        for s in range(seqs):
            place = pl.ds(s + direction * seqs, span, stride=rows)
            gradient = jnp.concatenate(
                [part[j, place, :] for part in (du_ref, dc_ref) for j in range(chunks)], axis=1
            ).astype(BF16)
            onehot = jnp.where(source[s] == vocabulary, 1.0, 0.0).astype(BF16)
            acc_ref[groups_ref[s], :, direction * 2 * half : (direction + 1) * 2 * half] += dot(
                onehot, gradient, 1, 0
            )

    @pl.when(i == pl.num_programs(0) - 1)
    def _():
        total = jnp.zeros((1, 4 * half), F32)
        for g in range(acc_ref.shape[0]):
            total += column_sum(acc_ref[g])
            s_ref[g] = acc_ref[g].astype(BF16)
        bias_ref[...] = total


def gates_back_call(me, groups, z, c, prior, ds, gathered, gathered_back, ids, n_groups, parts):
    chunks, length, _ = z.shape
    seqs, steps = ids.shape
    span = length // parts
    width = 2 * chunks * LANES
    stream = pl.BlockSpec((chunks, span, LANES), lambda i, *_: (0, parts - 1 - i, 0))
    lanes = pl.BlockSpec((seqs, 1, steps // parts), lambda i, *_: (0, 0, parts - 1 - i))
    return launch(
        functools.partial(gates_back_kernel, seqs),
        (parts,),
        [me, groups],
        [z, c, prior, ds, gathered, gathered_back, ids[:, None, :], ids[:, None, ::-1]],
        [stream] * 4 + [whole(gathered.shape), pl.BlockSpec((gathered_back.shape[0], 3 * RIDE, LANES), lambda i, *_: (0, gathered_back.shape[1] // (3 * RIDE) - 1, 0)), lanes, lanes],
        [whole((n_groups, NCHAR, 2 * width)), whole((1, 2 * width))],
        [shape((n_groups, NCHAR, 2 * width), BF16), shape((1, 2 * width), F32)],
        [ pltpu.VMEM((chunks, span, LANES), F32), pltpu.VMEM((chunks, span, LANES), F32), pltpu.VMEM((chunks, 2 * seqs, LANES), F32), pltpu.VMEM((n_groups, NCHAR, 2 * width), F32), ],
        cost(4 * seqs * steps * NCHAR * width, 16 * chunks * length * LANES),
        "gates_back",
    )


def shifted(values, toks, low, high):
    total = values.shape[0]
    row = lax.broadcasted_iota(jnp.int32, (total, 1), 0)
    before = pltpu.roll(values, 1, 0)
    after = pltpu.roll(values, total - 1, 0)
    for s in range(total // toks):
        before = jnp.where(row == s * toks, low[s], before)
        after = jnp.where(row == (s + 1) * toks - 1, high[s], after)
    return before.astype(BF16), after.astype(BF16)


def conv_kernel(
    toks, f_ref, p_ref, normal_ref, proj_ref, norms_ref, low_ref, high_ref, w_ref, tok_g_ref,
    char_g_ref, tok_ref, char_ref, d_tok_ref, d_char_ref, dm_ref, sums_ref, begin_ref, end_ref,
    acc_ref, x_ref,
):
    half, k = pl.program_id(0), pl.program_id(1)
    width = f_ref.shape[1]

    @pl.when((half == 0) & (k == 0))
    def _():
        for part, source in enumerate((f_ref, p_ref)):
            columns = slice(part * width, (part + 1) * width)
            before, after = shifted(
                source[...].astype(F32),
                toks,
                low_ref[:, :, columns].astype(F32),
                high_ref[:, :, columns].astype(F32),
            )
            x_ref[0, :, columns] = before
            x_ref[1, :, columns] = source[...]
            x_ref[2, :, columns] = after

    product = dot(x_ref[k], flat_block(w_ref), 1, 0)

    @pl.when(k == 0)
    def _():
        acc_ref[...] = product

    @pl.when(k > 0)
    def _():
        acc_ref[...] += product

    def finish(which, base, grad_ref, out_ref, d_ref):
        normal, rstd = norm_forward(base + acc_ref[...])
        gain = norms_ref[2 + which : 3 + which]
        out_ref[...] = normal * gain + norms_ref[6 + which : 7 + which]
        gradient = grad_ref[...].astype(F32)
        sums_ref[0, 0:1, :] = column_sum(gradient * normal)
        sums_ref[0, 1:2, :] = column_sum(gradient)
        d_sum = norm_backward(normal, rstd, gain, gradient)
        d_ref[...] = d_sum
        low_sum = d_sum.astype(BF16)
        dm_ref[...] = low_sum
        for s in range(begin_ref.shape[0]):
            begin_ref[s] = low_sum[s * toks : s * toks + 1]
            end_ref[s] = low_sum[(s + 1) * toks - 1 : (s + 1) * toks]

    @pl.when((half == 0) & (k == 2))
    def _():
        finish(
            0, normal_ref[...] * norms_ref[1:2] + norms_ref[5:6], tok_g_ref, tok_ref, d_tok_ref
        )

    @pl.when((half == 1) & (k == 2))
    def _():
        finish(1, proj_ref[...], char_g_ref, char_ref, d_char_ref)


def conv_call(f_low, proj_low, normal1, proj, norms, low, high, packed, tok_grad, char_grad, seqs, carry):
    total, width = f_low.shape
    count = packed.shape[0]
    blk = 2 * width // count
    rows = (total, width)
    return launch(
        functools.partial(conv_kernel, total // seqs),
        (2, 3),
        [],
        [f_low, proj_low, normal1, proj, norms, low, high, packed, tok_grad, char_grad],
        [ whole(rows), whole(rows), whole(rows), whole(rows), whole(norms.shape), whole(low.shape), whole(high.shape), pl.BlockSpec((count, blk, width), lambda h, k: (0, 2 * k + h, 0)), whole(rows), whole(rows), ],
        [ whole(rows), whole(rows), whole(rows), whole(rows), pl.BlockSpec(rows, lambda h, k: (0, h)), pl.BlockSpec((1, 2, width), lambda h, k: (h, 0, 0)), pl.BlockSpec((seqs, 1, width), lambda h, k: (0, 0, h)), pl.BlockSpec((seqs, 1, width), lambda h, k: (0, 0, h)), ],
        [ stored(rows, F32), stored(rows, F32), shape(rows, F32), shape(rows, F32), shape((total, 2 * width), BF16), shape((2, 2, width), F32), shape((seqs, 1, 2 * width), BF16), shape((seqs, 1, 2 * width), BF16), ],
        [pltpu.VMEM(rows, F32), pltpu.VMEM((3, total, 2 * width), BF16)],
        cost(24 * total * width * width, 24 * width * width + 40 * total * width),
        "conv",
        carry,
    )


def place_blocks(part_ref, order_ref, send_ref, keep_ref, blk, row=0):
    count = part_ref.shape[0] // blk
    for pos in range(count):
        start = pl.multiple_of(order_ref[pos] * blk, 16)
        piece = part_ref[pl.ds(start, blk), :].astype(BF16)
        if pos < count // 2:
            keep_ref[pos, row : row + blk, :] = piece
        else:
            send_ref[pos - count // 2, row : row + blk, :] = piece


def conv_weight_kernel(
    toks, order_ref, f_ref, p_ref, other_f_ref, other_p_ref, dm_ref, other_dm_ref, low_ref,
    high_ref, begin_ref, end_ref, far_low_ref, far_high_ref, keep_a_ref, sent_a_ref, keep_b_ref,
    sent_b_ref, turned_ref, whole_ref, part_ref,
):
    k, half = pl.program_id(0), pl.program_id(1)
    total, width = f_ref.shape
    pieces = 2 * keep_a_ref.shape[0]
    blk = keep_a_ref.shape[1]

    @pl.when((k == 0) & (half == 0))
    def _():
        odd = (order_ref[0] & 1) == 1
        edges = (
            (low_ref[...], high_ref[...]),
            (
                jnp.where(odd, far_low_ref[...], end_ref[...]),
                jnp.where(odd, begin_ref[...], far_high_ref[...]),
            ),
        )
        pairs = ((f_ref, p_ref), (other_f_ref, other_p_ref))
        for core, (pair, (low, high)) in enumerate(zip(pairs, edges)):
            for part, source in enumerate(pair):
                columns = slice(part * width, (part + 1) * width)
                middle = source[...]
                before, after = shifted(
                    middle.astype(F32),
                    toks,
                    low[:, :, columns].astype(F32),
                    high[:, :, columns].astype(F32),
                )
                for at, value in enumerate((before, middle, after)):
                    whole_ref[at, columns, :] = value.T
            for pos in range(pieces):
                start = pl.multiple_of(order_ref[pos] * blk, 16)
                for at in range(3):
                    turned_ref[
                        at, pos * blk : (pos + 1) * blk, core * total : (core + 1) * total
                    ] = whole_ref[at, pl.ds(start, blk), :]

    turned = turned_ref[k]
    part_ref[...] = dot(turned[:, :total], dm_ref[...], 1, 0) + dot(
        turned[:, total:], other_dm_ref[...], 1, 0
    )

    def put(keep_ref, sent_ref, kept, sent):
        for index, (one, other) in enumerate(zip(kept, sent)):
            keep_ref[index] = part_ref[one * blk : (one + 1) * blk, :].astype(BF16)
            sent_ref[index] = part_ref[other * blk : (other + 1) * blk, :].astype(BF16)

    at = 2 * k + half

    @pl.when(at < 3)
    def _():
        put(keep_a_ref, sent_a_ref, range(pieces // 2), range(pieces // 2, pieces))

    @pl.when(at >= 3)
    def _():
        put(keep_b_ref, sent_b_ref, range(0, pieces, 2), range(1, pieces, 2))


def conv_weight_call(order, own, other, dm, other_dm, edges, count):
    total, width = own[0].shape
    toks = total // edges[0].shape[0]
    blk = 2 * width // count
    out = (count // 4, 3 * blk, width)
    first = pl.BlockSpec((count // 4, blk, width), lambda k, h, *_: (0, jnp.minimum(2 * k + h, 2), 0))
    second = pl.BlockSpec(
        (count // 4, blk, width), lambda k, h, *_: (0, jnp.maximum(2 * k + h - 3, 0), 0)
    )
    columns = pl.BlockSpec((total, width), lambda k, h, *_: (0, h))
    plain = [*own, *other]
    keep_a, sent_a, keep_b, sent_b = launch(
        functools.partial(conv_weight_kernel, toks),
        (3, 2),
        [order],
        [*plain, dm, other_dm, *edges],
        [*[whole(v.shape) for v in plain], columns, columns, *[whole(v.shape) for v in edges]],
        [first, first, second, second],
        [stored(out, BF16)] * 4,
        [
            pltpu.VMEM((3, width, 2 * total), BF16),
            pltpu.VMEM((3, 2 * width, total), BF16),
            pltpu.VMEM((width, width), F32),
        ],
        cost(24 * total * width * width, 12 * width * width),
        "conv_weight",
    )
    return [[keep_a, sent_a], [keep_b, sent_b]]


def conv_back_kernel(
    toks, dm_ref, low_ref, high_ref, w_ref, d_tok_ref, d_char_ref, normal_ref, rstd_ref,
    norms_ref, d_proj_ref, d_ffn_ref, sums_ref, shift_ref, acc_ref,
):
    k, half = pl.program_id(0), pl.program_id(1)
    width = d_tok_ref.shape[1]

    @pl.when((half == 0) & (k == 0))
    def _():
        for part in range(2):
            columns = slice(part * width, (part + 1) * width)
            source = dm_ref[:, columns]
            before, after = shifted(
                source.astype(F32),
                toks,
                low_ref[:, :, columns].astype(F32),
                high_ref[:, :, columns].astype(F32),
            )
            shift_ref[part] = after
            shift_ref[2 + part] = source
            shift_ref[4 + part] = before

    product = dot(shift_ref[2 * k + half], flat_block(w_ref), 1, 1)

    @pl.when((k == 0) & (half == 0))
    def _():
        acc_ref[...] = product

    @pl.when((k > 0) | (half > 0))
    def _():
        acc_ref[...] += product

    @pl.when((k == 2) & (half == 1))
    def _():
        d_proj_ref[...] = (d_char_ref[...] + acc_ref[:, width:]).astype(BF16)
        gradient = d_tok_ref[...] + acc_ref[:, :width]
        normal = normal_ref[...]
        sums_ref[0:1, :] = column_sum(gradient * normal)
        sums_ref[1:2, :] = column_sum(gradient)
        d_ffn_ref[...] = norm_backward(normal, rstd_ref[...], norms_ref[1:2], gradient)


def conv_back_call(d_merged, low, high, packed, d_tok, d_char, normal1, rstd1, norms, seqs):
    total, width = d_tok.shape
    count = packed.shape[0]
    blk = 2 * width // count
    rows = (total, width)
    return launch(
        functools.partial(conv_back_kernel, total // seqs),
        (3, 2),
        [],
        [d_merged, low, high, packed, d_tok, d_char, normal1, rstd1, norms],
        [ whole(d_merged.shape), whole(low.shape), whole(high.shape), pl.BlockSpec((count, blk, width), lambda k, h: (0, 2 * k + h, 0)), whole(rows), whole(rows), whole(rows), whole(rstd1.shape), whole(norms.shape), ],
        [whole(rows), whole(rows), whole((2, width))],
        [shape(rows, BF16), shape(rows, F32), shape((2, width), F32)],
        [ pltpu.VMEM((6, total, width), BF16), pltpu.VMEM((total, 2 * width), F32), ],
        cost(24 * total * width * width, 24 * width * width + 20 * total * width),
        "conv_back",
    )


def rest_kernel(
    order_ref, table_ref, s_ref, w0_ref, w1_ref, send_ref, keep_ref, part_ref,
):
    count, blk, width = w0_ref.shape
    rows = part_ref.shape[0]
    turned = flat_block(table_ref).T
    sums = s_ref[...].reshape(rows, 2 * width)
    for part in range(2):
        part_ref[0:width, :] = dot(turned, sums[:, part * width : (part + 1) * width], 1, 0)
        place_blocks(part_ref.at[0:width], order_ref, send_ref, keep_ref, blk, part * blk)
    part_ref[...] = dot(sums[:, :width], flat_block(w0_ref), 1, 1) + dot(
        sums[:, width:], flat_block(w1_ref), 1, 1
    )
    place_blocks(part_ref, order_ref, send_ref, keep_ref, rows // count, 2 * blk)


def rest_call(order, packed, at_table, at_gru, sums, height):
    count, _, width = packed.shape
    blk = width // count
    rows = sums.shape[0] * sums.shape[1]
    table_rows = rows // count
    out = (count // 2, height, width)
    return launch(
        rest_kernel,
        (1,),
        [order],
        [packed, sums, packed, packed],
        [
            pl.BlockSpec((count, table_rows, width), lambda i, *_: (0, at_table, 0)),
            whole(sums.shape),
            pl.BlockSpec((count, blk, width), lambda i, *_: (0, at_gru, 0)),
            pl.BlockSpec((count, blk, width), lambda i, *_: (0, at_gru + 1, 0)),
        ],
        [whole(out), whole(out)],
        [stored(out, BF16), stored(out, BF16)],
        [pltpu.VMEM((rows, width), F32)],
        cost(8 * rows * width * width, 20 * width * width),
        "rest",
    )


def qkv_back_kernel(
    seqs, order_ref, d_ref, x_ref, w_ref, d_attn_ref,
    sums0_ref, sums1_ref, sums23_ref, bias_ref, bias_up_ref, out_ref, send_ref, keep_ref, xt_ref,
    dt_ref, part_ref, small_ref,
):
    j = pl.program_id(0)
    per = d_ref.shape[1]
    head, toks = d_ref.shape[3:]
    pieces, _, width = send_ref.shape
    blk = width // (2 * pieces)
    half = width // 2

    def put(row):
        for pos in range(2 * pieces):
            start = pl.multiple_of(order_ref[pos] * blk, 16)
            piece = part_ref[pl.ds(start, blk), :].astype(BF16)
            if pos < pieces:
                keep_ref[pos, row, :] = piece
            else:
                send_ref[pos - pieces, row, :] = piece

    @pl.when(j == 0)
    def _():
        xt_ref[...] = x_ref[...].T
        out_ref[...] = d_attn_ref[...]
        small_ref[...] = jnp.zeros_like(small_ref)
        for row, ref in enumerate((sums0_ref, sums1_ref)):
            small_ref[row : row + 1] = ref[0:1]
            small_ref[4 + row : 5 + row] = ref[1:2]
        for which in range(2):
            small_ref[2 + which : 3 + which] = sums23_ref[which, 0:1]
            small_ref[6 + which : 7 + which] = sums23_ref[which, 1:2]
        for part in range(2):
            own = slice(part * half, (part + 1) * half)
            small_ref[8:9, own] = bias_ref[:, part * width : part * width + half]
            small_ref[9:10, own] = bias_ref[:, part * width + half : (part + 1) * width]
        for part in range(bias_up_ref.shape[1] // width):
            small_ref[10 + part : 11 + part] = bias_up_ref[:, part * width : (part + 1) * width]
        small = small_ref[...].astype(BF16)
        for pos in range(pieces):
            keep_ref[pos, 3 * blk : 3 * blk + SMALL_ROWS, :] = small
            send_ref[pos, 3 * blk : 3 * blk + SMALL_ROWS, :] = small

    for s in range(seqs):
        for h in range(HEADS):
            pair = s * HEADS + h
            dt_ref[h * head : (h + 1) * head, s * toks : (s + 1) * toks] = d_ref[
                pair // per, pair % per, 0
            ]
    gradient = dt_ref[...].T
    part_ref[...] = dot(xt_ref[...], gradient, 1, 0)
    put(pl.ds(pl.multiple_of(j * blk, 16), blk))
    out_ref[...] += dot(gradient, flat_block(w_ref), 1, 1)


def qkv_back_call(
    order, d_qkv, rows, packed, base, d_attn, small, seqs, height
):
    count, per, _, head, toks = d_qkv.shape
    total, width = rows.shape
    blk = width // count
    out = (count // 2, height, width)
    rest = [d_attn, *small]
    return launch(
        functools.partial(qkv_back_kernel, seqs),
        (3,),
        [order],
        [d_qkv, rows, packed, *rest],
        [
            pl.BlockSpec((count, per, 1, head, toks), lambda j, *_: (0, 0, j, 0, 0)),
            whole(rows.shape),
            pl.BlockSpec((count, blk, width), lambda j, *_: (0, base + j, 0)),
            *[whole(v.shape) for v in rest],
        ],
        [whole((total, width)), whole(out), whole(out)],
        [stored((total, width), F32), stored(out, BF16), stored(out, BF16)],
        [
            pltpu.VMEM((width, total), BF16),
            pltpu.VMEM((width, total), BF16),
            pltpu.VMEM((width, width), F32),
            pltpu.VMEM((SMALL_ROWS, width), F32),
        ],
        cost(16 * total * width * width, 20 * width * width + 16 * total * width),
        "qkv_back",
    )


def pack_kernel(layout, *refs):
    ins, out_ref = refs[:-1], refs[-1]
    at = 0
    out_ref[...] = jnp.zeros_like(out_ref)
    width = out_ref.shape[1]
    for ref, row in zip(ins, layout):
        height, columns = ref.shape
        if columns < width:
            out_ref[row : row + height, :columns] = ref[...]
        else:
            for block in range(columns // width):
                out_ref[row + block * height : row + (block + 1) * height, :] = ref[
                    :, block * width : (block + 1) * width
                ]


def pack(arrays, layout, rows, width):
    return launch(
        functools.partial(pack_kernel, layout),
        (1,),
        [],
        arrays,
        [whole(v.shape) for v in arrays],
        whole((rows, width)),
        shape((rows, width), BF16),
        [],
        cost(0, 4 * rows * width),
        "pack",
    )


def swap(value, axis, bit):
    size = lax.axis_size(axis)
    return lax.ppermute(value, axis, [(i, i ^ (1 << bit)) for i in range(size)])


def add_low(kept, arrived):
    return (kept.astype(F32) + arrived.astype(F32)).astype(BF16)


def fold_kernel(keep_top, keep_bottom, came_top, came_bottom, ka_ref, sa_ref, kb_ref, sb_ref):
    half = ka_ref.shape[0]
    for index in range(half):
        ka_ref[index] = add_low(keep_top[index], came_top[index])
        sa_ref[index] = add_low(keep_top[half + index], came_top[half + index])
        kb_ref[index] = add_low(keep_bottom[2 * index], came_bottom[2 * index])
        sb_ref[index] = add_low(keep_bottom[2 * index + 1], came_bottom[2 * index + 1])


def tiles(rows):
    return 3 if rows % 48 == 0 else 1


def fold_pieces_kernel(keep_top, keep_bottom, *refs):
    pieces = keep_top.shape[0]
    top, bottom, outs = refs[:pieces], refs[pieces : 2 * pieces], refs[2 * pieces :]
    ka_ref, sa_ref, kb_ref, sb_ref = outs
    half = pieces // 2
    for index in range(half):
        ka_ref[index] = add_low(keep_top[index], top[index][...])
        sa_ref[index] = add_low(keep_top[half + index], top[half + index][...])
        kb_ref[index] = add_low(keep_bottom[2 * index], bottom[2 * index][...])
        sb_ref[index] = add_low(keep_bottom[2 * index + 1], bottom[2 * index + 1][...])


def fold(keep, arrived):
    pieces, rows, width = keep.shape
    steps = tiles(rows // 2)
    tile = rows // 2 // steps
    top = pl.BlockSpec((pieces, tile, width), lambda i: (0, i, 0))
    bottom = pl.BlockSpec((pieces, tile, width), lambda i: (0, steps + i, 0))
    one_top = pl.BlockSpec((tile, width), lambda i: (i, 0))
    one_bottom = pl.BlockSpec((tile, width), lambda i: (steps + i, 0))
    ka, sa, kb, sb = launch(
        fold_pieces_kernel,
        (steps,),
        [],
        [keep, keep, *arrived, *arrived],
        [top, bottom] + [one_top] * pieces + [one_bottom] * pieces,
        [pl.BlockSpec((pieces // 2, tile, width), lambda i: (0, i, 0))] * 4,
        [stored((pieces // 2, rows // 2, width), BF16)] * 4,
        [],
        cost(pieces * rows * width, 6 * pieces * rows * width),
        "fold",
    )
    return [[ka, sa], [kb, sb]]


def send_links(state, step):
    bits = lax.axis_size("seq").bit_length() - 1
    return [
        [kept, swap(sent, "seq", bit)] for (kept, sent), bit in zip(state, (step, bits - step))
    ]


def split(state, carry=()):
    pieces, rows, width = state[0][0].shape
    steps = tiles(rows)
    spec = pl.BlockSpec((pieces, rows // steps, width), lambda i: (0, i, 0))
    out = pl.BlockSpec((pieces // 2, rows // steps, width), lambda i: (0, i, 0))
    ka, sa, kb, sb, *carried = launch(
        fold_kernel,
        (steps,),
        [],
        [state[0][0], state[1][0], state[0][1], state[1][1]],
        [spec] * 4,
        [out] * 4,
        [stored((pieces // 2, rows, width), BF16)] * 4,
        [],
        cost(pieces * rows * width, 12 * pieces * rows * width),
        "split",
        carry,
    )
    return [[ka, sa], [kb, sb]], carried


def cross_kernel(place_ref, ka_ref, kb_ref, ca_ref, cb_ref, kept_ref, sent_ref):
    high = (place_ref[0] & 1) == 1
    first = add_low(ka_ref[0], ca_ref[0])
    second = add_low(kb_ref[0], cb_ref[0])
    kept_ref[...] = jnp.where(high, second, first)
    sent_ref[...] = jnp.where(high, first, second)


def cross(place, state, carry=()):
    _, rows, width = state[0][0].shape
    steps = tiles(rows)
    spec = pl.BlockSpec((1, rows // steps, width), lambda i, *_: (0, i, 0))
    return launch(
        cross_kernel,
        (steps,),
        [place],
        [state[0][0], state[1][0], state[0][1], state[1][1]],
        [spec] * 4,
        [pl.BlockSpec((rows // steps, width), lambda i, *_: (i, 0))] * 2,
        [stored((rows, width), BF16)] * 2,
        [],
        cost(rows * width, 12 * rows * width),
        "cross",
        carry,
    )


def halve_kernel(bit, place_ref, kept_ref, came_ref, next_ref, sent_ref):
    high = ((place_ref[0] >> bit) & 1) == 1
    rows = next_ref.shape[0]
    first = add_low(kept_ref[:rows], came_ref[:rows])
    second = add_low(kept_ref[rows:], came_ref[rows:])
    next_ref[...] = jnp.where(high, second, first)
    sent_ref[...] = jnp.where(high, first, second)


def halve(place, bit, kept, came, carry):
    rows, width = kept.shape
    return launch(
        functools.partial(halve_kernel, bit),
        (1,),
        [place],
        [kept, came],
        [whole(kept.shape)] * 2,
        [whole((rows // 2, width))] * 2,
        [stored((rows // 2, width), BF16)] * 2,
        [],
        cost(rows * width, 6 * rows * width),
        "halve",
        carry,
    )


def add_kernel(kept_ref, came_ref, out_ref):
    out_ref[...] = add_low(kept_ref[...], came_ref[...])


def add(kept, came, carry):
    return launch(
        add_kernel,
        (1,),
        [],
        [kept, came],
        [whole(kept.shape)] * 2,
        whole(kept.shape),
        stored(kept.shape, BF16),
        [],
        cost(kept.size, 6 * kept.size),
        "add",
        carry,
    )


def assemble_kernel(bit, place_ref, held_ref, came_ref, out_ref):
    high = ((place_ref[0] >> bit) & 1) == 1
    rows = held_ref.shape[0]
    held, came = held_ref[...], came_ref[...]
    out_ref[:rows] = jnp.where(high, came, held)
    out_ref[rows:] = jnp.where(high, held, came)


def assemble(place, bit, held, came):
    rows, width = held.shape
    return launch(
        functools.partial(assemble_kernel, bit),
        (1,),
        [place],
        [held, came],
        [whole(held.shape)] * 2,
        whole((2 * rows, width)),
        stored((2 * rows, width), BF16),
        [],
        cost(rows * width, 8 * rows * width),
        "assemble",
    )


def finish_kernel(layout, place_ref, held_ref, came_ref, *out_refs):
    high = (place_ref[0] & 1) == 1
    rows = held_ref.shape[0]
    for begin, size, out, index in layout:
        part = slice(begin % rows, begin % rows + size)
        held, came = held_ref[part].astype(F32), came_ref[part].astype(F32)
        out_refs[out][index] = jnp.where(high == (begin < rows), came, held)


def cut(layout, rows):
    for begin, size, out, index in layout:
        edges = [begin, begin + size]
        if begin < rows < begin + size:
            edges.insert(1, rows)
        for low, high in zip(edges, edges[1:]):
            yield low, high - low, out, index[:-2] + (slice(low - begin, high - begin), index[-1])


def finish(place, held, came, layout, outs):
    layout = list(cut(layout, held.shape[0]))
    return launch(
        functools.partial(finish_kernel, layout),
        (1,),
        [place],
        [held, came],
        [whole(held.shape)] * 2,
        [whole(dims) for dims in outs],
        [stored(dims, F32) for dims in outs],
        [],
        cost(held.size, 16 * held.size),
        "finish",
    )


def across_halves(place, kept, sent, layout, outs):
    bits = lax.axis_size("batch").bit_length() - 1
    came = swap(sent, "batch", 0)
    carry = yield
    for bit in range(1, bits):
        kept, sent, *carry = halve(place, bit, kept, came, carry or ())
        came = swap(sent, "batch", bit)
        carry = yield carry
    held = add(kept, came, carry or ())
    held, carry = (held[0], held[1:]) if carry else (held, ())
    for bit in reversed(range(bits)):
        came = swap(held, "batch", bit)
        yield carry
        if bit:
            held = assemble(place, bit, held, came)
    yield finish(place, held, came, layout, outs)


def deal_kernel(place_ref, ka_ref, kb_ref, ca_ref, cb_ref, *refs):
    outs, sum_ref = refs[:-1], refs[-1]
    rows, part = ka_ref.shape[1], outs[0].shape[0]
    sum_ref[:rows] = add_low(ka_ref[0], ca_ref[0])
    sum_ref[rows:] = add_low(kb_ref[0], cb_ref[0])
    for mask, out_ref in enumerate(outs):
        start = pl.multiple_of((place_ref[0] ^ mask) * part, 16)
        out_ref[...] = sum_ref[pl.ds(start, part), :]


def total_kernel(*refs):
    total = refs[0][...].astype(F32)
    for ref in refs[1:-1]:
        total += ref[...].astype(F32)
    refs[-1][...] = total.astype(BF16)


def spread_kernel(layout, small_at, parts, place_ref, me_ref, *refs):
    ins, outs, all_ref = refs[:parts], refs[parts:-1], refs[-1]
    rows = ins[0].shape[0]
    for mask, ref in enumerate(ins):
        start = pl.multiple_of((place_ref[0] ^ mask) * rows, 16)
        all_ref[pl.ds(start, rows), :] = ref[...]
    for begin, size, out, index in layout:
        outs[out][index] = all_ref[begin : begin + size].astype(F32)
    blk, share = outs[-5].shape[1], outs[-1].shape[1]
    small = all_ref[small_at : small_at + SMALL_ROWS].astype(F32)
    width = small.shape[1]
    me = me_ref[0]
    mine = pltpu.roll(small, lax.rem(width - me * blk, width), 1)[:, :blk]
    outs[-5][...] = mine[0:4]
    outs[-4][...] = mine[4:8]
    outs[-3][...] = mine[8:9]
    outs[-2][...] = mine[9:10]
    spot = me * share
    turned = pltpu.roll(small, lax.rem(width - lax.rem(spot, width), width), 1)[:, :share]
    row = lax.broadcasted_iota(jnp.int32, turned.shape, 0)
    outs[-1][...] = column_sum(jnp.where(row == 10 + lax.div(spot, width), turned, 0.0))


def across_direct(place, me, state, layout, small_at, outs):
    parts = lax.axis_size("batch")
    _, rows, width = state[0][0].shape
    part = (2 * rows // parts, width)
    ends = [(mask, [(i, i ^ mask) for i in range(parts)]) for mask in range(1, parts)]
    pieces = launch(
        deal_kernel,
        (1,),
        [place],
        [state[0][0], state[1][0], state[0][1], state[1][1]],
        [whole(state[0][0].shape)] * 4,
        [whole(part)] * parts,
        [stored(part, BF16)] * parts,
        [pltpu.VMEM((2 * rows, width), BF16)],
        cost(rows * width, 12 * rows * width),
        "deal",
    )
    came = [lax.ppermute(pieces[mask], "batch", pairs) for mask, pairs in ends]
    yield
    held = launch(
        total_kernel,
        (1,),
        [],
        [pieces[0], *came],
        [whole(part)] * parts,
        whole(part),
        stored(part, BF16),
        [],
        cost(rows * width, 5 * rows * width),
        "total",
    )
    came = [lax.ppermute(held, "batch", pairs) for _, pairs in ends]
    yield
    yield launch(
        functools.partial(spread_kernel, layout, small_at, parts),
        (1,),
        [place, me],
        [held, *came],
        [whole(part)] * parts,
        [whole(dims) for dims in outs],
        [stored(dims, F32) for dims in outs],
        [pltpu.VMEM((2 * rows, width), BF16)],
        cost(rows * width, 12 * rows * width),
        "spread",
    )


def last(steps):
    result = None
    for result in steps:
        pass
    return result if isinstance(result, (list, tuple)) else [result]


def neighbours(first, last):
    count = lax.axis_size("seq")
    up = [(i, i + 1) for i in range(count - 1)]
    down = [(target, source) for source, target in up]
    return lax.ppermute(last, "seq", up), lax.ppermute(first, "seq", down)


def local(
    hidden, char_ids, group_ids, word_lengths, qkv_weight, out_weight, up_weight, ffn_bias,
    down_weight, gru_weight, gate_bias, candidate_bias, char_weight, conv_weight, char_table,
    norm_gain, norm_shift, tok_grad, char_grad,
):
    count = lax.axis_size("seq")
    bits = count.bit_length() - 1
    me = lax.axis_index("seq").astype(jnp.int32)
    seqs, toks, width = hidden.shape
    total = seqs * toks
    half = width // 2
    blk = width // count
    share = ffn_bias.shape[0]
    table_rows = char_table.shape[0]
    chars = char_ids.shape[1]
    reverse = [int(format(i, f"0{bits}b")[::-1], 2) for i in range(count)]
    order = jnp.asarray(reverse, jnp.int32) ^ me
    slot = sum(
        (((jnp.arange(count, dtype=jnp.int32) ^ me) >> b) & 1) << (bits - 1 - b) for b in range(bits)
    )
    me_one = me.reshape(1)

    place = lax.axis_index("batch").astype(jnp.int32).reshape(1)
    LATEST.clear()
    PLACED[:] = [True]
    NEAR.clear()

    table_at = share
    small_at = table_at + table_rows
    block_at = small_at + 16
    block_at += -block_at % blk
    pack_rows = block_at + 11 * blk
    small = jnp.concatenate(
        [norm_gain.T, norm_shift.T, gate_bias[None], candidate_bias[None]], 0
    )
    small = jnp.pad(small, ((0, 6), (0, width - blk)))
    small = small.at[10, :share].set(ffn_bias)
    arrays = [
        down_weight, char_table, small, gru_weight, qkv_weight, char_weight, out_weight, up_weight
    ]
    at_block = block_at // blk
    at_gru, at_qkv, at_char, at_out, at_up = (at_block + i for i in (0, 2, 5, 6, 7))
    layout = [0, table_at, small_at] + [i * blk for i in (at_gru, at_qkv, at_char, at_out, at_up)]
    at_table, at_down = table_at // table_rows, 0
    first = pack(arrays, layout, pack_rows, width)
    third = pack(
        [conv_weight[k] for k in range(3)], [k * 4 * blk for k in range(3)], 12 * blk, width
    )
    first = lax.all_gather(first, "seq", axis=0)
    third = lax.all_gather(third, "seq", axis=0)
    vectors = (
        first[:, small_at : small_at + 10, :blk].astype(F32).transpose(1, 0, 2).reshape(10, width)
    )
    bias_up = first[:, small_at + 10, :share].astype(F32).reshape(1, -1)
    norms = vectors

    rows = hidden.reshape(total, width)
    words = word_lengths.reshape(seqs, toks)
    ends = jnp.cumsum(words, axis=1)
    starts = ends - words
    lens = words.astype(F32)[..., None]

    qkv = qkv_call(rows, first, at_qkv, seqs, count)
    qkv = lax.all_to_all(qkv, "seq", 0, 0, tiled=True)
    z, c, block_totals = gates_call(group_ids, char_ids, first, at_gru, at_table, vectors)
    gathered = [block_totals] + [
        lax.ppermute(block_totals, "seq", [(i, i ^ mask) for i in range(count)])
        for mask in range(1, count)
    ]
    step = 512
    mixture, totals = attend_call(qkv, step)
    mixture = lax.all_to_all(mixture, "seq", 0, 0, tiled=True)
    gathered = collect(me_one, gathered)
    prior, pooled, proj, proj_low = states_call(
        me_one, z, c, gathered, starts[..., None], ends[..., None], lens, first, at_char, 2
    )
    mix_t, normal0, rstd0, normed, active, slope, normal1, rstd1, f_low = ffn_call(
        mixture, rows, first, at_out, at_up, at_down, bias_up, norms, seqs
    )

    def edges(left, right):
        joined = [v.reshape(seqs, toks, width) for v in (left, right)]
        return (
            jnp.concatenate([v[:, :1] for v in joined], -1),
            jnp.concatenate([v[:, -1:] for v in joined], -1),
        )

    begin, end = edges(f_low, proj_low)
    low, high = neighbours(begin, end)
    far_high = lax.ppermute(begin, "seq", [(i, i - 2) for i in range(2, count)])
    far_low = lax.ppermute(end, "seq", [(i, i + 2) for i in range(count - 2)])
    joined_edges = [low, high, begin, end, far_low, far_high]
    other = [swap(v, "seq", 0) for v in (f_low, proj_low)]
    tok_out, char_out, d_tok, d_char, d_merged, sums23, begin, end, *other = conv_call(
        f_low, proj_low, normal1, proj, norms, low, high, third,
        tok_grad.reshape(total, width), char_grad.reshape(total, width), seqs, other,
    )

    low, high = neighbours(begin, end)
    other_dm = swap(d_merged, "seq", 0)

    def onward(state, first_link, carry=()):
        for link in range(first_link + 1, bits):
            state, carry = split(state, carry)
            state = send_links(state, link)
        return state, carry

    def columns_of(begin, blocks, out):
        return [
            (begin + j * blk, blk, out, (slice(None), slice(j * width, (j + 1) * width)))
            for j in range(blocks)
        ]

    everything = (slice(None), slice(None))
    double = 2 * blk
    batch_bits = lax.axis_size("batch").bit_length() - 1
    unit = 8 * lax.axis_size("batch")
    height = max(2 * blk + table_rows, 3 * blk + SMALL_ROWS)
    height += -height % unit
    d_proj, d_ffn, sums1 = conv_back_call(
        d_merged, low, high, third, d_tok, d_char, normal1, rstd1, norms, seqs
    )
    conv_state = conv_weight_call(
        order, (f_low, proj_low), other, d_merged, other_dm, joined_edges, count
    )
    conv_state = send_links(conv_state, 1)
    ds, back_totals = states_back_call(
        d_proj, first, at_char, lens, starts[:, None, :], ends[:, None, :], z
    )
    send, keep, d_bias_up, d_attn, sums0, d_mix = ffn_back_call(
        slot, order, d_ffn, active, slope, normed, normal0, rstd0, norms, first, at_out, at_up,
        at_down, back_totals, mix_t, pooled, d_proj, seqs,
    )
    d_mix = lax.all_to_all(d_mix, "seq", 0, 0, tiled=True)
    ffn_came = [swap(piece, "seq", 0) for piece in send]
    conv_state, _ = onward(conv_state, 1)
    ffn_state = fold(keep, ffn_came)
    ffn_state = send_links(ffn_state, 1)
    d_qkv = attend_back_call(qkv, d_mix, totals, step)
    d_qkv = lax.all_to_all(d_qkv, "seq", 0, 0, tiled=True)
    conv_steps = across_halves(
        place, *cross(place, conv_state)[:2],
        [
            (r * double, double, 0, (r // 2, slice(None), slice(r % 2 * width, (r % 2 + 1) * width)))
            for r in range(6)
        ],
        [(3, double, 2 * width)],
    )
    next(conv_steps)
    sums, d_bias = gates_back_call(
        me_one, group_ids, z, c, prior, ds, gathered, d_mix, char_ids,
        count * table_rows // NCHAR, 2,
    )
    ffn_state, _ = onward(ffn_state, 1)
    for _ in range(1, batch_bits):
        next(conv_steps)
    rest_send, rest_keep = rest_call(order, first, at_table, at_gru, sums, height)
    hidden_grad, qkv_send, qkv_keep = qkv_back_call(
        order, d_qkv, rows, first, at_qkv, d_attn,
        [sums0, sums1, sums23, d_bias, d_bias_up], seqs, height,
    )
    PLACED.clear()
    ffn_steps = across_halves(
        place, *cross(place, ffn_state)[:2],
        [
            (0, share, 0, everything),
            *columns_of(share, 4, 1),
            (share + 4 * blk, blk, 2, everything),
            (share + 5 * blk, blk, 3, everything),
        ],
        [(share, width), (blk, 4 * width), (blk, width), (blk, width)],
    )
    next(ffn_steps)
    both = conv_steps.send([rest_send, qkv_send])
    rest_came, qkv_came = (swap(send, "seq", 0) for send in both)
    last_state, _ = split([[rest_keep, rest_came], [qkv_keep, qkv_came]])
    last_state = send_links(last_state, 1)
    for _ in range(1, batch_bits):
        next(ffn_steps)
    next(conv_steps)
    last_state, _ = onward(last_state, 1)
    (conv_grad,) = last(conv_steps)
    last_steps = across_direct(
        place, me_one, last_state,
        [
            *columns_of(0, 2, 0),
            (2 * blk, table_rows, 1, everything),
            *columns_of(height, 3, 2),
        ],
        height + 3 * blk,
        [
            (blk, 2 * width), (table_rows, width), (blk, 3 * width),
            (4, blk), (4, blk), (1, blk), (1, blk), (1, share),
        ],
    )
    next(last_steps)
    next(ffn_steps)
    next(ffn_steps)
    next(last_steps)
    down_grad, up_grad, out_grad, char_grad_w = last(ffn_steps)
    gru_grad, table_grad, qkv_grad, *small_grads = last(last_steps)
    d_gain, d_shift = (v.T for v in small_grads[:2])
    d_gate_b, d_cand_b, d_ffn_b = (v.reshape(-1) for v in small_grads[2:])
    shape_out = (seqs, toks, width)
    return (
        tok_out.reshape(shape_out),
        char_out.reshape(shape_out),
        hidden_grad.reshape(shape_out),
        qkv_grad,
        out_grad,
        up_grad,
        d_ffn_b,
        down_grad,
        gru_grad,
        d_gate_b,
        d_cand_b,
        char_grad_w,
        conv_grad,
        table_grad,
        d_gain,
        d_shift,
    )


def solution(mesh):
    rows, columns = P("seq", None), P("batch", "seq", None)
    return jax.shard_map(
        local,
        mesh=mesh,
        in_specs=(
            columns, P("batch", "seq"), P("batch"), columns, rows, rows, rows, P("seq"), rows,
            rows, P("seq"), P("seq"), rows, P(None, "seq", None), rows, rows, rows, columns,
            columns,
        ),
        out_specs=(
            columns, columns, columns, rows, rows, rows, P("seq"), rows, rows, P("seq"), P("seq"),
            rows, P(None, "seq", None), rows, rows, rows,
        ),
        check_vma=False,
    )
```

```python
import functools
import math

import jax
import jax.numpy as jnp
from jax import lax
from jax.experimental import pallas as pl
from jax.experimental.pallas import tpu as pltpu
from jax.sharding import PartitionSpec as P

HEADS = 12
NCHAR = 256
NORM_EPS = 1e-06
LANES = 128
SMALL_ROWS = 16
RIDE = 32
SCALE = 1000
F32 = jnp.float32
BF16 = jnp.bfloat16
VMEM_BYTES = 44 << 20
VMEM_MARGIN = 9 << 20


def dot(left, right, left_dim, right_dim):
    return lax.dot_general(
        left, right, (((left_dim,), (right_dim,)), ((), ())), preferred_element_type=F32
    )


def padded_bytes(dims, dtype):
    size = jnp.dtype(dtype).itemsize
    dims = (1, 1, *dims)
    rows = -(-dims[-2] * size // 32) * 32
    lanes = -(-dims[-1] // LANES) * LANES
    return math.prod(dims[:-2]) * rows * lanes


def params(grid_rank, blocks, scratch):
    need = sum(2 * padded_bytes(spec.block_shape, value.dtype) for spec, value in blocks)
    need += sum(padded_bytes(ref.shape, ref.dtype) for ref in scratch)
    return pltpu.CompilerParams(
        dimension_semantics=("arbitrary",) * grid_rank,
        vmem_limit_bytes=min(VMEM_BYTES, need + VMEM_MARGIN),
    )


def shape(dims, dtype):
    return jax.ShapeDtypeStruct(dims, dtype)


def stored(dims, dtype):
    return pltpu.HBM(dims, dtype) if PLACED else shape(dims, dtype)


def whole(dims):
    return pl.BlockSpec(dims, lambda *_: (0,) * len(dims))


def cost(flops, nbytes):
    return pl.CostEstimate(flops=int(flops) * SCALE, bytes_accessed=int(nbytes) * SCALE, transcendentals=0)


NEAR = []
LATEST = []
PLACED = []
TOKEN = jax.ShapeDtypeStruct((8, LANES), F32)


def launch(
    body, grid, prefetch, inputs, in_specs, out_specs, out_shape, scratch, price, name, carry=()
):
    deps = [pltpu.with_memory_space_constraint(v, pltpu.HBM) for v in LATEST]
    single = not isinstance(out_shape, (list, tuple))
    outs = [out_shape] if single else list(out_shape)
    specs = [out_specs] if single else list(out_specs)
    lead = len(prefetch) + len(inputs)
    extra = len(carry) + len(deps)
    anywhere = pl.BlockSpec(memory_space=pl.ANY)

    def kernel(*refs):
        own = refs[lead + extra :]
        body(*refs[:lead], *own[: len(outs)], *own[len(outs) + len(carry) + 1 :])

    inputs = [
        v
        if not PLACED or v.size < 1 << 16 or any(v is near for near in NEAR)
        else pltpu.with_memory_space_constraint(v, pltpu.HBM)
        for v in inputs
    ]
    results = pl.pallas_call(
        kernel,
        grid_spec=pltpu.PrefetchScalarGridSpec(
            num_scalar_prefetch=len(prefetch),
            grid=grid,
            in_specs=list(in_specs) + [anywhere] * extra,
            out_specs=specs + [anywhere] * (len(carry) + 1),
            scratch_shapes=scratch,
        ),
        out_shape=outs + [stored(v.shape, v.dtype) for v in (*carry, TOKEN)],
        input_output_aliases={lead + i: len(outs) + i for i in range(len(carry))},
        compiler_params=params(
            len(grid), [*zip(in_specs, inputs), *zip(specs, outs)], scratch
        ),
        cost_estimate=price,
        name=name,
    )(*prefetch, *inputs, *carry, *deps)
    NEAR.extend(v for v, out in zip(results, outs) if isinstance(out, jax.ShapeDtypeStruct))
    *results, LATEST[:] = *results[:-1], results[-1:]
    return results[0] if len(results) == 1 else results


def plan(body, grid, prefetch, inputs, in_specs, out_specs, out_shape, scratch, price, name):
    listed = isinstance(out_shape, (list, tuple))
    outs = (list(out_specs), list(out_shape)) if listed else ([out_specs], [out_shape])
    return body, grid, prefetch, inputs, in_specs, *outs, scratch, price, name


def together(plans, carry=()):
    bodies, grids, prefetch, inputs, in_specs, out_specs, outs, scratch, prices, names = zip(*plans)
    assert len(set(grids)) == 1
    groups = (prefetch, inputs, outs, scratch)

    def body(*refs):
        own = [[] for _ in plans]
        for group in groups:
            for refs_of, part in zip(own, group):
                refs_of.extend(refs[: len(part)])
                refs = refs[len(part) :]
        for one, refs_of in zip(bodies, own):
            one(*refs_of)

    def flat(parts):
        return [v for part in parts for v in part]

    price = pl.CostEstimate(
        flops=sum(v.flops for v in prices),
        bytes_accessed=sum(v.bytes_accessed for v in prices),
        transcendentals=0,
    )
    results = launch(
        body, grids[0], flat(prefetch), flat(inputs), flat(in_specs), flat(out_specs), flat(outs),
        flat(scratch), price, "_".join(names), carry,
    )
    results = list(results) if isinstance(results, (list, tuple)) else [results]
    found = []
    for part in outs:
        found.append(results[: len(part)])
        results = results[len(part) :]
    return found, results


class Steps:
    def __init__(self, plans):
        self.plans, self.result = plans, None
        self.plan = next(plans)

    def resume(self, values):
        try:
            self.plan = self.plans.send(values)
        except StopIteration as end:
            self.plan, self.result = None, end.value


def advance(*runs, carry=()):
    live = [run for run in runs if run.plan]
    found, carried = together([run.plan for run in live], carry)
    for run, values in zip(live, found):
        run.resume(values)
    return carried


def flat_block(ref):
    block = ref[...]
    return block.reshape(block.shape[0] * block.shape[1], block.shape[2])


def norm_forward(values):
    center = values - jnp.mean(values, -1, keepdims=True)
    rstd = lax.rsqrt(jnp.mean(center * center, -1, keepdims=True) + NORM_EPS)
    return center * rstd, rstd


def norm_backward(normal, rstd, gain, gradient):
    scaled = gradient * gain
    first = jnp.mean(scaled, -1, keepdims=True)
    second = jnp.mean(scaled * normal, -1, keepdims=True)
    return rstd * (scaled - first - normal * second)


def column_sum(values):
    return jnp.sum(values, 0, keepdims=True)


def gelu_parts(values):
    size = jnp.abs(values) * 0.7071067811865476
    bell = jnp.exp(-size * size)
    t = 1.0 / (1.0 + 0.3275911 * size)
    series = t * (
        0.254829592
        + t * (-0.284496736 + t * (1.421413741 + t * (-1.453152027 + t * 1.061405429)))
    )
    tail = 0.5 * series * bell
    phi_sum = jnp.where(values < 0, tail, 1.0 - tail)
    return values * phi_sum, phi_sum + values * (bell * 0.3989422804014327)


def qkv_kernel(seqs, toks, per, x_ref, w_ref, o_ref):
    acc = dot(x_ref[...], flat_block(w_ref), 1, 0)
    turned = acc.T.astype(BF16)
    width = turned.shape[0] // HEADS
    for s in range(seqs):
        for h in range(HEADS):
            pair = s * HEADS + h
            o_ref[pair // per, pair % per, 0] = turned[
                h * width : (h + 1) * width, s * toks : (s + 1) * toks
            ]


def qkv_call(rows, packed, base, seqs, count):
    total, width = rows.shape
    toks = total // seqs
    per = seqs * HEADS // count
    head = width // HEADS
    blk = width // count
    return launch(
        functools.partial(qkv_kernel, seqs, toks, per),
        (3,),
        [],
        [rows, packed],
        [ whole(rows.shape), pl.BlockSpec((count, blk, width), lambda j: (0, base + j, 0)), ],
        pl.BlockSpec((count, per, 1, head, toks), lambda j: (0, 0, j, 0, 0)),
        stored((count, per, 3, head, toks), BF16),
        [],
        cost(6 * total * width * width, 6 * width * width + 8 * total * width),
        "qkv",
    )


def spread(ref, index):
    return jnp.concatenate([ref[(i, *index)] for i in range(ref.shape[0])], axis=1)


def attend_kernel(step, scale, x_ref, o_ref, total_ref):
    queries = spread(x_ref, (0, 0)) * scale
    keys = spread(x_ref, (0, 1)).T
    values = spread(x_ref, (0, 2))
    toks = x_ref.shape[-1]
    for begin in range(0, queries.shape[1], step):
        scores = dot(keys, queries[:, begin : begin + step], 1, 0)
        highest = jnp.max(scores, 0, keepdims=True)
        expo = jnp.exp(scores - highest)
        totals = jnp.sum(expo, 0, keepdims=True)
        mixture = (dot(values, expo.astype(BF16), 1, 0) / totals).astype(BF16)
        total_ref[0, :, begin : begin + step] = highest + jnp.log(totals)
        for at in range(0, step, toks):
            o_ref[(begin + at) // toks, 0] = mixture[:, at : at + toks]


def attend_call(qkv, step):
    count, per, _, head, toks = qkv.shape
    length = count * toks
    scale = head**-0.5
    return launch(
        functools.partial(attend_kernel, step, scale),
        (per,),
        [],
        [qkv],
        [pl.BlockSpec((count, 1, 3, head, toks), lambda p: (0, p, 0, 0, 0))],
        [ pl.BlockSpec((count, 1, head, toks), lambda p: (0, p, 0, 0)), pl.BlockSpec((1, 1, length), lambda p: (p, 0, 0)), ],
        [stored((count, per, head, toks), BF16), shape((per, 1, length), F32)],
        [],
        cost(16 * per * length * length * head, 8 * per * length * head),
        "attend",
    )


def attend_back_kernel(step, scale, x_ref, g_ref, total_ref, o_ref):
    queries = spread(x_ref, (0, 0)) * scale
    keys_t = spread(x_ref, (0, 1))
    keys = keys_t.T
    values = spread(x_ref, (0, 2)).T
    grads = spread(g_ref, ())
    toks = x_ref.shape[-1]
    length = queries.shape[1]
    d_keys = jnp.zeros(queries.shape, F32)
    d_values = jnp.zeros(queries.shape, F32)
    for begin in range(0, length, step):
        query = queries[:, begin : begin + step]
        grad = grads[:, begin : begin + step]
        scores = dot(keys, query, 1, 0)
        probability = jnp.exp(scores - total_ref[0, :, begin : begin + step])
        d_prob = dot(values, grad, 1, 0)
        centered = jnp.sum(probability * d_prob, 0, keepdims=True)
        d_scores = (probability * (d_prob - centered)).astype(BF16)
        d_values += dot(grad, probability.astype(BF16), 1, 1)
        d_keys += dot(query, d_scores, 1, 1)
        d_query = (dot(keys_t, d_scores, 1, 0) * scale).astype(BF16)
        for at in range(0, step, toks):
            o_ref[(begin + at) // toks, 0, 0] = d_query[:, at : at + toks]
    d_keys = d_keys.astype(BF16)
    d_values = d_values.astype(BF16)
    for i in range(length // toks):
        o_ref[i, 0, 1] = d_keys[:, i * toks : (i + 1) * toks]
        o_ref[i, 0, 2] = d_values[:, i * toks : (i + 1) * toks]


def attend_back_call(qkv, grads, totals, step):
    count, per, _, head, toks = qkv.shape
    length = count * toks
    scale = head**-0.5
    return launch(
        functools.partial(attend_back_kernel, step, scale),
        (per,),
        [],
        [qkv, grads, totals],
        [ pl.BlockSpec((count, 1, 3, head, toks), lambda p: (0, p, 0, 0, 0)), pl.BlockSpec((count, head, toks), lambda p: (0, p, 0)), pl.BlockSpec((1, 1, length), lambda p: (p, 0, 0)), ],
        pl.BlockSpec((count, 1, 3, head, toks), lambda p: (0, p, 0, 0, 0)),
        stored(qkv.shape, BF16),
        [],
        cost(40 * per * length * length * head, 14 * per * length * head),
        "attend_back",
    )


def ffn_kernel(
    seqs,
    o_ref,
    x_ref,
    w_out_ref,
    w_up_ref,
    w_down_ref,
    bias_ref,
    norms_ref,
    mix_ref,
    normal0_ref,
    rstd0_ref,
    a_ref,
    g_ref,
    slope_ref,
    normal1_ref,
    rstd1_ref,
    f_ref,
    acc_ref,
):
    j = pl.program_id(0)
    per = o_ref.shape[1]
    head, toks = o_ref.shape[2:]

    @pl.when(j == 0)
    def _():
        for s in range(seqs):
            for h in range(HEADS):
                pair = s * HEADS + h
                mix_ref[h * head : (h + 1) * head, s * toks : (s + 1) * toks] = o_ref[
                    pair // per, pair % per
                ]
        attended = dot(mix_ref[...].T, flat_block(w_out_ref), 1, 0)
        normal, rstd = norm_forward(x_ref[...].astype(F32) + attended)
        normal0_ref[...] = normal
        rstd0_ref[...] = rstd
        normed = normal * norms_ref[0:1] + norms_ref[4:5]
        a_ref[...] = normed.astype(BF16)
        acc_ref[...] = normed

    up = dot(a_ref[...], flat_block(w_up_ref), 1, 0) + bias_ref[...]
    active, slope = gelu_parts(up)
    active = active.astype(BF16)
    g_ref[...] = active
    slope_ref[...] = slope
    acc_ref[...] += dot(active, flat_block(w_down_ref), 1, 0)

    @pl.when(j == pl.num_programs(0) - 1)
    def _():
        normal, rstd = norm_forward(acc_ref[...])
        normal1_ref[...] = normal
        rstd1_ref[...] = rstd
        f_ref[...] = (normal * norms_ref[1:2] + norms_ref[5:6]).astype(BF16)


def ffn_call(mixture, rows, packed, at_out, at_up, at_down, bias, norms, seqs):
    count, per, head, toks = mixture.shape
    total, width = rows.shape
    hidden = bias.shape[1]
    chunks = hidden // width
    blk = width // count
    owners = count // chunks
    return launch(
        functools.partial(ffn_kernel, seqs),
        (chunks,),
        [],
        [mixture, rows, packed, packed, packed, bias, norms],
        [ whole(mixture.shape), whole(rows.shape), pl.BlockSpec((count, blk, width), lambda j: (0, at_out, 0)), pl.BlockSpec((count, blk, width), lambda j: (0, at_up + j, 0)), pl.BlockSpec((owners, hidden // count, width), lambda j: (j, at_down, 0)), pl.BlockSpec((1, width), lambda j: (0, j)), whole(norms.shape), ],
        [ whole((width, total)), whole((total, width)), whole((total, 1)), whole((total, width)), pl.BlockSpec((total, width), lambda j: (0, j)), pl.BlockSpec((total, width), lambda j: (0, j)), whole((total, width)), whole((total, 1)), whole((total, width)), ],
        [ stored((width, total), BF16), stored((total, width), F32), stored((total, 1), F32), stored((total, width), BF16), stored((total, hidden), BF16), stored((total, hidden), F32), shape((total, width), F32), shape((total, 1), F32), shape((total, width), BF16)],
        [pltpu.VMEM((total, width), F32)],
        cost( 2 * total * width * (width + 2 * hidden), 4 * hidden * width + 10 * total * hidden ),
        "ffn",
    )


def ffn_back_kernel(
    seqs,
    slot_ref,
    order_ref,
    d_ref,
    g_ref,
    slope_ref,
    a_ref,
    normal_ref,
    rstd_ref,
    norms_ref,
    w_out_ref,
    w_up_ref,
    w_down_ref,
    total_ref,
    mix_ref,
    pooled_ref,
    d_proj_ref,
    *refs,
):
    j = pl.program_id(0)
    count, blk, width = w_up_ref.shape
    owners, share, _ = w_down_ref.shape
    half = count // 2
    send_refs, refs = refs[:half], refs[half:]
    keep_ref, bias_ref, d_attn_ref, sums_ref, d_mix_ref = refs[:5]
    db_ref, at_ref, acc_ref, part_ref, down_ref = refs[5:]

    @pl.when(j == 0)
    def _():
        db_ref[...] = d_ref[...].astype(BF16)
        at_ref[...] = a_ref[...].T
        acc_ref[...] = d_ref[...]

    part_ref[...] = dot(g_ref[...].T, db_ref[...], 1, 0)
    for i in range(owners):
        slot = slot_ref[j * owners + i]
        down_ref[slot] = part_ref[i * share : (i + 1) * share, :].astype(BF16)

    d_up = (dot(db_ref[...], flat_block(w_down_ref), 1, 1) * slope_ref[...]).astype(BF16)
    bias_ref[...] = column_sum(d_up.astype(F32))
    part_ref[...] = dot(at_ref[...], d_up, 1, 0)
    place = pl.ds(pl.multiple_of(share + j * blk, 16), blk)
    for pos in range(count):
        piece = part_ref[pl.ds(pl.multiple_of(order_ref[pos] * blk, 16), blk), :].astype(BF16)
        if pos < half:
            keep_ref[pos, place, :] = piece
        else:
            send_refs[pos - half][place, :] = piece
    acc_ref[...] += dot(d_up, flat_block(w_up_ref), 1, 1)

    @pl.when(j == pl.num_programs(0) - 1)
    def _():
        for pos in range(half):
            keep_ref[pos, 0:share, :] = down_ref[pos]
            send_refs[pos][0:share, :] = down_ref[half + pos]
        gradient = acc_ref[...]
        normal = normal_ref[...]
        sums_ref[0:1, :] = column_sum(gradient * normal)
        sums_ref[1:2, :] = column_sum(gradient)
        d_sum = norm_backward(normal, rstd_ref[...], norms_ref[0:1], gradient)
        d_attn_ref[...] = d_sum
        low = d_sum.astype(BF16)

        def put(row):
            for pos in range(count):
                start = pl.multiple_of(order_ref[pos] * blk, 16)
                piece = part_ref[pl.ds(start, blk), :].astype(BF16)
                if pos < half:
                    keep_ref[pos, row : row + blk, :] = piece
                else:
                    send_refs[pos - half][row : row + blk, :] = piece

        base = keep_ref.shape[1] - 2 * blk
        part_ref[...] = dot(mix_ref[...], low, 1, 0)
        put(base)
        part_ref[...] = dot(pooled_ref[...].T, d_proj_ref[...], 1, 0)
        put(base + blk)
        turned = dot(flat_block(w_out_ref), low, 1, 1).astype(BF16)
        per = seqs * HEADS // count
        head, toks = width // HEADS, d_mix_ref.shape[2]
        for s in range(seqs):
            for h in range(HEADS):
                pair = s * HEADS + h
                row = pair % per * head
                d_mix_ref[pair // per, row : row + head] = turned[
                    h * head : (h + 1) * head, s * toks : (s + 1) * toks
                ]
        rest = jnp.concatenate([total_ref[j] for j in range(total_ref.shape[0])], 0)
        rest = jnp.concatenate([rest, jnp.zeros((RIDE - rest.shape[0], LANES), F32)], 0)
        for part in range(3):
            low = rest.astype(BF16)
            rest = rest - low.astype(F32)
            row = per * head + part * RIDE
            for device in range(count):
                d_mix_ref[device, row : row + RIDE] = low


def ffn_back_call(
    slot, order, d_ffn, active, slope, normed, normal, rstd, norms, packed, at_out, at_up, at_down, totals, mixture, pooled, d_proj, seqs):
    total, width = d_ffn.shape
    hidden = active.shape[1]
    count = packed.shape[0]
    chunks = hidden // width
    blk = width // count
    share = hidden // count
    owners = count // chunks
    per = seqs * HEADS // count
    head = width // HEADS
    toks = total // seqs
    rows_out = share + (chunks + 2) * blk
    wide = pl.BlockSpec((total, width), lambda j, *_: (0, j))
    results = launch(
        functools.partial(ffn_back_kernel, seqs),
        (chunks,),
        [slot, order],
        [d_ffn, active, slope, normed, normal, rstd, norms, packed, packed, packed, totals, mixture, pooled, d_proj],
        [ whole(d_ffn.shape), wide, wide, whole(normed.shape), whole(normal.shape), whole(rstd.shape), whole(norms.shape), pl.BlockSpec((count, blk, width), lambda j, *_: (0, at_out, 0)), pl.BlockSpec((count, blk, width), lambda j, *_: (0, at_up + j, 0)), pl.BlockSpec((owners, share, width), lambda j, *_: (j, at_down, 0)), whole(totals.shape), whole(mixture.shape), whole(pooled.shape), whole(d_proj.shape), ],
        [ *[whole((rows_out, width))] * (count // 2), whole((count // 2, rows_out, width)), pl.BlockSpec((1, width), lambda j, *_: (0, j)), whole((total, width)), whole((2, width)), whole((count, per * head + 3 * RIDE, toks)), ],
        [ *[stored((rows_out, width), BF16)] * (count // 2), stored((count // 2, rows_out, width), BF16), stored((1, hidden), F32), stored((total, width), F32), stored((2, width), F32), stored((count, per * head + 3 * RIDE, toks), BF16), ],
        [ pltpu.VMEM((total, width), BF16), pltpu.VMEM((width, total), BF16), pltpu.VMEM((total, width), F32), pltpu.VMEM((width, width), F32), pltpu.VMEM((count, share, width), BF16), ],
        cost( 8 * total * width * hidden + 2 * total * width * width, 8 * hidden * width + 10 * total * hidden, ),
        "ffn_back",
    )
    return results[: count // 2], *results[count // 2 :]


def gates_kernel(
    seqs, groups_ref, ids_ref, back_ids_ref, table_ref, w_fwd_ref, w_rev_ref, bias_ref,
    z_ref, c_ref, totals_ref,
):
    s = pl.program_id(0)
    steps = ids_ref.shape[1]
    rows = 2 * seqs
    table = flat_block(table_ref)
    vocabulary = lax.broadcasted_iota(jnp.int32, (steps, NCHAR), 1)
    chunks = z_ref.shape[0]
    half = chunks * LANES
    for direction, (source, weight) in enumerate(((ids_ref, w_fwd_ref), (back_ids_ref, w_rev_ref))):
        onehot = jnp.where(source[0] == vocabulary, 1.0, 0.0).astype(BF16)
        embedded = dot(onehot, table, 1, 0).astype(BF16)
        gate_input = dot(embedded, flat_block(weight), 1, 0)
        own = slice(direction * half, (direction + 1) * half)
        update = jax.nn.sigmoid(gate_input[:, :half] + bias_ref[8:9, own])
        candidate = jnp.tanh(gate_input[:, half:] + bias_ref[9:10, own])
        place = pl.ds(s + direction * seqs, steps, stride=rows)
        for j in range(chunks):
            z_ref[j, place, :] = update[:, j * LANES : (j + 1) * LANES]
            c_ref[j, place, :] = candidate[:, j * LANES : (j + 1) * LANES]

    @pl.when(s == pl.num_programs(0) - 1)
    def _():
        def one(t, carry):
            states, products = carry
            place = pl.ds(pl.multiple_of(t * rows, rows), rows)
            new_states, new_products = [], []
            for j in range(chunks):
                update = z_ref[j, place, :]
                decay = 1.0 - update
                new_states.append(decay * states[j] + update * c_ref[j, place, :])
                new_products.append(products[j] * decay)
            return tuple(new_states), tuple(new_products)

        zero = jnp.zeros((rows, LANES), F32)
        states, products = lax.fori_loop(
            0, steps, one, ((zero,) * chunks, (zero + 1.0,) * chunks), unroll=8
        )
        for j in range(chunks):
            totals_ref[0, j] = products[j]
            totals_ref[1, j] = states[j]


def gates_call(groups, ids, packed, at_gru, at_table, bias):
    seqs, steps = ids.shape
    count, _, width = packed.shape
    blk = width // count
    table_rows = 4 * NCHAR // count
    per_group = NCHAR // table_rows
    chunks = width // 2 // LANES
    laid = (chunks, steps * 2 * seqs, LANES)
    return launch(
        functools.partial(gates_kernel, seqs),
        (seqs,),
        [groups],
        [ids[..., None], ids[:, ::-1, None], packed, packed, packed, bias],
        [ pl.BlockSpec((1, steps, 1), lambda s, g: (s, 0, 0)), pl.BlockSpec((1, steps, 1), lambda s, g: (s, 0, 0)), pl.BlockSpec((per_group, table_rows, width), lambda s, g: (g[s], at_table, 0)), pl.BlockSpec((count, blk, width), lambda s, g: (0, at_gru, 0)), pl.BlockSpec((count, blk, width), lambda s, g: (0, at_gru + 1, 0)), whole(bias.shape), ],
        [whole(laid), whole(laid), whole((2, chunks, 2 * seqs, LANES))],
        [stored(laid, F32), stored(laid, F32), stored((2, chunks, 2 * seqs, LANES), F32)],
        [],
        cost( 2 * seqs * steps * width * (2 * NCHAR + 2 * width), 16 * seqs * steps * width ),
        "gates",
    )


def entry_state(me, totals, products, rows, seqs, forward):
    count, chunks = products.shape[0], products.shape[1]
    first = lax.broadcasted_iota(jnp.int32, (rows, LANES), 0) < seqs
    result = []
    for j in range(chunks):
        state = jnp.zeros((rows, LANES), F32)
        for lap in range(count):
            up, down = lap, count - 1 - lap
            one, other = (up, down) if forward else (down, up)
            product = jnp.where(first, products[one, j], products[other, j])
            total = jnp.where(first, totals[one, j], totals[other, j])
            up_in, down_in = (up < me).astype(F32), (down > me).astype(F32)
            ahead = jnp.where(first, up_in, down_in) if forward else jnp.where(first, down_in, up_in)
            state = jnp.where(ahead > 0.5, product * state + total, state)
        result.append(state)
    return result


def states_kernel(
    seqs, me_ref, z_ref, c_ref, all_ref, starts_ref, ends_ref, lens_ref, w_ref,
    prior_ref, pooled_ref, proj_ref, proj_low_ref, hold_ref, state_ref, acc_ref,
):
    i = pl.program_id(0)
    last = pl.num_programs(0) - 1
    rows = 2 * seqs
    chunks = z_ref.shape[0]
    span = z_ref.shape[1] // rows
    toks = starts_ref.shape[1]
    half = chunks * LANES

    @pl.when(i == 0)
    def _():
        entry = entry_state(me_ref[0], all_ref[:, 1], all_ref[:, 0], rows, seqs, True)
        for j in range(chunks):
            state_ref[j] = entry[j]
        acc_ref[...] = jnp.zeros_like(acc_ref)

    def one(t, states):
        place = pl.ds(pl.multiple_of(t * rows, rows), rows)
        result = []
        for j in range(chunks):
            prior_ref[j, place, :] = states[j]
            update = z_ref[j, place, :]
            state = (1.0 - update) * states[j] + update * c_ref[j, place, :]
            hold_ref[j, place, :] = state
            result.append(state)
        return tuple(result)

    states = lax.fori_loop(0, span, one, tuple(state_ref[j] for j in range(chunks)), unroll=8)
    for j in range(chunks):
        state_ref[j] = states[j]
    count = lax.broadcasted_iota(jnp.int32, (toks, span), 1) + i * span
    for direction in range(2):
        place_of = count if direction == 0 else (last + 1) * span - 1 - count
        for s in range(seqs):
            member = jnp.where(
                (place_of >= starts_ref[s]) & (place_of < ends_ref[s]), 1.0, 0.0
            ).astype(BF16)
            held = jnp.concatenate(
                [
                    hold_ref[j, pl.ds(s + direction * seqs, span, stride=rows), :]
                    for j in range(chunks)
                ],
                axis=1,
            ).astype(BF16)
            acc_ref[s * toks : (s + 1) * toks, direction * half : (direction + 1) * half] += dot(
                member, held, 1, 0
            )

    @pl.when(i == last)
    def _():
        for s in range(seqs):
            rows_of = slice(s * toks, (s + 1) * toks)
            pooled_ref[rows_of, :] = (acc_ref[rows_of, :] / lens_ref[s]).astype(BF16)
        proj = dot(pooled_ref[...], flat_block(w_ref), 1, 0)
        proj_ref[...] = proj
        proj_low_ref[...] = proj.astype(BF16)


def collect_kernel(me_ref, *refs):
    for mask, ref in enumerate(refs[:-1]):
        refs[-1][me_ref[0] ^ mask] = ref[...]


def collect(me, parts):
    out = (len(parts), *parts[0].shape)
    return launch(
        collect_kernel,
        (1,),
        [me],
        parts,
        [whole(v.shape) for v in parts],
        whole(out),
        shape(out, parts[0].dtype),
        [],
        cost(0, 8 * len(parts) * parts[0].size),
        "collect",
    )


def states_call(me, z, c, gathered, starts, ends, lens, packed, at_char, parts):
    chunks, length, _ = z.shape
    seqs, toks, _ = starts.shape
    count, _, width = packed.shape
    blk = width // count
    span = length // parts
    total = seqs * toks
    stream = pl.BlockSpec((chunks, span, LANES), lambda i, *_: (0, i, 0))
    return launch(
        functools.partial(states_kernel, seqs),
        (parts,),
        [me],
        [z, c, gathered, starts, ends, lens, packed],
        [ stream, stream, whole(gathered.shape), whole(starts.shape), whole(ends.shape), whole(lens.shape), pl.BlockSpec((count, blk, width), lambda i, *_: (0, at_char, 0)), ],
        [stream] + [whole((total, width))] * 3,
        [stored(z.shape, F32), stored((total, width), BF16), stored((total, width), F32), shape((total, width), BF16), ],
        [ pltpu.VMEM((chunks, span, LANES), F32), pltpu.VMEM((chunks, 2 * seqs, LANES), F32), pltpu.VMEM((total, width), F32), ],
        cost(2 * total * width * (width + length // 8), 12 * chunks * length * LANES),
        "states",
    )


def states_back_kernel(
    seqs, d_ref, w_ref, lens_ref, starts_ref, ends_ref, z_ref, ds_ref, total_ref,
):
    rows = 2 * seqs
    chunks = z_ref.shape[0]
    steps = z_ref.shape[1] // rows
    toks = starts_ref.shape[2]
    half = chunks * LANES
    d_pooled = dot(d_ref[...], flat_block(w_ref), 1, 1)
    count = lax.broadcasted_iota(jnp.int32, (steps, toks), 0)
    for s in range(seqs):
        d_summed = (d_pooled[s * toks : (s + 1) * toks] / lens_ref[s]).astype(BF16)
        for direction in range(2):
            place_of = count if direction == 0 else steps - 1 - count
            member = jnp.where(
                (place_of >= starts_ref[s]) & (place_of < ends_ref[s]), 1.0, 0.0
            ).astype(BF16)
            d_states = dot(member, d_summed[:, direction * half : (direction + 1) * half], 1, 0)
            for j in range(chunks):
                ds_ref[j, pl.ds(s + direction * seqs, steps, stride=rows), :] = d_states[
                    :, j * LANES : (j + 1) * LANES
                ]

    def one(lap, carried):
        place = pl.ds(pl.multiple_of((steps - 1 - lap) * rows, rows), rows)
        return tuple(
            (1.0 - z_ref[j, place, :]) * (ds_ref[j, place, :] + carried[j]) for j in range(chunks)
        )

    zero = jnp.zeros((rows, LANES), F32)
    carried = lax.fori_loop(0, steps, one, (zero,) * chunks, unroll=8)
    for j in range(chunks):
        total_ref[j] = carried[j]


def states_back_call(d_proj, packed, at_char, lens, starts, ends, z):
    chunks, length, _ = z.shape
    seqs = starts.shape[0]
    count, _, width = packed.shape
    blk = width // count
    return launch(
        functools.partial(states_back_kernel, seqs),
        (1,),
        [],
        [d_proj, packed, lens, starts, ends, z],
        [ whole(d_proj.shape), pl.BlockSpec((count, blk, width), lambda i: (0, at_char, 0)), whole(lens.shape), whole(starts.shape), whole(ends.shape), whole(z.shape), ],
        [whole(z.shape), whole((chunks, 2 * seqs, LANES))],
        [stored(z.shape, F32), shape((chunks, 2 * seqs, LANES), F32)],
        [],
        cost( 2 * d_proj.shape[0] * width * (width + length // 8), 8 * chunks * length * LANES ),
        "states_back",
    )


def gates_back_kernel(
    seqs, me_ref, groups_ref, z_ref, c_ref, prior_ref, ds_ref, all_ref, back_ref, ids_ref,
    back_ids_ref, s_ref, bias_ref, du_ref, dc_ref, carried_ref, acc_ref,
):
    i = pl.program_id(0)
    rows = 2 * seqs
    chunks = z_ref.shape[0]
    span = z_ref.shape[1] // rows
    half = chunks * LANES

    @pl.when(i == 0)
    def _():
        parts = back_ref[...].astype(F32)
        summed = parts[:, :RIDE] + parts[:, RIDE : 2 * RIDE] + parts[:, 2 * RIDE :]
        totals = summed[:, : chunks * rows].reshape(-1, chunks, rows, LANES)
        entry = entry_state(me_ref[0], totals, all_ref[:, 0], rows, seqs, False)
        for j in range(chunks):
            carried_ref[j] = entry[j]
        acc_ref[...] = jnp.zeros_like(acc_ref)

    def one(lap, carried):
        place = pl.ds(pl.multiple_of((span - 1 - lap) * rows, rows), rows)
        result = []
        for j in range(chunks):
            update = z_ref[j, place, :]
            candidate = c_ref[j, place, :]
            total = ds_ref[j, place, :] + carried[j]
            decay = 1.0 - update
            gated = total * update
            du_ref[j, place, :] = gated * decay * (candidate - prior_ref[j, place, :])
            dc_ref[j, place, :] = gated * (1.0 - candidate * candidate)
            result.append(decay * total)
        return tuple(result)

    carried = lax.fori_loop(0, span, one, tuple(carried_ref[j] for j in range(chunks)), unroll=8)
    for j in range(chunks):
        carried_ref[j] = carried[j]
    vocabulary = lax.broadcasted_iota(jnp.int32, (NCHAR, span), 0)
    for direction in range(2):
        source = ids_ref if direction == 0 else back_ids_ref
        for s in range(seqs):
            place = pl.ds(s + direction * seqs, span, stride=rows)
            gradient = jnp.concatenate(
                [part[j, place, :] for part in (du_ref, dc_ref) for j in range(chunks)], axis=1
            ).astype(BF16)
            onehot = jnp.where(source[s] == vocabulary, 1.0, 0.0).astype(BF16)
            acc_ref[groups_ref[s], :, direction * 2 * half : (direction + 1) * 2 * half] += dot(
                onehot, gradient, 1, 0
            )

    @pl.when(i == pl.num_programs(0) - 1)
    def _():
        total = jnp.zeros((1, 4 * half), F32)
        for g in range(acc_ref.shape[0]):
            total += column_sum(acc_ref[g])
            s_ref[g] = acc_ref[g].astype(BF16)
        bias_ref[...] = total


def gates_back_call(me, groups, z, c, prior, ds, gathered, gathered_back, ids, n_groups, parts):
    chunks, length, _ = z.shape
    seqs, steps = ids.shape
    span = length // parts
    width = 2 * chunks * LANES
    stream = pl.BlockSpec((chunks, span, LANES), lambda i, *_: (0, parts - 1 - i, 0))
    lanes = pl.BlockSpec((seqs, 1, steps // parts), lambda i, *_: (0, 0, parts - 1 - i))
    return launch(
        functools.partial(gates_back_kernel, seqs),
        (parts,),
        [me, groups],
        [z, c, prior, ds, gathered, gathered_back, ids[:, None, :], ids[:, None, ::-1]],
        [stream] * 4 + [whole(gathered.shape), pl.BlockSpec((gathered_back.shape[0], 3 * RIDE, LANES), lambda i, *_: (0, gathered_back.shape[1] // (3 * RIDE) - 1, 0)), lanes, lanes],
        [whole((n_groups, NCHAR, 2 * width)), whole((1, 2 * width))],
        [shape((n_groups, NCHAR, 2 * width), BF16), shape((1, 2 * width), F32)],
        [ pltpu.VMEM((chunks, span, LANES), F32), pltpu.VMEM((chunks, span, LANES), F32), pltpu.VMEM((chunks, 2 * seqs, LANES), F32), pltpu.VMEM((n_groups, NCHAR, 2 * width), F32), ],
        cost(4 * seqs * steps * NCHAR * width, 16 * chunks * length * LANES),
        "gates_back",
    )


def shifted(values, toks, low, high):
    total = values.shape[0]
    row = lax.broadcasted_iota(jnp.int32, (total, 1), 0)
    before = pltpu.roll(values, 1, 0)
    after = pltpu.roll(values, total - 1, 0)
    for s in range(total // toks):
        before = jnp.where(row == s * toks, low[s], before)
        after = jnp.where(row == (s + 1) * toks - 1, high[s], after)
    return before.astype(BF16), after.astype(BF16)


def conv_kernel(
    toks, f_ref, p_ref, normal_ref, proj_ref, norms_ref, low_ref, high_ref, w_ref, tok_g_ref,
    char_g_ref, tok_ref, char_ref, d_tok_ref, d_char_ref, dm_ref, sums_ref, begin_ref, end_ref,
    acc_ref, x_ref,
):
    half, k = pl.program_id(0), pl.program_id(1)
    width = f_ref.shape[1]

    @pl.when((half == 0) & (k == 0))
    def _():
        for part, source in enumerate((f_ref, p_ref)):
            columns = slice(part * width, (part + 1) * width)
            before, after = shifted(
                source[...].astype(F32),
                toks,
                low_ref[:, :, columns].astype(F32),
                high_ref[:, :, columns].astype(F32),
            )
            x_ref[0, :, columns] = before
            x_ref[1, :, columns] = source[...]
            x_ref[2, :, columns] = after

    product = dot(x_ref[k], flat_block(w_ref), 1, 0)

    @pl.when(k == 0)
    def _():
        acc_ref[...] = product

    @pl.when(k > 0)
    def _():
        acc_ref[...] += product

    def finish(which, base, grad_ref, out_ref, d_ref):
        normal, rstd = norm_forward(base + acc_ref[...])
        gain = norms_ref[2 + which : 3 + which]
        out_ref[...] = normal * gain + norms_ref[6 + which : 7 + which]
        gradient = grad_ref[...].astype(F32)
        sums_ref[0, 0:1, :] = column_sum(gradient * normal)
        sums_ref[0, 1:2, :] = column_sum(gradient)
        d_sum = norm_backward(normal, rstd, gain, gradient)
        d_ref[...] = d_sum
        low_sum = d_sum.astype(BF16)
        dm_ref[...] = low_sum
        for s in range(begin_ref.shape[0]):
            begin_ref[s] = low_sum[s * toks : s * toks + 1]
            end_ref[s] = low_sum[(s + 1) * toks - 1 : (s + 1) * toks]

    @pl.when((half == 0) & (k == 2))
    def _():
        finish(
            0, normal_ref[...] * norms_ref[1:2] + norms_ref[5:6], tok_g_ref, tok_ref, d_tok_ref
        )

    @pl.when((half == 1) & (k == 2))
    def _():
        finish(1, proj_ref[...], char_g_ref, char_ref, d_char_ref)


def conv_call(f_low, proj_low, normal1, proj, norms, low, high, packed, tok_grad, char_grad, seqs, carry):
    total, width = f_low.shape
    count = packed.shape[0]
    blk = 2 * width // count
    rows = (total, width)
    return launch(
        functools.partial(conv_kernel, total // seqs),
        (2, 3),
        [],
        [f_low, proj_low, normal1, proj, norms, low, high, packed, tok_grad, char_grad],
        [ whole(rows), whole(rows), whole(rows), whole(rows), whole(norms.shape), whole(low.shape), whole(high.shape), pl.BlockSpec((count, blk, width), lambda h, k: (0, 2 * k + h, 0)), whole(rows), whole(rows), ],
        [ whole(rows), whole(rows), whole(rows), whole(rows), pl.BlockSpec(rows, lambda h, k: (0, h)), pl.BlockSpec((1, 2, width), lambda h, k: (h, 0, 0)), pl.BlockSpec((seqs, 1, width), lambda h, k: (0, 0, h)), pl.BlockSpec((seqs, 1, width), lambda h, k: (0, 0, h)), ],
        [ stored(rows, F32), stored(rows, F32), shape(rows, F32), shape(rows, F32), shape((total, 2 * width), BF16), shape((2, 2, width), F32), shape((seqs, 1, 2 * width), BF16), shape((seqs, 1, 2 * width), BF16), ],
        [pltpu.VMEM(rows, F32), pltpu.VMEM((3, total, 2 * width), BF16)],
        cost(24 * total * width * width, 24 * width * width + 40 * total * width),
        "conv",
        carry,
    )


def place_blocks(part_ref, order_ref, send_ref, keep_ref, blk, row=0):
    count = part_ref.shape[0] // blk
    for pos in range(count):
        start = pl.multiple_of(order_ref[pos] * blk, 16)
        piece = part_ref[pl.ds(start, blk), :].astype(BF16)
        if pos < count // 2:
            keep_ref[pos, row : row + blk, :] = piece
        else:
            send_ref[pos - count // 2, row : row + blk, :] = piece


def conv_weight_kernel(
    toks, order_ref, f_ref, p_ref, other_f_ref, other_p_ref, dm_ref, other_dm_ref, low_ref,
    high_ref, other_low_ref, other_high_ref, keep_a_ref, sent_a_ref, keep_b_ref, sent_b_ref,
    turned_ref, whole_ref, part_ref,
):
    k, half = pl.program_id(0), pl.program_id(1)
    total, width = f_ref.shape
    pieces = 2 * keep_a_ref.shape[0]
    blk = keep_a_ref.shape[1]

    @pl.when((k == 0) & (half == 0))
    def _():
        edges = ((low_ref[...], high_ref[...]), (other_low_ref[...], other_high_ref[...]))
        pairs = ((f_ref, p_ref), (other_f_ref, other_p_ref))
        for core, (pair, (low, high)) in enumerate(zip(pairs, edges)):
            for part, source in enumerate(pair):
                columns = slice(part * width, (part + 1) * width)
                middle = source[...]
                before, after = shifted(
                    middle.astype(F32),
                    toks,
                    low[:, :, columns].astype(F32),
                    high[:, :, columns].astype(F32),
                )
                for at, value in enumerate((before, middle, after)):
                    whole_ref[at, columns, :] = value.T
            for pos in range(pieces):
                start = pl.multiple_of(order_ref[pos] * blk, 16)
                for at in range(3):
                    turned_ref[
                        at, pos * blk : (pos + 1) * blk, core * total : (core + 1) * total
                    ] = whole_ref[at, pl.ds(start, blk), :]

    turned = turned_ref[k]
    part_ref[...] = dot(turned[:, :total], dm_ref[...], 1, 0) + dot(
        turned[:, total:], other_dm_ref[...], 1, 0
    )

    def put(keep_ref, sent_ref, kept, sent):
        for index, (one, other) in enumerate(zip(kept, sent)):
            keep_ref[index] = part_ref[one * blk : (one + 1) * blk, :].astype(BF16)
            sent_ref[index] = part_ref[other * blk : (other + 1) * blk, :].astype(BF16)

    at = 2 * k + half

    @pl.when(at < 3)
    def _():
        put(keep_a_ref, sent_a_ref, range(pieces // 2), range(pieces // 2, pieces))

    @pl.when(at >= 3)
    def _():
        put(keep_b_ref, sent_b_ref, range(0, pieces, 2), range(1, pieces, 2))


def conv_weight_call(order, own, other, dm, other_dm, edges, count):
    total, width = own[0].shape
    toks = total // edges[0].shape[0]
    blk = 2 * width // count
    out = (count // 4, 3 * blk, width)
    first = pl.BlockSpec((count // 4, blk, width), lambda k, h, *_: (0, jnp.minimum(2 * k + h, 2), 0))
    second = pl.BlockSpec(
        (count // 4, blk, width), lambda k, h, *_: (0, jnp.maximum(2 * k + h - 3, 0), 0)
    )
    columns = pl.BlockSpec((total, width), lambda k, h, *_: (0, h))
    plain = [*own, *other]
    keep_a, sent_a, keep_b, sent_b = launch(
        functools.partial(conv_weight_kernel, toks),
        (3, 2),
        [order],
        [*plain, dm, other_dm, *edges],
        [*[whole(v.shape) for v in plain], columns, columns, *[whole(v.shape) for v in edges]],
        [first, first, second, second],
        [stored(out, BF16)] * 4,
        [
            pltpu.VMEM((3, width, 2 * total), BF16),
            pltpu.VMEM((3, 2 * width, total), BF16),
            pltpu.VMEM((width, width), F32),
        ],
        cost(24 * total * width * width, 12 * width * width),
        "conv_weight",
    )
    return [[keep_a, sent_a], [keep_b, sent_b]]


def conv_back_kernel(
    toks, dm_ref, low_ref, high_ref, w_ref, d_tok_ref, d_char_ref, normal_ref, rstd_ref,
    norms_ref, d_proj_ref, d_ffn_ref, sums_ref, shift_ref, acc_ref,
):
    k, half = pl.program_id(0), pl.program_id(1)
    width = d_tok_ref.shape[1]

    @pl.when((half == 0) & (k == 0))
    def _():
        for part in range(2):
            columns = slice(part * width, (part + 1) * width)
            source = dm_ref[:, columns]
            before, after = shifted(
                source.astype(F32),
                toks,
                low_ref[:, :, columns].astype(F32),
                high_ref[:, :, columns].astype(F32),
            )
            shift_ref[part] = after
            shift_ref[2 + part] = source
            shift_ref[4 + part] = before

    product = dot(shift_ref[2 * k + half], flat_block(w_ref), 1, 1)

    @pl.when((k == 0) & (half == 0))
    def _():
        acc_ref[...] = product

    @pl.when((k > 0) | (half > 0))
    def _():
        acc_ref[...] += product

    @pl.when((k == 2) & (half == 1))
    def _():
        d_proj_ref[...] = (d_char_ref[...] + acc_ref[:, width:]).astype(BF16)
        gradient = d_tok_ref[...] + acc_ref[:, :width]
        normal = normal_ref[...]
        sums_ref[0:1, :] = column_sum(gradient * normal)
        sums_ref[1:2, :] = column_sum(gradient)
        d_ffn_ref[...] = norm_backward(normal, rstd_ref[...], norms_ref[1:2], gradient)


def conv_back_call(d_merged, low, high, packed, d_tok, d_char, normal1, rstd1, norms, seqs):
    total, width = d_tok.shape
    count = packed.shape[0]
    blk = 2 * width // count
    rows = (total, width)
    return launch(
        functools.partial(conv_back_kernel, total // seqs),
        (3, 2),
        [],
        [d_merged, low, high, packed, d_tok, d_char, normal1, rstd1, norms],
        [ whole(d_merged.shape), whole(low.shape), whole(high.shape), pl.BlockSpec((count, blk, width), lambda k, h: (0, 2 * k + h, 0)), whole(rows), whole(rows), whole(rows), whole(rstd1.shape), whole(norms.shape), ],
        [whole(rows), whole(rows), whole((2, width))],
        [shape(rows, BF16), shape(rows, F32), shape((2, width), F32)],
        [ pltpu.VMEM((6, total, width), BF16), pltpu.VMEM((total, 2 * width), F32), ],
        cost(24 * total * width * width, 24 * width * width + 20 * total * width),
        "conv_back",
    )


def rest_kernel(
    order_ref, table_ref, s_ref, w0_ref, w1_ref, send_ref, keep_ref, part_ref,
):
    count, blk, width = w0_ref.shape
    rows = part_ref.shape[0]
    turned = flat_block(table_ref).T
    sums = s_ref[...].reshape(rows, 2 * width)
    for part in range(2):
        part_ref[0:width, :] = dot(turned, sums[:, part * width : (part + 1) * width], 1, 0)
        place_blocks(part_ref.at[0:width], order_ref, send_ref, keep_ref, blk, part * blk)
    part_ref[...] = dot(sums[:, :width], flat_block(w0_ref), 1, 1) + dot(
        sums[:, width:], flat_block(w1_ref), 1, 1
    )
    place_blocks(part_ref, order_ref, send_ref, keep_ref, rows // count, 2 * blk)


def rest_call(order, packed, at_table, at_gru, sums, height):
    count, _, width = packed.shape
    blk = width // count
    rows = sums.shape[0] * sums.shape[1]
    table_rows = rows // count
    out = (count // 2, height, width)
    return launch(
        rest_kernel,
        (1,),
        [order],
        [packed, sums, packed, packed],
        [
            pl.BlockSpec((count, table_rows, width), lambda i, *_: (0, at_table, 0)),
            whole(sums.shape),
            pl.BlockSpec((count, blk, width), lambda i, *_: (0, at_gru, 0)),
            pl.BlockSpec((count, blk, width), lambda i, *_: (0, at_gru + 1, 0)),
        ],
        [whole(out), whole(out)],
        [stored(out, BF16), stored(out, BF16)],
        [pltpu.VMEM((rows, width), F32)],
        cost(8 * rows * width * width, 20 * width * width),
        "rest",
    )


def qkv_back_kernel(
    seqs, order_ref, d_ref, x_ref, w_ref, d_attn_ref,
    sums0_ref, sums1_ref, sums23_ref, bias_ref, bias_up_ref, out_ref, send_ref, keep_ref, xt_ref,
    dt_ref, part_ref, small_ref,
):
    j = pl.program_id(0)
    per = d_ref.shape[1]
    head, toks = d_ref.shape[3:]
    pieces, _, width = send_ref.shape
    blk = width // (2 * pieces)
    half = width // 2

    def put(row):
        for pos in range(2 * pieces):
            start = pl.multiple_of(order_ref[pos] * blk, 16)
            piece = part_ref[pl.ds(start, blk), :].astype(BF16)
            if pos < pieces:
                keep_ref[pos, row, :] = piece
            else:
                send_ref[pos - pieces, row, :] = piece

    @pl.when(j == 0)
    def _():
        xt_ref[...] = x_ref[...].T
        out_ref[...] = d_attn_ref[...]
        small_ref[...] = jnp.zeros_like(small_ref)
        for row, ref in enumerate((sums0_ref, sums1_ref)):
            small_ref[row : row + 1] = ref[0:1]
            small_ref[4 + row : 5 + row] = ref[1:2]
        for which in range(2):
            small_ref[2 + which : 3 + which] = sums23_ref[which, 0:1]
            small_ref[6 + which : 7 + which] = sums23_ref[which, 1:2]
        for part in range(2):
            own = slice(part * half, (part + 1) * half)
            small_ref[8:9, own] = bias_ref[:, part * width : part * width + half]
            small_ref[9:10, own] = bias_ref[:, part * width + half : (part + 1) * width]
        for part in range(bias_up_ref.shape[1] // width):
            small_ref[10 + part : 11 + part] = bias_up_ref[:, part * width : (part + 1) * width]
        small = small_ref[...].astype(BF16)
        for pos in range(pieces):
            keep_ref[pos, 3 * blk : 3 * blk + SMALL_ROWS, :] = small
            send_ref[pos, 3 * blk : 3 * blk + SMALL_ROWS, :] = small

    for s in range(seqs):
        for h in range(HEADS):
            pair = s * HEADS + h
            dt_ref[h * head : (h + 1) * head, s * toks : (s + 1) * toks] = d_ref[
                pair // per, pair % per, 0
            ]
    gradient = dt_ref[...].T
    part_ref[...] = dot(xt_ref[...], gradient, 1, 0)
    put(pl.ds(pl.multiple_of(j * blk, 16), blk))
    out_ref[...] += dot(gradient, flat_block(w_ref), 1, 1)


def qkv_back_call(
    order, d_qkv, rows, packed, base, d_attn, small, seqs, height
):
    count, per, _, head, toks = d_qkv.shape
    total, width = rows.shape
    blk = width // count
    out = (count // 2, height, width)
    rest = [d_attn, *small]
    return launch(
        functools.partial(qkv_back_kernel, seqs),
        (3,),
        [order],
        [d_qkv, rows, packed, *rest],
        [
            pl.BlockSpec((count, per, 1, head, toks), lambda j, *_: (0, 0, j, 0, 0)),
            whole(rows.shape),
            pl.BlockSpec((count, blk, width), lambda j, *_: (0, base + j, 0)),
            *[whole(v.shape) for v in rest],
        ],
        [whole((total, width)), whole(out), whole(out)],
        [stored((total, width), F32), stored(out, BF16), stored(out, BF16)],
        [
            pltpu.VMEM((width, total), BF16),
            pltpu.VMEM((width, total), BF16),
            pltpu.VMEM((width, width), F32),
            pltpu.VMEM((SMALL_ROWS, width), F32),
        ],
        cost(16 * total * width * width, 20 * width * width + 16 * total * width),
        "qkv_back",
    )


def pack_kernel(layout, *refs):
    ins, out_ref = refs[:-1], refs[-1]
    at = 0
    out_ref[...] = jnp.zeros_like(out_ref)
    width = out_ref.shape[1]
    for ref, row in zip(ins, layout):
        height, columns = ref.shape
        if columns < width:
            out_ref[row : row + height, :columns] = ref[...]
        else:
            for block in range(columns // width):
                out_ref[row + block * height : row + (block + 1) * height, :] = ref[
                    :, block * width : (block + 1) * width
                ]


def pack(arrays, layout, rows, width):
    return launch(
        functools.partial(pack_kernel, layout),
        (1,),
        [],
        arrays,
        [whole(v.shape) for v in arrays],
        whole((rows, width)),
        shape((rows, width), BF16),
        [],
        cost(0, 4 * rows * width),
        "pack",
    )


def swap(value, axis, bit):
    size = lax.axis_size(axis)
    return lax.ppermute(value, axis, [(i, i ^ (1 << bit)) for i in range(size)])


def add_low(kept, arrived):
    return (kept.astype(F32) + arrived.astype(F32)).astype(BF16)


def fold_kernel(keep_top, keep_bottom, came_top, came_bottom, ka_ref, sa_ref, kb_ref, sb_ref):
    half = ka_ref.shape[0]
    for index in range(half):
        ka_ref[index] = add_low(keep_top[index], came_top[index])
        sa_ref[index] = add_low(keep_top[half + index], came_top[half + index])
        kb_ref[index] = add_low(keep_bottom[2 * index], came_bottom[2 * index])
        sb_ref[index] = add_low(keep_bottom[2 * index + 1], came_bottom[2 * index + 1])


def tiles(rows):
    return 3 if PLACED and rows % 48 == 0 else 1


def fold_pieces_kernel(keep_top, keep_bottom, *refs):
    pieces = keep_top.shape[0]
    top, bottom, outs = refs[:pieces], refs[pieces : 2 * pieces], refs[2 * pieces :]
    ka_ref, sa_ref, kb_ref, sb_ref = outs
    half = pieces // 2
    for index in range(half):
        ka_ref[index] = add_low(keep_top[index], top[index][...])
        sa_ref[index] = add_low(keep_top[half + index], top[half + index][...])
        kb_ref[index] = add_low(keep_bottom[2 * index], bottom[2 * index][...])
        sb_ref[index] = add_low(keep_bottom[2 * index + 1], bottom[2 * index + 1][...])


def fold(keep, arrived):
    pieces, rows, width = keep.shape
    steps = tiles(rows // 2)
    tile = rows // 2 // steps
    top = pl.BlockSpec((pieces, tile, width), lambda i: (0, i, 0))
    bottom = pl.BlockSpec((pieces, tile, width), lambda i: (0, steps + i, 0))
    one_top = pl.BlockSpec((tile, width), lambda i: (i, 0))
    one_bottom = pl.BlockSpec((tile, width), lambda i: (steps + i, 0))
    ka, sa, kb, sb = launch(
        fold_pieces_kernel,
        (steps,),
        [],
        [keep, keep, *arrived, *arrived],
        [top, bottom] + [one_top] * pieces + [one_bottom] * pieces,
        [pl.BlockSpec((pieces // 2, tile, width), lambda i: (0, i, 0))] * 4,
        [stored((pieces // 2, rows // 2, width), BF16)] * 4,
        [],
        cost(pieces * rows * width, 6 * pieces * rows * width),
        "fold",
    )
    return [[ka, sa], [kb, sb]]


def send_links(state, step):
    bits = lax.axis_size("seq").bit_length() - 1
    return [
        [kept, swap(sent, "seq", bit)] for (kept, sent), bit in zip(state, (step, bits - step))
    ]


def split(state):
    pieces, rows, width = state[0][0].shape
    steps = tiles(rows)
    spec = pl.BlockSpec((pieces, rows // steps, width), lambda i, *_: (0, i, 0))
    out = pl.BlockSpec((pieces // 2, rows // steps, width), lambda i, *_: (0, i, 0))
    return plan(
        fold_kernel,
        (steps,),
        [],
        [state[0][0], state[1][0], state[0][1], state[1][1]],
        [spec] * 4,
        [out] * 4,
        [stored((pieces // 2, rows, width), BF16)] * 4,
        [],
        cost(pieces * rows * width, 12 * pieces * rows * width),
        "split",
    )


def paired(values):
    ka, sa, kb, sb = values
    return [[ka, sa], [kb, sb]]


def cross_kernel(place_ref, ka_ref, kb_ref, ca_ref, cb_ref, kept_ref, sent_ref):
    high = (place_ref[0] & 1) == 1
    first = add_low(ka_ref[0], ca_ref[0])
    second = add_low(kb_ref[0], cb_ref[0])
    kept_ref[...] = jnp.where(high, second, first)
    sent_ref[...] = jnp.where(high, first, second)


def cross(place, state):
    _, rows, width = state[0][0].shape
    steps = tiles(rows)
    spec = pl.BlockSpec((1, rows // steps, width), lambda i, *_: (0, i, 0))
    return plan(
        cross_kernel,
        (steps,),
        [place],
        [state[0][0], state[1][0], state[0][1], state[1][1]],
        [spec] * 4,
        [pl.BlockSpec((rows // steps, width), lambda i, *_: (i, 0))] * 2,
        [stored((rows, width), BF16)] * 2,
        [],
        cost(rows * width, 12 * rows * width),
        "cross",
    )


def halve_kernel(bit, place_ref, kept_ref, came_ref, next_ref, sent_ref):
    high = ((place_ref[0] >> bit) & 1) == 1
    rows = next_ref.shape[0]
    first = add_low(kept_ref[:rows], came_ref[:rows])
    second = add_low(kept_ref[rows:], came_ref[rows:])
    next_ref[...] = jnp.where(high, second, first)
    sent_ref[...] = jnp.where(high, first, second)


def halve(place, bit, kept, came):
    rows, width = kept.shape
    return plan(
        functools.partial(halve_kernel, bit),
        (1,),
        [place],
        [kept, came],
        [whole(kept.shape)] * 2,
        [whole((rows // 2, width))] * 2,
        [stored((rows // 2, width), BF16)] * 2,
        [],
        cost(rows * width, 6 * rows * width),
        "halve",
    )


def add_kernel(kept_ref, came_ref, out_ref):
    out_ref[...] = add_low(kept_ref[...], came_ref[...])


def add(kept, came):
    return plan(
        add_kernel,
        (1,),
        [],
        [kept, came],
        [whole(kept.shape)] * 2,
        whole(kept.shape),
        stored(kept.shape, BF16),
        [],
        cost(kept.size, 6 * kept.size),
        "add",
    )


def assemble_kernel(bit, place_ref, held_ref, came_ref, out_ref):
    high = ((place_ref[0] >> bit) & 1) == 1
    rows = held_ref.shape[0]
    held, came = held_ref[...], came_ref[...]
    out_ref[:rows] = jnp.where(high, came, held)
    out_ref[rows:] = jnp.where(high, held, came)


def assemble(place, bit, held, came):
    rows, width = held.shape
    return plan(
        functools.partial(assemble_kernel, bit),
        (1,),
        [place],
        [held, came],
        [whole(held.shape)] * 2,
        whole((2 * rows, width)),
        stored((2 * rows, width), BF16),
        [],
        cost(rows * width, 8 * rows * width),
        "assemble",
    )


def finish_kernel(layout, place_ref, held_ref, came_ref, *out_refs):
    high = (place_ref[0] & 1) == 1
    rows = held_ref.shape[0]
    for begin, size, out, index in layout:
        part = slice(begin % rows, begin % rows + size)
        held, came = held_ref[part].astype(F32), came_ref[part].astype(F32)
        out_refs[out][index] = jnp.where(high == (begin < rows), came, held)


def cut(layout, rows):
    for begin, size, out, index in layout:
        edges = [begin, begin + size]
        if begin < rows < begin + size:
            edges.insert(1, rows)
        for low, high in zip(edges, edges[1:]):
            yield low, high - low, out, index[:-2] + (slice(low - begin, high - begin), index[-1])


def finish(place, held, came, layout, outs):
    layout = list(cut(layout, held.shape[0]))
    return plan(
        functools.partial(finish_kernel, layout),
        (1,),
        [place],
        [held, came],
        [whole(held.shape)] * 2,
        [whole(dims) for dims in outs],
        [stored(dims, F32) for dims in outs],
        [],
        cost(held.size, 16 * held.size),
        "finish",
    )


def across_halves(place, kept, sent, layout, outs):
    bits = lax.axis_size("batch").bit_length() - 1
    came = swap(sent, "batch", 0)
    for bit in range(1, bits):
        kept, sent = yield halve(place, bit, kept, came)
        came = swap(sent, "batch", bit)
    (held,) = yield add(kept, came)
    for bit in reversed(range(bits)):
        came = swap(held, "batch", bit)
        if bit:
            (held,) = yield assemble(place, bit, held, came)
    return (yield finish(place, held, came, layout, outs))


def deal_kernel(place_ref, ka_ref, kb_ref, ca_ref, cb_ref, *refs):
    outs, sum_ref = refs[:-1], refs[-1]
    rows, part = ka_ref.shape[1], outs[0].shape[0]
    sum_ref[:rows] = add_low(ka_ref[0], ca_ref[0])
    sum_ref[rows:] = add_low(kb_ref[0], cb_ref[0])
    for mask, out_ref in enumerate(outs):
        start = pl.multiple_of((place_ref[0] ^ mask) * part, 16)
        out_ref[...] = sum_ref[pl.ds(start, part), :]


def total_kernel(*refs):
    total = refs[0][...].astype(F32)
    for ref in refs[1:-1]:
        total += ref[...].astype(F32)
    refs[-1][...] = total.astype(BF16)


def spread_kernel(layout, small_at, parts, place_ref, me_ref, *refs):
    ins, outs, all_ref = refs[:parts], refs[parts:-1], refs[-1]
    rows = ins[0].shape[0]
    for mask, ref in enumerate(ins):
        start = pl.multiple_of((place_ref[0] ^ mask) * rows, 16)
        all_ref[pl.ds(start, rows), :] = ref[...]
    for begin, size, out, index in layout:
        outs[out][index] = all_ref[begin : begin + size].astype(F32)
    blk, share = outs[-5].shape[1], outs[-1].shape[1]
    small = all_ref[small_at : small_at + SMALL_ROWS].astype(F32)
    width = small.shape[1]
    me = me_ref[0]
    mine = pltpu.roll(small, lax.rem(width - me * blk, width), 1)[:, :blk]
    outs[-5][...] = mine[0:4]
    outs[-4][...] = mine[4:8]
    outs[-3][...] = mine[8:9]
    outs[-2][...] = mine[9:10]
    spot = me * share
    turned = pltpu.roll(small, lax.rem(width - lax.rem(spot, width), width), 1)[:, :share]
    row = lax.broadcasted_iota(jnp.int32, turned.shape, 0)
    outs[-1][...] = column_sum(jnp.where(row == 10 + lax.div(spot, width), turned, 0.0))


def across_direct(place, me, state, layout, small_at, outs):
    for link in range(2, lax.axis_size("seq").bit_length() - 1):
        state = send_links(paired((yield split(state))), link)
    parts = lax.axis_size("batch")
    _, rows, width = state[0][0].shape
    part = (2 * rows // parts, width)
    ends = [(mask, [(i, i ^ mask) for i in range(parts)]) for mask in range(1, parts)]
    pieces = yield plan(
        deal_kernel,
        (1,),
        [place],
        [state[0][0], state[1][0], state[0][1], state[1][1]],
        [whole(state[0][0].shape)] * 4,
        [whole(part)] * parts,
        [stored(part, BF16)] * parts,
        [pltpu.VMEM((2 * rows, width), BF16)],
        cost(rows * width, 12 * rows * width),
        "deal",
    )
    came = [lax.ppermute(pieces[mask], "batch", pairs) for mask, pairs in ends]
    (held,) = yield plan(
        total_kernel,
        (1,),
        [],
        [pieces[0], *came],
        [whole(part)] * parts,
        [whole(part)],
        [stored(part, BF16)],
        [],
        cost(rows * width, 5 * rows * width),
        "total",
    )
    came = [lax.ppermute(held, "batch", pairs) for _, pairs in ends]
    return (
        yield plan(
            functools.partial(spread_kernel, layout, small_at, parts),
            (1,),
            [place, me],
            [held, *came],
            [whole(part)] * parts,
            [whole(dims) for dims in outs],
            [stored(dims, F32) for dims in outs],
            [pltpu.VMEM((2 * rows, width), BF16)],
            cost(rows * width, 12 * rows * width),
            "spread",
        )
    )


def neighbours(first, last):
    count = lax.axis_size("seq")
    up = [(i, i + 1) for i in range(count - 1)]
    down = [(target, source) for source, target in up]
    return lax.ppermute(last, "seq", up), lax.ppermute(first, "seq", down)


def local(
    hidden, char_ids, group_ids, word_lengths, qkv_weight, out_weight, up_weight, ffn_bias,
    down_weight, gru_weight, gate_bias, candidate_bias, char_weight, conv_weight, char_table,
    norm_gain, norm_shift, tok_grad, char_grad,
):
    count = lax.axis_size("seq")
    bits = count.bit_length() - 1
    me = lax.axis_index("seq").astype(jnp.int32)
    seqs, toks, width = hidden.shape
    total = seqs * toks
    half = width // 2
    blk = width // count
    share = ffn_bias.shape[0]
    table_rows = char_table.shape[0]
    chars = char_ids.shape[1]
    reverse = [int(format(i, f"0{bits}b")[::-1], 2) for i in range(count)]
    order = jnp.asarray(reverse, jnp.int32) ^ me
    slot = sum(
        (((jnp.arange(count, dtype=jnp.int32) ^ me) >> b) & 1) << (bits - 1 - b) for b in range(bits)
    )
    me_one = me.reshape(1)

    place = lax.axis_index("batch").astype(jnp.int32).reshape(1)
    LATEST.clear()
    PLACED[:] = [True]
    NEAR.clear()

    table_at = share
    small_at = table_at + table_rows
    block_at = small_at + 16
    block_at += -block_at % blk
    pack_rows = block_at + 11 * blk
    small = jnp.concatenate(
        [norm_gain.T, norm_shift.T, gate_bias[None], candidate_bias[None]], 0
    )
    small = jnp.pad(small, ((0, 6), (0, width - blk)))
    small = small.at[10, :share].set(ffn_bias)
    arrays = [
        down_weight, char_table, small, gru_weight, qkv_weight, char_weight, out_weight, up_weight
    ]
    at_block = block_at // blk
    at_gru, at_qkv, at_char, at_out, at_up = (at_block + i for i in (0, 2, 5, 6, 7))
    layout = [0, table_at, small_at] + [i * blk for i in (at_gru, at_qkv, at_char, at_out, at_up)]
    at_table, at_down = table_at // table_rows, 0
    first = pack(arrays, layout, pack_rows, width)
    third = pack(
        [conv_weight[k] for k in range(3)], [k * 4 * blk for k in range(3)], 12 * blk, width
    )
    first = lax.all_gather(first, "seq", axis=0)
    third = lax.all_gather(third, "seq", axis=0)
    vectors = (
        first[:, small_at : small_at + 10, :blk].astype(F32).transpose(1, 0, 2).reshape(10, width)
    )
    bias_up = first[:, small_at + 10, :share].astype(F32).reshape(1, -1)
    norms = vectors

    rows = hidden.reshape(total, width)
    words = word_lengths.reshape(seqs, toks)
    ends = jnp.cumsum(words, axis=1)
    starts = ends - words
    lens = words.astype(F32)[..., None]

    qkv = qkv_call(rows, first, at_qkv, seqs, count)
    qkv = lax.all_to_all(qkv, "seq", 0, 0, tiled=True)
    z, c, block_totals = gates_call(group_ids, char_ids, first, at_gru, at_table, vectors)
    gathered = [block_totals] + [
        lax.ppermute(block_totals, "seq", [(i, i ^ mask) for i in range(count)])
        for mask in range(1, count)
    ]
    step = (1 << 19) // (count * toks)
    mixture, totals = attend_call(qkv, 2 * step)
    mixture = lax.all_to_all(mixture, "seq", 0, 0, tiled=True)
    gathered = collect(me_one, gathered)
    prior, pooled, proj, proj_low = states_call(
        me_one, z, c, gathered, starts[..., None], ends[..., None], lens, first, at_char, 2
    )
    mix_t, normal0, rstd0, normed, active, slope, normal1, rstd1, f_low = ffn_call(
        mixture, rows, first, at_out, at_up, at_down, bias_up, norms, seqs
    )

    def edges(left, right):
        joined = [v.reshape(seqs, toks, width) for v in (left, right)]
        return (
            jnp.concatenate([v[:, :1] for v in joined], -1),
            jnp.concatenate([v[:, -1:] for v in joined], -1),
        )

    begin, end = edges(f_low, proj_low)
    low, high = neighbours(begin, end)
    other = [swap(v, "seq", 0) for v in (f_low, proj_low)]
    tok_out, char_out, d_tok, d_char, d_merged, sums23, begin, end, *other = conv_call(
        f_low, proj_low, normal1, proj, norms, low, high, third,
        tok_grad.reshape(total, width), char_grad.reshape(total, width), seqs, other,
    )

    joined_edges = [low, high, swap(low, "seq", 0), swap(high, "seq", 0)]
    low, high = neighbours(begin, end)
    other_dm = swap(d_merged, "seq", 0)

    def onward(state, first_link):
        for link in range(first_link + 1, bits):
            ((values,), _) = together([split(state)])
            state = send_links(paired(values), link)
        return state

    def columns_of(begin, blocks, out):
        return [
            (begin + j * blk, blk, out, (slice(None), slice(j * width, (j + 1) * width)))
            for j in range(blocks)
        ]

    everything = (slice(None), slice(None))
    double = 2 * blk
    batch_bits = lax.axis_size("batch").bit_length() - 1
    unit = 8 * lax.axis_size("batch")
    height = max(2 * blk + table_rows, 3 * blk + SMALL_ROWS)
    height += -height % unit
    d_proj, d_ffn, sums1 = conv_back_call(
        d_merged, low, high, third, d_tok, d_char, normal1, rstd1, norms, seqs
    )
    conv_state = conv_weight_call(
        order, (f_low, proj_low), other, d_merged, other_dm, joined_edges, count
    )
    conv_state = send_links(conv_state, 1)
    ds, back_totals = states_back_call(
        d_proj, first, at_char, lens, starts[:, None, :], ends[:, None, :], z
    )
    send, keep, d_bias_up, d_attn, sums0, d_mix = ffn_back_call(
        slot, order, d_ffn, active, slope, normed, normal0, rstd0, norms, first, at_out, at_up,
        at_down, back_totals, mix_t, pooled, d_proj, seqs,
    )
    d_mix = lax.all_to_all(d_mix, "seq", 0, 0, tiled=True)
    ffn_came = [swap(piece, "seq", 0) for piece in send]
    conv_state = onward(conv_state, 1)
    ffn_state = fold(keep, ffn_came)
    ffn_state = send_links(ffn_state, 1)
    d_qkv = attend_back_call(qkv, d_mix, totals, step)
    PLACED.clear()
    d_qkv = lax.all_to_all(d_qkv, "seq", 0, 0, tiled=True)
    ((halves,), _) = together([cross(place, conv_state)])
    conv_run = Steps(
        across_halves(
            place, *halves,
            [
                (
                    r * double, double, 0,
                    (r // 2, slice(None), slice(r % 2 * width, (r % 2 + 1) * width)),
                )
                for r in range(6)
            ],
            [(3, double, 2 * width)],
        )
    )
    sums, d_bias = gates_back_call(
        me_one, group_ids, z, c, prior, ds, gathered, d_mix, char_ids,
        count * table_rows // NCHAR, 2,
    )
    ffn_state = onward(ffn_state, 1)
    for _ in range(1, batch_bits):
        advance(conv_run)
    rest_send, rest_keep = rest_call(order, first, at_table, at_gru, sums, height)
    hidden_grad, qkv_send, qkv_keep = qkv_back_call(
        order, d_qkv, rows, first, at_qkv, d_attn,
        [sums0, sums1, sums23, d_bias, d_bias_up], seqs, height,
    )
    PLACED.clear()
    (halves, (held,)), (rest_send, qkv_send) = together(
        [cross(place, ffn_state), conv_run.plan], [rest_send, qkv_send]
    )
    conv_run.resume([held])
    ffn_run = Steps(
        across_halves(
            place, *halves,
            [
                (0, share, 0, everything),
                *columns_of(share, 4, 1),
                (share + 4 * blk, blk, 2, everything),
                (share + 5 * blk, blk, 3, everything),
            ],
            [(share, width), (blk, 4 * width), (blk, width), (blk, width)],
        )
    )
    rest_came, qkv_came = (swap(send, "seq", 0) for send in (rest_send, qkv_send))
    ((values,), _) = together([split([[rest_keep, rest_came], [qkv_keep, qkv_came]])])
    last_run = Steps(
        across_direct(
            place, me_one, send_links(paired(values), 1),
            [
                *columns_of(0, 2, 0),
                (2 * blk, table_rows, 1, everything),
                *columns_of(height, 3, 2),
            ],
            height + 3 * blk,
            [
                (blk, 2 * width), (table_rows, width), (blk, 3 * width),
                (4, blk), (4, blk), (1, blk), (1, blk), (1, share),
            ],
        )
    )
    advance(conv_run, ffn_run, last_run)
    advance(ffn_run, last_run)
    while conv_run.plan or ffn_run.plan or last_run.plan:
        advance(conv_run, ffn_run, last_run)
    (conv_grad,) = conv_run.result
    down_grad, up_grad, out_grad, char_grad_w = ffn_run.result
    gru_grad, table_grad, qkv_grad, *small_grads = last_run.result
    d_gain, d_shift = (v.T for v in small_grads[:2])
    d_gate_b, d_cand_b, d_ffn_b = (v.reshape(-1) for v in small_grads[2:])
    shape_out = (seqs, toks, width)
    return (
        tok_out.reshape(shape_out),
        char_out.reshape(shape_out),
        hidden_grad.reshape(shape_out),
        qkv_grad,
        out_grad,
        up_grad,
        d_ffn_b,
        down_grad,
        gru_grad,
        d_gate_b,
        d_cand_b,
        char_grad_w,
        conv_grad,
        table_grad,
        d_gain,
        d_shift,
    )


def solution(mesh):
    rows, columns = P("seq", None), P("batch", "seq", None)
    return jax.shard_map(
        local,
        mesh=mesh,
        in_specs=(
            columns, P("batch", "seq"), P("batch"), columns, rows, rows, rows, P("seq"), rows,
            rows, P("seq"), P("seq"), rows, P(None, "seq", None), rows, rows, rows, columns,
            columns,
        ),
        out_specs=(
            columns, columns, columns, rows, rows, rows, P("seq"), rows, rows, P("seq"), P("seq"),
            rows, P(None, "seq", None), rows, rows, rows,
        ),
        check_vma=False,
    )
```

```python
import functools
import math

import jax
import jax.numpy as jnp
from jax import lax
from jax.experimental import pallas as pl
from jax.experimental.pallas import tpu as pltpu
from jax.sharding import PartitionSpec as P

HEADS = 12
NCHAR = 256
NORM_EPS = 1e-06
LANES = 128
SMALL_ROWS = 16
RIDE = 32
SCALE = 1000
F32 = jnp.float32
BF16 = jnp.bfloat16
VMEM_BYTES = 44 << 20
VMEM_MARGIN = 9 << 20


def dot(left, right, left_dim, right_dim):
    return lax.dot_general(
        left, right, (((left_dim,), (right_dim,)), ((), ())), preferred_element_type=F32
    )


def padded_bytes(dims, dtype):
    size = jnp.dtype(dtype).itemsize
    dims = (1, 1, *dims)
    rows = -(-dims[-2] * size // 32) * 32
    lanes = -(-dims[-1] // LANES) * LANES
    return math.prod(dims[:-2]) * rows * lanes


def params(grid_rank, blocks, scratch):
    need = sum(2 * padded_bytes(spec.block_shape, value.dtype) for spec, value in blocks)
    need += sum(padded_bytes(ref.shape, ref.dtype) for ref in scratch)
    return pltpu.CompilerParams(
        dimension_semantics=("arbitrary",) * grid_rank,
        vmem_limit_bytes=min(VMEM_BYTES, need + VMEM_MARGIN),
    )


def shape(dims, dtype):
    return jax.ShapeDtypeStruct(dims, dtype)


def stored(dims, dtype):
    return pltpu.HBM(dims, dtype) if PLACED else shape(dims, dtype)


def whole(dims):
    return pl.BlockSpec(dims, lambda *_: (0,) * len(dims))


def cost(flops, nbytes):
    return pl.CostEstimate(flops=int(flops) * SCALE, bytes_accessed=int(nbytes) * SCALE, transcendentals=0)


NEAR = []
LATEST = []
PLACED = []
TOKEN = jax.ShapeDtypeStruct((8, LANES), F32)


def launch(
    body, grid, prefetch, inputs, in_specs, out_specs, out_shape, scratch, price, name, carry=()
):
    deps = [pltpu.with_memory_space_constraint(v, pltpu.HBM) for v in LATEST]
    single = not isinstance(out_shape, (list, tuple))
    outs = [out_shape] if single else list(out_shape)
    specs = [out_specs] if single else list(out_specs)
    lead = len(prefetch) + len(inputs)
    extra = len(carry) + len(deps)
    anywhere = pl.BlockSpec(memory_space=pl.ANY)

    def kernel(*refs):
        own = refs[lead + extra :]
        body(*refs[:lead], *own[: len(outs)], *own[len(outs) + len(carry) + 1 :])

    inputs = [
        v
        if not PLACED or v.size < 1 << 16 or any(v is near for near in NEAR)
        else pltpu.with_memory_space_constraint(v, pltpu.HBM)
        for v in inputs
    ]
    results = pl.pallas_call(
        kernel,
        grid_spec=pltpu.PrefetchScalarGridSpec(
            num_scalar_prefetch=len(prefetch),
            grid=grid,
            in_specs=list(in_specs) + [anywhere] * extra,
            out_specs=specs + [anywhere] * (len(carry) + 1),
            scratch_shapes=scratch,
        ),
        out_shape=outs + [stored(v.shape, v.dtype) for v in (*carry, TOKEN)],
        input_output_aliases={lead + i: len(outs) + i for i in range(len(carry))},
        compiler_params=params(
            len(grid), [*zip(in_specs, inputs), *zip(specs, outs)], scratch
        ),
        cost_estimate=price,
        name=name,
    )(*prefetch, *inputs, *carry, *deps)
    NEAR.extend(v for v, out in zip(results, outs) if isinstance(out, jax.ShapeDtypeStruct))
    *results, LATEST[:] = *results[:-1], results[-1:]
    return results[0] if len(results) == 1 else results


def plan(body, grid, prefetch, inputs, in_specs, out_specs, out_shape, scratch, price, name):
    listed = isinstance(out_shape, (list, tuple))
    outs = (list(out_specs), list(out_shape)) if listed else ([out_specs], [out_shape])
    return body, grid, prefetch, inputs, in_specs, *outs, scratch, price, name


def together(plans, carry=()):
    bodies, grids, prefetch, inputs, in_specs, out_specs, outs, scratch, prices, names = zip(*plans)
    assert len(set(grids)) == 1
    groups = (prefetch, inputs, outs, scratch)

    def body(*refs):
        own = [[] for _ in plans]
        for group in groups:
            for refs_of, part in zip(own, group):
                refs_of.extend(refs[: len(part)])
                refs = refs[len(part) :]
        for one, refs_of in zip(bodies, own):
            one(*refs_of)

    def flat(parts):
        return [v for part in parts for v in part]

    price = pl.CostEstimate(
        flops=sum(v.flops for v in prices),
        bytes_accessed=sum(v.bytes_accessed for v in prices),
        transcendentals=0,
    )
    results = launch(
        body, grids[0], flat(prefetch), flat(inputs), flat(in_specs), flat(out_specs), flat(outs),
        flat(scratch), price, "_".join(names), carry,
    )
    results = list(results) if isinstance(results, (list, tuple)) else [results]
    found = []
    for part in outs:
        found.append(results[: len(part)])
        results = results[len(part) :]
    return found, results


class Steps:
    def __init__(self, plans):
        self.plans, self.result = plans, None
        self.plan = next(plans)

    def resume(self, values):
        try:
            self.plan = self.plans.send(values)
        except StopIteration as end:
            self.plan, self.result = None, end.value


def advance(*runs, carry=()):
    live = [run for run in runs if run.plan]
    found, carried = together([run.plan for run in live], carry)
    for run, values in zip(live, found):
        run.resume(values)
    return carried


def flat_block(ref):
    block = ref[...]
    return block.reshape(block.shape[0] * block.shape[1], block.shape[2])


def norm_forward(values):
    center = values - jnp.mean(values, -1, keepdims=True)
    rstd = lax.rsqrt(jnp.mean(center * center, -1, keepdims=True) + NORM_EPS)
    return center * rstd, rstd


def norm_backward(normal, rstd, gain, gradient):
    scaled = gradient * gain
    first = jnp.mean(scaled, -1, keepdims=True)
    second = jnp.mean(scaled * normal, -1, keepdims=True)
    return rstd * (scaled - first - normal * second)


def column_sum(values):
    return jnp.sum(values, 0, keepdims=True)


def gelu_parts(values):
    size = jnp.abs(values) * 0.7071067811865476
    bell = jnp.exp(-size * size)
    t = 1.0 / (1.0 + 0.3275911 * size)
    series = t * (
        0.254829592
        + t * (-0.284496736 + t * (1.421413741 + t * (-1.453152027 + t * 1.061405429)))
    )
    tail = 0.5 * series * bell
    phi_sum = jnp.where(values < 0, tail, 1.0 - tail)
    return values * phi_sum, phi_sum + values * (bell * 0.3989422804014327)


def qkv_kernel(seqs, toks, per, x_ref, w_ref, o_ref):
    acc = dot(x_ref[...], flat_block(w_ref), 1, 0)
    turned = acc.T.astype(BF16)
    width = turned.shape[0] // HEADS
    for s in range(seqs):
        for h in range(HEADS):
            pair = s * HEADS + h
            o_ref[pair // per, pair % per, 0] = turned[
                h * width : (h + 1) * width, s * toks : (s + 1) * toks
            ]


def qkv_call(rows, packed, base, seqs, count):
    total, width = rows.shape
    toks = total // seqs
    per = seqs * HEADS // count
    head = width // HEADS
    blk = width // count
    return launch(
        functools.partial(qkv_kernel, seqs, toks, per),
        (3,),
        [],
        [rows, packed],
        [ whole(rows.shape), pl.BlockSpec((count, blk, width), lambda j: (0, base + j, 0)), ],
        pl.BlockSpec((count, per, 1, head, toks), lambda j: (0, 0, j, 0, 0)),
        stored((count, per, 3, head, toks), BF16),
        [],
        cost(6 * total * width * width, 6 * width * width + 8 * total * width),
        "qkv",
    )


def spread(ref, index):
    return jnp.concatenate([ref[(i, *index)] for i in range(ref.shape[0])], axis=1)


def attend_kernel(step, scale, x_ref, o_ref, total_ref):
    queries = spread(x_ref, (0, 0)) * scale
    keys = spread(x_ref, (0, 1)).T
    values = spread(x_ref, (0, 2))
    toks = x_ref.shape[-1]
    for begin in range(0, queries.shape[1], step):
        scores = dot(keys, queries[:, begin : begin + step], 1, 0)
        highest = jnp.max(scores, 0, keepdims=True)
        expo = jnp.exp(scores - highest)
        totals = jnp.sum(expo, 0, keepdims=True)
        mixture = (dot(values, expo.astype(BF16), 1, 0) / totals).astype(BF16)
        total_ref[0, :, begin : begin + step] = highest + jnp.log(totals)
        for at in range(0, step, toks):
            o_ref[(begin + at) // toks, 0] = mixture[:, at : at + toks]


def attend_call(qkv, step):
    count, per, _, head, toks = qkv.shape
    length = count * toks
    scale = head**-0.5
    return launch(
        functools.partial(attend_kernel, step, scale),
        (per,),
        [],
        [qkv],
        [pl.BlockSpec((count, 1, 3, head, toks), lambda p: (0, p, 0, 0, 0))],
        [ pl.BlockSpec((count, 1, head, toks), lambda p: (0, p, 0, 0)), pl.BlockSpec((1, 1, length), lambda p: (p, 0, 0)), ],
        [stored((count, per, head, toks), BF16), shape((per, 1, length), F32)],
        [],
        cost(16 * per * length * length * head, 8 * per * length * head),
        "attend",
    )


def attend_back_kernel(step, scale, x_ref, g_ref, total_ref, o_ref):
    queries = spread(x_ref, (0, 0)) * scale
    keys_t = spread(x_ref, (0, 1))
    keys = keys_t.T
    values = spread(x_ref, (0, 2)).T
    grads = spread(g_ref, ())
    toks = x_ref.shape[-1]
    length = queries.shape[1]
    d_keys = jnp.zeros(queries.shape, F32)
    d_values = jnp.zeros(queries.shape, F32)
    for begin in range(0, length, step):
        query = queries[:, begin : begin + step]
        grad = grads[:, begin : begin + step]
        scores = dot(keys, query, 1, 0)
        probability = jnp.exp(scores - total_ref[0, :, begin : begin + step])
        d_prob = dot(values, grad, 1, 0)
        centered = jnp.sum(probability * d_prob, 0, keepdims=True)
        d_scores = (probability * (d_prob - centered)).astype(BF16)
        d_values += dot(grad, probability.astype(BF16), 1, 1)
        d_keys += dot(query, d_scores, 1, 1)
        d_query = (dot(keys_t, d_scores, 1, 0) * scale).astype(BF16)
        for at in range(0, step, toks):
            o_ref[(begin + at) // toks, 0, 0] = d_query[:, at : at + toks]
    d_keys = d_keys.astype(BF16)
    d_values = d_values.astype(BF16)
    for i in range(length // toks):
        o_ref[i, 0, 1] = d_keys[:, i * toks : (i + 1) * toks]
        o_ref[i, 0, 2] = d_values[:, i * toks : (i + 1) * toks]


def attend_back_call(qkv, grads, totals, step):
    count, per, _, head, toks = qkv.shape
    length = count * toks
    scale = head**-0.5
    return launch(
        functools.partial(attend_back_kernel, step, scale),
        (per,),
        [],
        [qkv, grads, totals],
        [ pl.BlockSpec((count, 1, 3, head, toks), lambda p: (0, p, 0, 0, 0)), pl.BlockSpec((count, head, toks), lambda p: (0, p, 0)), pl.BlockSpec((1, 1, length), lambda p: (p, 0, 0)), ],
        pl.BlockSpec((count, 1, 3, head, toks), lambda p: (0, p, 0, 0, 0)),
        stored(qkv.shape, BF16),
        [],
        cost(40 * per * length * length * head, 14 * per * length * head),
        "attend_back",
    )


def ffn_kernel(
    seqs,
    o_ref,
    x_ref,
    w_out_ref,
    w_up_ref,
    w_down_ref,
    bias_ref,
    norms_ref,
    mix_ref,
    normal0_ref,
    rstd0_ref,
    a_ref,
    g_ref,
    slope_ref,
    normal1_ref,
    rstd1_ref,
    f_ref,
    acc_ref,
):
    j = pl.program_id(0)
    per = o_ref.shape[1]
    head, toks = o_ref.shape[2:]

    @pl.when(j == 0)
    def _():
        for s in range(seqs):
            for h in range(HEADS):
                pair = s * HEADS + h
                mix_ref[h * head : (h + 1) * head, s * toks : (s + 1) * toks] = o_ref[
                    pair // per, pair % per
                ]
        attended = dot(mix_ref[...].T, flat_block(w_out_ref), 1, 0)
        normal, rstd = norm_forward(x_ref[...].astype(F32) + attended)
        normal0_ref[...] = normal
        rstd0_ref[...] = rstd
        normed = normal * norms_ref[0:1] + norms_ref[4:5]
        a_ref[...] = normed.astype(BF16)
        acc_ref[...] = normed

    up = dot(a_ref[...], flat_block(w_up_ref), 1, 0) + bias_ref[...]
    active, slope = gelu_parts(up)
    active = active.astype(BF16)
    g_ref[...] = active
    slope_ref[...] = slope
    acc_ref[...] += dot(active, flat_block(w_down_ref), 1, 0)

    @pl.when(j == pl.num_programs(0) - 1)
    def _():
        normal, rstd = norm_forward(acc_ref[...])
        normal1_ref[...] = normal
        rstd1_ref[...] = rstd
        f_ref[...] = (normal * norms_ref[1:2] + norms_ref[5:6]).astype(BF16)


def ffn_call(mixture, rows, packed, at_out, at_up, at_down, bias, norms, seqs):
    count, per, head, toks = mixture.shape
    total, width = rows.shape
    hidden = bias.shape[1]
    chunks = hidden // width
    blk = width // count
    owners = count // chunks
    return launch(
        functools.partial(ffn_kernel, seqs),
        (chunks,),
        [],
        [mixture, rows, packed, packed, packed, bias, norms],
        [ whole(mixture.shape), whole(rows.shape), pl.BlockSpec((count, blk, width), lambda j: (0, at_out, 0)), pl.BlockSpec((count, blk, width), lambda j: (0, at_up + j, 0)), pl.BlockSpec((owners, hidden // count, width), lambda j: (j, at_down, 0)), pl.BlockSpec((1, width), lambda j: (0, j)), whole(norms.shape), ],
        [ whole((width, total)), whole((total, width)), whole((total, 1)), whole((total, width)), pl.BlockSpec((total, width), lambda j: (0, j)), pl.BlockSpec((total, width), lambda j: (0, j)), whole((total, width)), whole((total, 1)), whole((total, width)), ],
        [ stored((width, total), BF16), stored((total, width), F32), stored((total, 1), F32), stored((total, width), BF16), stored((total, hidden), BF16), stored((total, hidden), F32), shape((total, width), F32), shape((total, 1), F32), shape((total, width), BF16)],
        [pltpu.VMEM((total, width), F32)],
        cost( 2 * total * width * (width + 2 * hidden), 4 * hidden * width + 10 * total * hidden ),
        "ffn",
    )


def ffn_back_kernel(
    seqs,
    slot_ref,
    order_ref,
    d_ref,
    g_ref,
    slope_ref,
    a_ref,
    normal_ref,
    rstd_ref,
    norms_ref,
    w_out_ref,
    w_up_ref,
    w_down_ref,
    total_ref,
    mix_ref,
    pooled_ref,
    d_proj_ref,
    *refs,
):
    j = pl.program_id(0)
    count, blk, width = w_up_ref.shape
    owners, share, _ = w_down_ref.shape
    half = count // 2
    send_refs, refs = refs[:half], refs[half:]
    keep_ref, bias_ref, d_attn_ref, sums_ref, d_mix_ref = refs[:5]
    db_ref, at_ref, acc_ref, part_ref, down_ref = refs[5:]

    @pl.when(j == 0)
    def _():
        db_ref[...] = d_ref[...].astype(BF16)
        at_ref[...] = a_ref[...].T
        acc_ref[...] = d_ref[...]

    part_ref[...] = dot(g_ref[...].T, db_ref[...], 1, 0)
    for i in range(owners):
        slot = slot_ref[j * owners + i]
        down_ref[slot] = part_ref[i * share : (i + 1) * share, :].astype(BF16)

    d_up = (dot(db_ref[...], flat_block(w_down_ref), 1, 1) * slope_ref[...]).astype(BF16)
    bias_ref[...] = column_sum(d_up.astype(F32))
    part_ref[...] = dot(at_ref[...], d_up, 1, 0)
    place = pl.ds(pl.multiple_of(share + j * blk, 16), blk)
    for pos in range(count):
        piece = part_ref[pl.ds(pl.multiple_of(order_ref[pos] * blk, 16), blk), :].astype(BF16)
        if pos < half:
            keep_ref[pos, place, :] = piece
        else:
            send_refs[pos - half][place, :] = piece
    acc_ref[...] += dot(d_up, flat_block(w_up_ref), 1, 1)

    @pl.when(j == pl.num_programs(0) - 1)
    def _():
        for pos in range(half):
            keep_ref[pos, 0:share, :] = down_ref[pos]
            send_refs[pos][0:share, :] = down_ref[half + pos]
        gradient = acc_ref[...]
        normal = normal_ref[...]
        sums_ref[0:1, :] = column_sum(gradient * normal)
        sums_ref[1:2, :] = column_sum(gradient)
        d_sum = norm_backward(normal, rstd_ref[...], norms_ref[0:1], gradient)
        d_attn_ref[...] = d_sum
        low = d_sum.astype(BF16)

        def put(row):
            for pos in range(count):
                start = pl.multiple_of(order_ref[pos] * blk, 16)
                piece = part_ref[pl.ds(start, blk), :].astype(BF16)
                if pos < half:
                    keep_ref[pos, row : row + blk, :] = piece
                else:
                    send_refs[pos - half][row : row + blk, :] = piece

        base = keep_ref.shape[1] - 2 * blk
        part_ref[...] = dot(mix_ref[...], low, 1, 0)
        put(base)
        part_ref[...] = dot(pooled_ref[...].T, d_proj_ref[...], 1, 0)
        put(base + blk)
        turned = dot(flat_block(w_out_ref), low, 1, 1).astype(BF16)
        per = seqs * HEADS // count
        head, toks = width // HEADS, d_mix_ref.shape[2]
        for s in range(seqs):
            for h in range(HEADS):
                pair = s * HEADS + h
                row = pair % per * head
                d_mix_ref[pair // per, row : row + head] = turned[
                    h * head : (h + 1) * head, s * toks : (s + 1) * toks
                ]
        rest = jnp.concatenate([total_ref[j] for j in range(total_ref.shape[0])], 0)
        rest = jnp.concatenate([rest, jnp.zeros((RIDE - rest.shape[0], LANES), F32)], 0)
        for part in range(3):
            low = rest.astype(BF16)
            rest = rest - low.astype(F32)
            row = per * head + part * RIDE
            for device in range(count):
                d_mix_ref[device, row : row + RIDE] = low


def ffn_back_call(
    slot, order, d_ffn, active, slope, normed, normal, rstd, norms, packed, at_out, at_up, at_down, totals, mixture, pooled, d_proj, seqs):
    total, width = d_ffn.shape
    hidden = active.shape[1]
    count = packed.shape[0]
    chunks = hidden // width
    blk = width // count
    share = hidden // count
    owners = count // chunks
    per = seqs * HEADS // count
    head = width // HEADS
    toks = total // seqs
    rows_out = share + (chunks + 2) * blk
    wide = pl.BlockSpec((total, width), lambda j, *_: (0, j))
    results = launch(
        functools.partial(ffn_back_kernel, seqs),
        (chunks,),
        [slot, order],
        [d_ffn, active, slope, normed, normal, rstd, norms, packed, packed, packed, totals, mixture, pooled, d_proj],
        [ whole(d_ffn.shape), wide, wide, whole(normed.shape), whole(normal.shape), whole(rstd.shape), whole(norms.shape), pl.BlockSpec((count, blk, width), lambda j, *_: (0, at_out, 0)), pl.BlockSpec((count, blk, width), lambda j, *_: (0, at_up + j, 0)), pl.BlockSpec((owners, share, width), lambda j, *_: (j, at_down, 0)), whole(totals.shape), whole(mixture.shape), whole(pooled.shape), whole(d_proj.shape), ],
        [ *[whole((rows_out, width))] * (count // 2), whole((count // 2, rows_out, width)), pl.BlockSpec((1, width), lambda j, *_: (0, j)), whole((total, width)), whole((2, width)), whole((count, per * head + 3 * RIDE, toks)), ],
        [ *[stored((rows_out, width), BF16)] * (count // 2), stored((count // 2, rows_out, width), BF16), stored((1, hidden), F32), stored((total, width), F32), stored((2, width), F32), stored((count, per * head + 3 * RIDE, toks), BF16), ],
        [ pltpu.VMEM((total, width), BF16), pltpu.VMEM((width, total), BF16), pltpu.VMEM((total, width), F32), pltpu.VMEM((width, width), F32), pltpu.VMEM((count, share, width), BF16), ],
        cost( 8 * total * width * hidden + 2 * total * width * width, 8 * hidden * width + 10 * total * hidden, ),
        "ffn_back",
    )
    return results[: count // 2], *results[count // 2 :]


def gates_kernel(
    seqs, groups_ref, ids_ref, back_ids_ref, table_ref, w_fwd_ref, w_rev_ref, bias_ref,
    z_ref, c_ref, totals_ref,
):
    s = pl.program_id(0)
    steps = ids_ref.shape[1]
    rows = 2 * seqs
    table = flat_block(table_ref)
    vocabulary = lax.broadcasted_iota(jnp.int32, (steps, NCHAR), 1)
    chunks = z_ref.shape[0]
    half = chunks * LANES
    for direction, (source, weight) in enumerate(((ids_ref, w_fwd_ref), (back_ids_ref, w_rev_ref))):
        onehot = jnp.where(source[0] == vocabulary, 1.0, 0.0).astype(BF16)
        embedded = dot(onehot, table, 1, 0).astype(BF16)
        gate_input = dot(embedded, flat_block(weight), 1, 0)
        own = slice(direction * half, (direction + 1) * half)
        update = jax.nn.sigmoid(gate_input[:, :half] + bias_ref[8:9, own])
        candidate = jnp.tanh(gate_input[:, half:] + bias_ref[9:10, own])
        place = pl.ds(s + direction * seqs, steps, stride=rows)
        for j in range(chunks):
            z_ref[j, place, :] = update[:, j * LANES : (j + 1) * LANES]
            c_ref[j, place, :] = candidate[:, j * LANES : (j + 1) * LANES]

    @pl.when(s == pl.num_programs(0) - 1)
    def _():
        def one(t, carry):
            states, products = carry
            place = pl.ds(pl.multiple_of(t * rows, rows), rows)
            new_states, new_products = [], []
            for j in range(chunks):
                update = z_ref[j, place, :]
                decay = 1.0 - update
                new_states.append(decay * states[j] + update * c_ref[j, place, :])
                new_products.append(products[j] * decay)
            return tuple(new_states), tuple(new_products)

        zero = jnp.zeros((rows, LANES), F32)
        states, products = lax.fori_loop(
            0, steps, one, ((zero,) * chunks, (zero + 1.0,) * chunks), unroll=8
        )
        for j in range(chunks):
            totals_ref[0, j] = products[j]
            totals_ref[1, j] = states[j]


def gates_call(groups, ids, packed, at_gru, at_table, bias):
    seqs, steps = ids.shape
    count, _, width = packed.shape
    blk = width // count
    table_rows = 4 * NCHAR // count
    per_group = NCHAR // table_rows
    chunks = width // 2 // LANES
    laid = (chunks, steps * 2 * seqs, LANES)
    return launch(
        functools.partial(gates_kernel, seqs),
        (seqs,),
        [groups],
        [ids[..., None], ids[:, ::-1, None], packed, packed, packed, bias],
        [ pl.BlockSpec((1, steps, 1), lambda s, g: (s, 0, 0)), pl.BlockSpec((1, steps, 1), lambda s, g: (s, 0, 0)), pl.BlockSpec((per_group, table_rows, width), lambda s, g: (g[s], at_table, 0)), pl.BlockSpec((count, blk, width), lambda s, g: (0, at_gru, 0)), pl.BlockSpec((count, blk, width), lambda s, g: (0, at_gru + 1, 0)), whole(bias.shape), ],
        [whole(laid), whole(laid), whole((2, chunks, 2 * seqs, LANES))],
        [stored(laid, F32), stored(laid, F32), stored((2, chunks, 2 * seqs, LANES), F32)],
        [],
        cost( 2 * seqs * steps * width * (2 * NCHAR + 2 * width), 16 * seqs * steps * width ),
        "gates",
    )


def entry_state(me, totals, products, rows, seqs, forward):
    count, chunks = products.shape[0], products.shape[1]
    first = lax.broadcasted_iota(jnp.int32, (rows, LANES), 0) < seqs
    result = []
    for j in range(chunks):
        state = jnp.zeros((rows, LANES), F32)
        for lap in range(count):
            up, down = lap, count - 1 - lap
            one, other = (up, down) if forward else (down, up)
            product = jnp.where(first, products[one, j], products[other, j])
            total = jnp.where(first, totals[one, j], totals[other, j])
            up_in, down_in = (up < me).astype(F32), (down > me).astype(F32)
            ahead = jnp.where(first, up_in, down_in) if forward else jnp.where(first, down_in, up_in)
            state = jnp.where(ahead > 0.5, product * state + total, state)
        result.append(state)
    return result


def states_kernel(
    seqs, me_ref, z_ref, c_ref, all_ref, starts_ref, ends_ref, lens_ref, w_ref,
    prior_ref, pooled_ref, proj_ref, proj_low_ref, hold_ref, state_ref, acc_ref,
):
    i = pl.program_id(0)
    last = pl.num_programs(0) - 1
    rows = 2 * seqs
    chunks = z_ref.shape[0]
    span = z_ref.shape[1] // rows
    toks = starts_ref.shape[1]
    half = chunks * LANES

    @pl.when(i == 0)
    def _():
        entry = entry_state(me_ref[0], all_ref[:, 1], all_ref[:, 0], rows, seqs, True)
        for j in range(chunks):
            state_ref[j] = entry[j]
        acc_ref[...] = jnp.zeros_like(acc_ref)

    def one(t, states):
        place = pl.ds(pl.multiple_of(t * rows, rows), rows)
        result = []
        for j in range(chunks):
            prior_ref[j, place, :] = states[j]
            update = z_ref[j, place, :]
            state = (1.0 - update) * states[j] + update * c_ref[j, place, :]
            hold_ref[j, place, :] = state
            result.append(state)
        return tuple(result)

    states = lax.fori_loop(0, span, one, tuple(state_ref[j] for j in range(chunks)), unroll=8)
    for j in range(chunks):
        state_ref[j] = states[j]
    count = lax.broadcasted_iota(jnp.int32, (toks, span), 1) + i * span
    for direction in range(2):
        place_of = count if direction == 0 else (last + 1) * span - 1 - count
        for s in range(seqs):
            member = jnp.where(
                (place_of >= starts_ref[s]) & (place_of < ends_ref[s]), 1.0, 0.0
            ).astype(BF16)
            held = jnp.concatenate(
                [
                    hold_ref[j, pl.ds(s + direction * seqs, span, stride=rows), :]
                    for j in range(chunks)
                ],
                axis=1,
            ).astype(BF16)
            acc_ref[s * toks : (s + 1) * toks, direction * half : (direction + 1) * half] += dot(
                member, held, 1, 0
            )

    @pl.when(i == last)
    def _():
        for s in range(seqs):
            rows_of = slice(s * toks, (s + 1) * toks)
            pooled_ref[rows_of, :] = (acc_ref[rows_of, :] / lens_ref[s]).astype(BF16)
        proj = dot(pooled_ref[...], flat_block(w_ref), 1, 0)
        proj_ref[...] = proj
        proj_low_ref[...] = proj.astype(BF16)


def collect_kernel(me_ref, *refs):
    for mask, ref in enumerate(refs[:-1]):
        refs[-1][me_ref[0] ^ mask] = ref[...]


def collect(me, parts):
    out = (len(parts), *parts[0].shape)
    return launch(
        collect_kernel,
        (1,),
        [me],
        parts,
        [whole(v.shape) for v in parts],
        whole(out),
        shape(out, parts[0].dtype),
        [],
        cost(0, 8 * len(parts) * parts[0].size),
        "collect",
    )


def states_call(me, z, c, gathered, starts, ends, lens, packed, at_char, parts):
    chunks, length, _ = z.shape
    seqs, toks, _ = starts.shape
    count, _, width = packed.shape
    blk = width // count
    span = length // parts
    total = seqs * toks
    stream = pl.BlockSpec((chunks, span, LANES), lambda i, *_: (0, i, 0))
    return launch(
        functools.partial(states_kernel, seqs),
        (parts,),
        [me],
        [z, c, gathered, starts, ends, lens, packed],
        [ stream, stream, whole(gathered.shape), whole(starts.shape), whole(ends.shape), whole(lens.shape), pl.BlockSpec((count, blk, width), lambda i, *_: (0, at_char, 0)), ],
        [stream] + [whole((total, width))] * 3,
        [stored(z.shape, F32), stored((total, width), BF16), stored((total, width), F32), shape((total, width), BF16), ],
        [ pltpu.VMEM((chunks, span, LANES), F32), pltpu.VMEM((chunks, 2 * seqs, LANES), F32), pltpu.VMEM((total, width), F32), ],
        cost(2 * total * width * (width + length // 8), 12 * chunks * length * LANES),
        "states",
    )


def states_back_kernel(
    seqs, d_ref, w_ref, lens_ref, starts_ref, ends_ref, z_ref, ds_ref, total_ref,
):
    rows = 2 * seqs
    chunks = z_ref.shape[0]
    steps = z_ref.shape[1] // rows
    toks = starts_ref.shape[2]
    half = chunks * LANES
    d_pooled = dot(d_ref[...], flat_block(w_ref), 1, 1)
    count = lax.broadcasted_iota(jnp.int32, (steps, toks), 0)
    for s in range(seqs):
        d_summed = (d_pooled[s * toks : (s + 1) * toks] / lens_ref[s]).astype(BF16)
        for direction in range(2):
            place_of = count if direction == 0 else steps - 1 - count
            member = jnp.where(
                (place_of >= starts_ref[s]) & (place_of < ends_ref[s]), 1.0, 0.0
            ).astype(BF16)
            d_states = dot(member, d_summed[:, direction * half : (direction + 1) * half], 1, 0)
            for j in range(chunks):
                ds_ref[j, pl.ds(s + direction * seqs, steps, stride=rows), :] = d_states[
                    :, j * LANES : (j + 1) * LANES
                ]

    def one(lap, carried):
        place = pl.ds(pl.multiple_of((steps - 1 - lap) * rows, rows), rows)
        return tuple(
            (1.0 - z_ref[j, place, :]) * (ds_ref[j, place, :] + carried[j]) for j in range(chunks)
        )

    zero = jnp.zeros((rows, LANES), F32)
    carried = lax.fori_loop(0, steps, one, (zero,) * chunks, unroll=8)
    for j in range(chunks):
        total_ref[j] = carried[j]


def states_back_call(d_proj, packed, at_char, lens, starts, ends, z):
    chunks, length, _ = z.shape
    seqs = starts.shape[0]
    count, _, width = packed.shape
    blk = width // count
    return launch(
        functools.partial(states_back_kernel, seqs),
        (1,),
        [],
        [d_proj, packed, lens, starts, ends, z],
        [ whole(d_proj.shape), pl.BlockSpec((count, blk, width), lambda i: (0, at_char, 0)), whole(lens.shape), whole(starts.shape), whole(ends.shape), whole(z.shape), ],
        [whole(z.shape), whole((chunks, 2 * seqs, LANES))],
        [stored(z.shape, F32), shape((chunks, 2 * seqs, LANES), F32)],
        [],
        cost( 2 * d_proj.shape[0] * width * (width + length // 8), 8 * chunks * length * LANES ),
        "states_back",
    )


def gates_back_kernel(
    seqs, me_ref, groups_ref, z_ref, c_ref, prior_ref, ds_ref, all_ref, back_ref, ids_ref,
    back_ids_ref, s_ref, bias_ref, du_ref, dc_ref, carried_ref, acc_ref,
):
    i = pl.program_id(0)
    rows = 2 * seqs
    chunks = z_ref.shape[0]
    span = z_ref.shape[1] // rows
    half = chunks * LANES

    @pl.when(i == 0)
    def _():
        parts = back_ref[...].astype(F32)
        summed = parts[:, :RIDE] + parts[:, RIDE : 2 * RIDE] + parts[:, 2 * RIDE :]
        totals = summed[:, : chunks * rows].reshape(-1, chunks, rows, LANES)
        entry = entry_state(me_ref[0], totals, all_ref[:, 0], rows, seqs, False)
        for j in range(chunks):
            carried_ref[j] = entry[j]
        acc_ref[...] = jnp.zeros_like(acc_ref)

    def one(lap, carried):
        place = pl.ds(pl.multiple_of((span - 1 - lap) * rows, rows), rows)
        result = []
        for j in range(chunks):
            update = z_ref[j, place, :]
            candidate = c_ref[j, place, :]
            total = ds_ref[j, place, :] + carried[j]
            decay = 1.0 - update
            gated = total * update
            du_ref[j, place, :] = gated * decay * (candidate - prior_ref[j, place, :])
            dc_ref[j, place, :] = gated * (1.0 - candidate * candidate)
            result.append(decay * total)
        return tuple(result)

    carried = lax.fori_loop(0, span, one, tuple(carried_ref[j] for j in range(chunks)), unroll=8)
    for j in range(chunks):
        carried_ref[j] = carried[j]
    vocabulary = lax.broadcasted_iota(jnp.int32, (NCHAR, span), 0)
    for direction in range(2):
        source = ids_ref if direction == 0 else back_ids_ref
        for s in range(seqs):
            place = pl.ds(s + direction * seqs, span, stride=rows)
            gradient = jnp.concatenate(
                [part[j, place, :] for part in (du_ref, dc_ref) for j in range(chunks)], axis=1
            ).astype(BF16)
            onehot = jnp.where(source[s] == vocabulary, 1.0, 0.0).astype(BF16)
            acc_ref[groups_ref[s], :, direction * 2 * half : (direction + 1) * 2 * half] += dot(
                onehot, gradient, 1, 0
            )

    @pl.when(i == pl.num_programs(0) - 1)
    def _():
        total = jnp.zeros((1, 4 * half), F32)
        for g in range(acc_ref.shape[0]):
            total += column_sum(acc_ref[g])
            s_ref[g] = acc_ref[g].astype(BF16)
        bias_ref[...] = total


def gates_back_call(me, groups, z, c, prior, ds, gathered, gathered_back, ids, n_groups, parts):
    chunks, length, _ = z.shape
    seqs, steps = ids.shape
    span = length // parts
    width = 2 * chunks * LANES
    stream = pl.BlockSpec((chunks, span, LANES), lambda i, *_: (0, parts - 1 - i, 0))
    lanes = pl.BlockSpec((seqs, 1, steps // parts), lambda i, *_: (0, 0, parts - 1 - i))
    return launch(
        functools.partial(gates_back_kernel, seqs),
        (parts,),
        [me, groups],
        [z, c, prior, ds, gathered, gathered_back, ids[:, None, :], ids[:, None, ::-1]],
        [stream] * 4 + [whole(gathered.shape), pl.BlockSpec((gathered_back.shape[0], 3 * RIDE, LANES), lambda i, *_: (0, gathered_back.shape[1] // (3 * RIDE) - 1, 0)), lanes, lanes],
        [whole((n_groups, NCHAR, 2 * width)), whole((1, 2 * width))],
        [shape((n_groups, NCHAR, 2 * width), BF16), shape((1, 2 * width), F32)],
        [ pltpu.VMEM((chunks, span, LANES), F32), pltpu.VMEM((chunks, span, LANES), F32), pltpu.VMEM((chunks, 2 * seqs, LANES), F32), pltpu.VMEM((n_groups, NCHAR, 2 * width), F32), ],
        cost(4 * seqs * steps * NCHAR * width, 16 * chunks * length * LANES),
        "gates_back",
    )


def shifted(values, toks, low, high):
    total = values.shape[0]
    row = lax.broadcasted_iota(jnp.int32, (total, 1), 0)
    before = pltpu.roll(values, 1, 0)
    after = pltpu.roll(values, total - 1, 0)
    for s in range(total // toks):
        before = jnp.where(row == s * toks, low[s], before)
        after = jnp.where(row == (s + 1) * toks - 1, high[s], after)
    return before.astype(BF16), after.astype(BF16)


def conv_kernel(
    toks, f_ref, p_ref, normal_ref, proj_ref, norms_ref, low_ref, high_ref, w_ref, tok_g_ref,
    char_g_ref, tok_ref, char_ref, d_tok_ref, d_char_ref, dm_ref, sums_ref, begin_ref, end_ref,
    acc_ref, x_ref,
):
    half, k = pl.program_id(0), pl.program_id(1)
    width = f_ref.shape[1]

    @pl.when((half == 0) & (k == 0))
    def _():
        for part, source in enumerate((f_ref, p_ref)):
            columns = slice(part * width, (part + 1) * width)
            before, after = shifted(
                source[...].astype(F32),
                toks,
                low_ref[:, :, columns].astype(F32),
                high_ref[:, :, columns].astype(F32),
            )
            x_ref[0, :, columns] = before
            x_ref[1, :, columns] = source[...]
            x_ref[2, :, columns] = after

    product = dot(x_ref[k], flat_block(w_ref), 1, 0)

    @pl.when(k == 0)
    def _():
        acc_ref[...] = product

    @pl.when(k > 0)
    def _():
        acc_ref[...] += product

    def finish(which, base, grad_ref, out_ref, d_ref):
        normal, rstd = norm_forward(base + acc_ref[...])
        gain = norms_ref[2 + which : 3 + which]
        out_ref[...] = normal * gain + norms_ref[6 + which : 7 + which]
        gradient = grad_ref[...].astype(F32)
        sums_ref[0, 0:1, :] = column_sum(gradient * normal)
        sums_ref[0, 1:2, :] = column_sum(gradient)
        d_sum = norm_backward(normal, rstd, gain, gradient)
        d_ref[...] = d_sum
        low_sum = d_sum.astype(BF16)
        dm_ref[...] = low_sum
        for s in range(begin_ref.shape[0]):
            begin_ref[s] = low_sum[s * toks : s * toks + 1]
            end_ref[s] = low_sum[(s + 1) * toks - 1 : (s + 1) * toks]

    @pl.when((half == 0) & (k == 2))
    def _():
        finish(
            0, normal_ref[...] * norms_ref[1:2] + norms_ref[5:6], tok_g_ref, tok_ref, d_tok_ref
        )

    @pl.when((half == 1) & (k == 2))
    def _():
        finish(1, proj_ref[...], char_g_ref, char_ref, d_char_ref)


def conv_call(f_low, proj_low, normal1, proj, norms, low, high, packed, tok_grad, char_grad, seqs, carry):
    total, width = f_low.shape
    count = packed.shape[0]
    blk = 2 * width // count
    rows = (total, width)
    return launch(
        functools.partial(conv_kernel, total // seqs),
        (2, 3),
        [],
        [f_low, proj_low, normal1, proj, norms, low, high, packed, tok_grad, char_grad],
        [ whole(rows), whole(rows), whole(rows), whole(rows), whole(norms.shape), whole(low.shape), whole(high.shape), pl.BlockSpec((count, blk, width), lambda h, k: (0, 2 * k + h, 0)), whole(rows), whole(rows), ],
        [ whole(rows), whole(rows), whole(rows), whole(rows), pl.BlockSpec(rows, lambda h, k: (0, h)), pl.BlockSpec((1, 2, width), lambda h, k: (h, 0, 0)), pl.BlockSpec((seqs, 1, width), lambda h, k: (0, 0, h)), pl.BlockSpec((seqs, 1, width), lambda h, k: (0, 0, h)), ],
        [ stored(rows, F32), stored(rows, F32), shape(rows, F32), shape(rows, F32), shape((total, 2 * width), BF16), shape((2, 2, width), F32), shape((seqs, 1, 2 * width), BF16), shape((seqs, 1, 2 * width), BF16), ],
        [pltpu.VMEM(rows, F32), pltpu.VMEM((3, total, 2 * width), BF16)],
        cost(24 * total * width * width, 24 * width * width + 40 * total * width),
        "conv",
        carry,
    )


def place_blocks(part_ref, order_ref, send_ref, keep_ref, blk, row=0):
    count = part_ref.shape[0] // blk
    for pos in range(count):
        start = pl.multiple_of(order_ref[pos] * blk, 16)
        piece = part_ref[pl.ds(start, blk), :].astype(BF16)
        if pos < count // 2:
            keep_ref[pos, row : row + blk, :] = piece
        else:
            send_ref[pos - count // 2, row : row + blk, :] = piece


def conv_weight_kernel(
    toks, order_ref, f_ref, p_ref, other_f_ref, other_p_ref, dm_ref, other_dm_ref, low_ref,
    high_ref, other_low_ref, other_high_ref, keep_a_ref, sent_a_ref, keep_b_ref, sent_b_ref,
    turned_ref, whole_ref, part_ref,
):
    k, half = pl.program_id(0), pl.program_id(1)
    total, width = f_ref.shape
    pieces = 2 * keep_a_ref.shape[0]
    blk = keep_a_ref.shape[1]

    @pl.when((k == 0) & (half == 0))
    def _():
        edges = ((low_ref[...], high_ref[...]), (other_low_ref[...], other_high_ref[...]))
        pairs = ((f_ref, p_ref), (other_f_ref, other_p_ref))
        for core, (pair, (low, high)) in enumerate(zip(pairs, edges)):
            for part, source in enumerate(pair):
                columns = slice(part * width, (part + 1) * width)
                middle = source[...]
                before, after = shifted(
                    middle.astype(F32),
                    toks,
                    low[:, :, columns].astype(F32),
                    high[:, :, columns].astype(F32),
                )
                for at, value in enumerate((before, middle, after)):
                    whole_ref[at, columns, :] = value.T
            for pos in range(pieces):
                start = pl.multiple_of(order_ref[pos] * blk, 16)
                for at in range(3):
                    turned_ref[
                        at, pos * blk : (pos + 1) * blk, core * total : (core + 1) * total
                    ] = whole_ref[at, pl.ds(start, blk), :]

    turned = turned_ref[k]
    part_ref[...] = dot(turned[:, :total], dm_ref[...], 1, 0) + dot(
        turned[:, total:], other_dm_ref[...], 1, 0
    )

    def put(keep_ref, sent_ref, kept, sent):
        for index, (one, other) in enumerate(zip(kept, sent)):
            keep_ref[index] = part_ref[one * blk : (one + 1) * blk, :].astype(BF16)
            sent_ref[index] = part_ref[other * blk : (other + 1) * blk, :].astype(BF16)

    at = 2 * k + half

    @pl.when(at < 3)
    def _():
        put(keep_a_ref, sent_a_ref, range(pieces // 2), range(pieces // 2, pieces))

    @pl.when(at >= 3)
    def _():
        put(keep_b_ref, sent_b_ref, range(0, pieces, 2), range(1, pieces, 2))


def conv_weight_call(order, own, other, dm, other_dm, edges, count):
    total, width = own[0].shape
    toks = total // edges[0].shape[0]
    blk = 2 * width // count
    out = (count // 4, 3 * blk, width)
    first = pl.BlockSpec((count // 4, blk, width), lambda k, h, *_: (0, jnp.minimum(2 * k + h, 2), 0))
    second = pl.BlockSpec(
        (count // 4, blk, width), lambda k, h, *_: (0, jnp.maximum(2 * k + h - 3, 0), 0)
    )
    columns = pl.BlockSpec((total, width), lambda k, h, *_: (0, h))
    plain = [*own, *other]
    keep_a, sent_a, keep_b, sent_b = launch(
        functools.partial(conv_weight_kernel, toks),
        (3, 2),
        [order],
        [*plain, dm, other_dm, *edges],
        [*[whole(v.shape) for v in plain], columns, columns, *[whole(v.shape) for v in edges]],
        [first, first, second, second],
        [stored(out, BF16)] * 4,
        [
            pltpu.VMEM((3, width, 2 * total), BF16),
            pltpu.VMEM((3, 2 * width, total), BF16),
            pltpu.VMEM((width, width), F32),
        ],
        cost(24 * total * width * width, 12 * width * width),
        "conv_weight",
    )
    return [[keep_a, sent_a], [keep_b, sent_b]]


def conv_back_kernel(
    toks, dm_ref, low_ref, high_ref, w_ref, d_tok_ref, d_char_ref, normal_ref, rstd_ref,
    norms_ref, d_proj_ref, d_ffn_ref, sums_ref, shift_ref, acc_ref,
):
    k, half = pl.program_id(0), pl.program_id(1)
    width = d_tok_ref.shape[1]

    @pl.when((half == 0) & (k == 0))
    def _():
        for part in range(2):
            columns = slice(part * width, (part + 1) * width)
            source = dm_ref[:, columns]
            before, after = shifted(
                source.astype(F32),
                toks,
                low_ref[:, :, columns].astype(F32),
                high_ref[:, :, columns].astype(F32),
            )
            shift_ref[part] = after
            shift_ref[2 + part] = source
            shift_ref[4 + part] = before

    product = dot(shift_ref[2 * k + half], flat_block(w_ref), 1, 1)

    @pl.when((k == 0) & (half == 0))
    def _():
        acc_ref[...] = product

    @pl.when((k > 0) | (half > 0))
    def _():
        acc_ref[...] += product

    @pl.when((k == 2) & (half == 1))
    def _():
        d_proj_ref[...] = (d_char_ref[...] + acc_ref[:, width:]).astype(BF16)
        gradient = d_tok_ref[...] + acc_ref[:, :width]
        normal = normal_ref[...]
        sums_ref[0:1, :] = column_sum(gradient * normal)
        sums_ref[1:2, :] = column_sum(gradient)
        d_ffn_ref[...] = norm_backward(normal, rstd_ref[...], norms_ref[1:2], gradient)


def conv_back_call(d_merged, low, high, packed, d_tok, d_char, normal1, rstd1, norms, seqs):
    total, width = d_tok.shape
    count = packed.shape[0]
    blk = 2 * width // count
    rows = (total, width)
    return launch(
        functools.partial(conv_back_kernel, total // seqs),
        (3, 2),
        [],
        [d_merged, low, high, packed, d_tok, d_char, normal1, rstd1, norms],
        [ whole(d_merged.shape), whole(low.shape), whole(high.shape), pl.BlockSpec((count, blk, width), lambda k, h: (0, 2 * k + h, 0)), whole(rows), whole(rows), whole(rows), whole(rstd1.shape), whole(norms.shape), ],
        [whole(rows), whole(rows), whole((2, width))],
        [shape(rows, BF16), shape(rows, F32), shape((2, width), F32)],
        [ pltpu.VMEM((6, total, width), BF16), pltpu.VMEM((total, 2 * width), F32), ],
        cost(24 * total * width * width, 24 * width * width + 20 * total * width),
        "conv_back",
    )


def rest_kernel(
    order_ref, table_ref, s_ref, w0_ref, w1_ref, send_ref, keep_ref, part_ref,
):
    count, blk, width = w0_ref.shape
    rows = part_ref.shape[0]
    turned = flat_block(table_ref).T
    sums = s_ref[...].reshape(rows, 2 * width)
    for part in range(2):
        part_ref[0:width, :] = dot(turned, sums[:, part * width : (part + 1) * width], 1, 0)
        place_blocks(part_ref.at[0:width], order_ref, send_ref, keep_ref, blk, part * blk)
    part_ref[...] = dot(sums[:, :width], flat_block(w0_ref), 1, 1) + dot(
        sums[:, width:], flat_block(w1_ref), 1, 1
    )
    place_blocks(part_ref, order_ref, send_ref, keep_ref, rows // count, 2 * blk)


def rest_call(order, packed, at_table, at_gru, sums, height):
    count, _, width = packed.shape
    blk = width // count
    rows = sums.shape[0] * sums.shape[1]
    table_rows = rows // count
    out = (count // 2, height, width)
    return launch(
        rest_kernel,
        (1,),
        [order],
        [packed, sums, packed, packed],
        [
            pl.BlockSpec((count, table_rows, width), lambda i, *_: (0, at_table, 0)),
            whole(sums.shape),
            pl.BlockSpec((count, blk, width), lambda i, *_: (0, at_gru, 0)),
            pl.BlockSpec((count, blk, width), lambda i, *_: (0, at_gru + 1, 0)),
        ],
        [whole(out), whole(out)],
        [stored(out, BF16), stored(out, BF16)],
        [pltpu.VMEM((rows, width), F32)],
        cost(8 * rows * width * width, 20 * width * width),
        "rest",
    )


def qkv_back_kernel(
    seqs, order_ref, d_ref, x_ref, w_ref, d_attn_ref,
    sums0_ref, sums1_ref, sums23_ref, bias_ref, bias_up_ref, out_ref, send_ref, keep_ref, xt_ref,
    dt_ref, part_ref, small_ref,
):
    j = pl.program_id(0)
    per = d_ref.shape[1]
    head, toks = d_ref.shape[3:]
    pieces, _, width = send_ref.shape
    blk = width // (2 * pieces)
    half = width // 2

    def put(row):
        for pos in range(2 * pieces):
            start = pl.multiple_of(order_ref[pos] * blk, 16)
            piece = part_ref[pl.ds(start, blk), :].astype(BF16)
            if pos < pieces:
                keep_ref[pos, row, :] = piece
            else:
                send_ref[pos - pieces, row, :] = piece

    @pl.when(j == 0)
    def _():
        xt_ref[...] = x_ref[...].T
        out_ref[...] = d_attn_ref[...]
        small_ref[...] = jnp.zeros_like(small_ref)
        for row, ref in enumerate((sums0_ref, sums1_ref)):
            small_ref[row : row + 1] = ref[0:1]
            small_ref[4 + row : 5 + row] = ref[1:2]
        for which in range(2):
            small_ref[2 + which : 3 + which] = sums23_ref[which, 0:1]
            small_ref[6 + which : 7 + which] = sums23_ref[which, 1:2]
        for part in range(2):
            own = slice(part * half, (part + 1) * half)
            small_ref[8:9, own] = bias_ref[:, part * width : part * width + half]
            small_ref[9:10, own] = bias_ref[:, part * width + half : (part + 1) * width]
        for part in range(bias_up_ref.shape[1] // width):
            small_ref[10 + part : 11 + part] = bias_up_ref[:, part * width : (part + 1) * width]
        small = small_ref[...].astype(BF16)
        for pos in range(pieces):
            keep_ref[pos, 3 * blk : 3 * blk + SMALL_ROWS, :] = small
            send_ref[pos, 3 * blk : 3 * blk + SMALL_ROWS, :] = small

    for s in range(seqs):
        for h in range(HEADS):
            pair = s * HEADS + h
            dt_ref[h * head : (h + 1) * head, s * toks : (s + 1) * toks] = d_ref[
                pair // per, pair % per, 0
            ]
    gradient = dt_ref[...].T
    part_ref[...] = dot(xt_ref[...], gradient, 1, 0)
    put(pl.ds(pl.multiple_of(j * blk, 16), blk))
    out_ref[...] += dot(gradient, flat_block(w_ref), 1, 1)


def qkv_back_call(
    order, d_qkv, rows, packed, base, d_attn, small, seqs, height
):
    count, per, _, head, toks = d_qkv.shape
    total, width = rows.shape
    blk = width // count
    out = (count // 2, height, width)
    rest = [d_attn, *small]
    return launch(
        functools.partial(qkv_back_kernel, seqs),
        (3,),
        [order],
        [d_qkv, rows, packed, *rest],
        [
            pl.BlockSpec((count, per, 1, head, toks), lambda j, *_: (0, 0, j, 0, 0)),
            whole(rows.shape),
            pl.BlockSpec((count, blk, width), lambda j, *_: (0, base + j, 0)),
            *[whole(v.shape) for v in rest],
        ],
        [whole((total, width)), whole(out), whole(out)],
        [stored((total, width), F32), stored(out, BF16), stored(out, BF16)],
        [
            pltpu.VMEM((width, total), BF16),
            pltpu.VMEM((width, total), BF16),
            pltpu.VMEM((width, width), F32),
            pltpu.VMEM((SMALL_ROWS, width), F32),
        ],
        cost(16 * total * width * width, 20 * width * width + 16 * total * width),
        "qkv_back",
    )


def pack_kernel(layout, *refs):
    ins, out_ref = refs[:-1], refs[-1]
    at = 0
    out_ref[...] = jnp.zeros_like(out_ref)
    width = out_ref.shape[1]
    for ref, row in zip(ins, layout):
        height, columns = ref.shape
        if columns < width:
            out_ref[row : row + height, :columns] = ref[...]
        else:
            for block in range(columns // width):
                out_ref[row + block * height : row + (block + 1) * height, :] = ref[
                    :, block * width : (block + 1) * width
                ]


def pack(arrays, layout, rows, width):
    return launch(
        functools.partial(pack_kernel, layout),
        (1,),
        [],
        arrays,
        [whole(v.shape) for v in arrays],
        whole((rows, width)),
        shape((rows, width), BF16),
        [],
        cost(0, 4 * rows * width),
        "pack",
    )


def swap(value, axis, bit):
    size = lax.axis_size(axis)
    return lax.ppermute(value, axis, [(i, i ^ (1 << bit)) for i in range(size)])


def add_low(kept, arrived):
    return (kept.astype(F32) + arrived.astype(F32)).astype(BF16)


def fold_kernel(keep_top, keep_bottom, came_top, came_bottom, ka_ref, sa_ref, kb_ref, sb_ref):
    half = ka_ref.shape[0]
    for index in range(half):
        ka_ref[index] = add_low(keep_top[index], came_top[index])
        sa_ref[index] = add_low(keep_top[half + index], came_top[half + index])
        kb_ref[index] = add_low(keep_bottom[2 * index], came_bottom[2 * index])
        sb_ref[index] = add_low(keep_bottom[2 * index + 1], came_bottom[2 * index + 1])


def tiles(rows):
    return 3 if PLACED and rows % 48 == 0 else 1


def fold_pieces_kernel(keep_top, keep_bottom, *refs):
    pieces = keep_top.shape[0]
    top, bottom, outs = refs[:pieces], refs[pieces : 2 * pieces], refs[2 * pieces :]
    ka_ref, sa_ref, kb_ref, sb_ref = outs
    half = pieces // 2
    for index in range(half):
        ka_ref[index] = add_low(keep_top[index], top[index][...])
        sa_ref[index] = add_low(keep_top[half + index], top[half + index][...])
        kb_ref[index] = add_low(keep_bottom[2 * index], bottom[2 * index][...])
        sb_ref[index] = add_low(keep_bottom[2 * index + 1], bottom[2 * index + 1][...])


def fold(keep, arrived):
    pieces, rows, width = keep.shape
    steps = tiles(rows // 2)
    tile = rows // 2 // steps
    top = pl.BlockSpec((pieces, tile, width), lambda i: (0, i, 0))
    bottom = pl.BlockSpec((pieces, tile, width), lambda i: (0, steps + i, 0))
    one_top = pl.BlockSpec((tile, width), lambda i: (i, 0))
    one_bottom = pl.BlockSpec((tile, width), lambda i: (steps + i, 0))
    ka, sa, kb, sb = launch(
        fold_pieces_kernel,
        (steps,),
        [],
        [keep, keep, *arrived, *arrived],
        [top, bottom] + [one_top] * pieces + [one_bottom] * pieces,
        [pl.BlockSpec((pieces // 2, tile, width), lambda i: (0, i, 0))] * 4,
        [stored((pieces // 2, rows // 2, width), BF16)] * 4,
        [],
        cost(pieces * rows * width, 6 * pieces * rows * width),
        "fold",
    )
    return [[ka, sa], [kb, sb]]


def send_links(state, step):
    bits = lax.axis_size("seq").bit_length() - 1
    return [
        [kept, swap(sent, "seq", bit)] for (kept, sent), bit in zip(state, (step, bits - step))
    ]


def split(state):
    pieces, rows, width = state[0][0].shape
    steps = tiles(rows)
    spec = pl.BlockSpec((pieces, rows // steps, width), lambda i, *_: (0, i, 0))
    out = pl.BlockSpec((pieces // 2, rows // steps, width), lambda i, *_: (0, i, 0))
    return plan(
        fold_kernel,
        (steps,),
        [],
        [state[0][0], state[1][0], state[0][1], state[1][1]],
        [spec] * 4,
        [out] * 4,
        [stored((pieces // 2, rows, width), BF16)] * 4,
        [],
        cost(pieces * rows * width, 12 * pieces * rows * width),
        "split",
    )


def paired(values):
    ka, sa, kb, sb = values
    return [[ka, sa], [kb, sb]]


def cross_kernel(place_ref, ka_ref, kb_ref, ca_ref, cb_ref, kept_ref, sent_ref):
    high = (place_ref[0] & 1) == 1
    first = add_low(ka_ref[0], ca_ref[0])
    second = add_low(kb_ref[0], cb_ref[0])
    kept_ref[...] = jnp.where(high, second, first)
    sent_ref[...] = jnp.where(high, first, second)


def cross(place, state):
    _, rows, width = state[0][0].shape
    steps = tiles(rows)
    spec = pl.BlockSpec((1, rows // steps, width), lambda i, *_: (0, i, 0))
    return plan(
        cross_kernel,
        (steps,),
        [place],
        [state[0][0], state[1][0], state[0][1], state[1][1]],
        [spec] * 4,
        [pl.BlockSpec((rows // steps, width), lambda i, *_: (i, 0))] * 2,
        [stored((rows, width), BF16)] * 2,
        [],
        cost(rows * width, 12 * rows * width),
        "cross",
    )


def halve_kernel(bit, place_ref, kept_ref, came_ref, next_ref, sent_ref):
    high = ((place_ref[0] >> bit) & 1) == 1
    rows = next_ref.shape[0]
    first = add_low(kept_ref[:rows], came_ref[:rows])
    second = add_low(kept_ref[rows:], came_ref[rows:])
    next_ref[...] = jnp.where(high, second, first)
    sent_ref[...] = jnp.where(high, first, second)


def halve(place, bit, kept, came):
    rows, width = kept.shape
    return plan(
        functools.partial(halve_kernel, bit),
        (1,),
        [place],
        [kept, came],
        [whole(kept.shape)] * 2,
        [whole((rows // 2, width))] * 2,
        [stored((rows // 2, width), BF16)] * 2,
        [],
        cost(rows * width, 6 * rows * width),
        "halve",
    )


def add_kernel(kept_ref, came_ref, out_ref):
    out_ref[...] = add_low(kept_ref[...], came_ref[...])


def add(kept, came):
    return plan(
        add_kernel,
        (1,),
        [],
        [kept, came],
        [whole(kept.shape)] * 2,
        whole(kept.shape),
        stored(kept.shape, BF16),
        [],
        cost(kept.size, 6 * kept.size),
        "add",
    )


def assemble_kernel(bit, place_ref, held_ref, came_ref, out_ref):
    high = ((place_ref[0] >> bit) & 1) == 1
    rows = held_ref.shape[0]
    held, came = held_ref[...], came_ref[...]
    out_ref[:rows] = jnp.where(high, came, held)
    out_ref[rows:] = jnp.where(high, held, came)


def assemble(place, bit, held, came):
    rows, width = held.shape
    return plan(
        functools.partial(assemble_kernel, bit),
        (1,),
        [place],
        [held, came],
        [whole(held.shape)] * 2,
        whole((2 * rows, width)),
        stored((2 * rows, width), BF16),
        [],
        cost(rows * width, 8 * rows * width),
        "assemble",
    )


def finish_kernel(layout, place_ref, held_ref, came_ref, *out_refs):
    high = (place_ref[0] & 1) == 1
    rows = held_ref.shape[0]
    for begin, size, out, index in layout:
        part = slice(begin % rows, begin % rows + size)
        held, came = held_ref[part].astype(F32), came_ref[part].astype(F32)
        out_refs[out][index] = jnp.where(high == (begin < rows), came, held)


def cut(layout, rows):
    for begin, size, out, index in layout:
        edges = [begin, begin + size]
        if begin < rows < begin + size:
            edges.insert(1, rows)
        for low, high in zip(edges, edges[1:]):
            yield low, high - low, out, index[:-2] + (slice(low - begin, high - begin), index[-1])


def finish(place, held, came, layout, outs):
    layout = list(cut(layout, held.shape[0]))
    return plan(
        functools.partial(finish_kernel, layout),
        (1,),
        [place],
        [held, came],
        [whole(held.shape)] * 2,
        [whole(dims) for dims in outs],
        [stored(dims, F32) for dims in outs],
        [],
        cost(held.size, 16 * held.size),
        "finish",
    )


def across_halves(place, kept, sent, layout, outs, merged=False):
    bits = lax.axis_size("batch").bit_length() - 1
    came = swap(sent, "batch", 0)
    halved = bits - 1 if merged else bits
    for bit in range(1, halved):
        kept, sent = yield halve(place, bit, kept, came)
        came = swap(sent, "batch", bit)
    (held,) = yield add(kept, came)
    for bit in range(halved, bits):
        (held,) = yield add(held, swap(held, "batch", bit))
    for bit in reversed(range(halved)):
        came = swap(held, "batch", bit)
        if bit:
            (held,) = yield assemble(place, bit, held, came)
    return (yield finish(place, held, came, layout, outs))


def deal_kernel(place_ref, ka_ref, kb_ref, ca_ref, cb_ref, *refs):
    outs, sum_ref = refs[:-1], refs[-1]
    rows, part = ka_ref.shape[1], outs[0].shape[0]
    sum_ref[:rows] = add_low(ka_ref[0], ca_ref[0])
    sum_ref[rows:] = add_low(kb_ref[0], cb_ref[0])
    for mask, out_ref in enumerate(outs):
        start = pl.multiple_of((place_ref[0] ^ mask) * part, 16)
        out_ref[...] = sum_ref[pl.ds(start, part), :]


def total_kernel(*refs):
    total = refs[0][...].astype(F32)
    for ref in refs[1:-1]:
        total += ref[...].astype(F32)
    refs[-1][...] = total.astype(BF16)


def spread_kernel(layout, small_at, parts, place_ref, me_ref, *refs):
    ins, outs, all_ref = refs[:parts], refs[parts:-1], refs[-1]
    rows = ins[0].shape[0]
    for mask, ref in enumerate(ins):
        start = pl.multiple_of((place_ref[0] ^ mask) * rows, 16)
        all_ref[pl.ds(start, rows), :] = ref[...]
    for begin, size, out, index in layout:
        outs[out][index] = all_ref[begin : begin + size].astype(F32)
    blk, share = outs[-5].shape[1], outs[-1].shape[1]
    small = all_ref[small_at : small_at + SMALL_ROWS].astype(F32)
    width = small.shape[1]
    me = me_ref[0]
    mine = pltpu.roll(small, lax.rem(width - me * blk, width), 1)[:, :blk]
    outs[-5][...] = mine[0:4]
    outs[-4][...] = mine[4:8]
    outs[-3][...] = mine[8:9]
    outs[-2][...] = mine[9:10]
    spot = me * share
    turned = pltpu.roll(small, lax.rem(width - lax.rem(spot, width), width), 1)[:, :share]
    row = lax.broadcasted_iota(jnp.int32, turned.shape, 0)
    outs[-1][...] = column_sum(jnp.where(row == 10 + lax.div(spot, width), turned, 0.0))


def across_direct(place, me, state, layout, small_at, outs):
    for link in range(2, lax.axis_size("seq").bit_length() - 1):
        state = send_links(paired((yield split(state))), link)
    parts = lax.axis_size("batch")
    _, rows, width = state[0][0].shape
    part = (2 * rows // parts, width)
    ends = [(mask, [(i, i ^ mask) for i in range(parts)]) for mask in range(1, parts)]
    pieces = yield plan(
        deal_kernel,
        (1,),
        [place],
        [state[0][0], state[1][0], state[0][1], state[1][1]],
        [whole(state[0][0].shape)] * 4,
        [whole(part)] * parts,
        [stored(part, BF16)] * parts,
        [pltpu.VMEM((2 * rows, width), BF16)],
        cost(rows * width, 12 * rows * width),
        "deal",
    )
    came = [lax.ppermute(pieces[mask], "batch", pairs) for mask, pairs in ends]
    (held,) = yield plan(
        total_kernel,
        (1,),
        [],
        [pieces[0], *came],
        [whole(part)] * parts,
        [whole(part)],
        [stored(part, BF16)],
        [],
        cost(rows * width, 5 * rows * width),
        "total",
    )
    came = [lax.ppermute(held, "batch", pairs) for _, pairs in ends]
    return (
        yield plan(
            functools.partial(spread_kernel, layout, small_at, parts),
            (1,),
            [place, me],
            [held, *came],
            [whole(part)] * parts,
            [whole(dims) for dims in outs],
            [stored(dims, F32) for dims in outs],
            [pltpu.VMEM((2 * rows, width), BF16)],
            cost(rows * width, 12 * rows * width),
            "spread",
        )
    )


def neighbours(first, last):
    count = lax.axis_size("seq")
    up = [(i, i + 1) for i in range(count - 1)]
    down = [(target, source) for source, target in up]
    return lax.ppermute(last, "seq", up), lax.ppermute(first, "seq", down)


def local(
    hidden, char_ids, group_ids, word_lengths, qkv_weight, out_weight, up_weight, ffn_bias,
    down_weight, gru_weight, gate_bias, candidate_bias, char_weight, conv_weight, char_table,
    norm_gain, norm_shift, tok_grad, char_grad,
):
    count = lax.axis_size("seq")
    bits = count.bit_length() - 1
    me = lax.axis_index("seq").astype(jnp.int32)
    seqs, toks, width = hidden.shape
    total = seqs * toks
    half = width // 2
    blk = width // count
    share = ffn_bias.shape[0]
    table_rows = char_table.shape[0]
    chars = char_ids.shape[1]
    reverse = [int(format(i, f"0{bits}b")[::-1], 2) for i in range(count)]
    order = jnp.asarray(reverse, jnp.int32) ^ me
    slot = sum(
        (((jnp.arange(count, dtype=jnp.int32) ^ me) >> b) & 1) << (bits - 1 - b) for b in range(bits)
    )
    me_one = me.reshape(1)

    place = lax.axis_index("batch").astype(jnp.int32).reshape(1)
    LATEST.clear()
    PLACED[:] = [True]
    NEAR.clear()

    table_at = share
    small_at = table_at + table_rows
    block_at = small_at + 16
    block_at += -block_at % blk
    pack_rows = block_at + 11 * blk
    small = jnp.concatenate(
        [norm_gain.T, norm_shift.T, gate_bias[None], candidate_bias[None]], 0
    )
    small = jnp.pad(small, ((0, 6), (0, width - blk)))
    small = small.at[10, :share].set(ffn_bias)
    arrays = [
        down_weight, char_table, small, gru_weight, qkv_weight, char_weight, out_weight, up_weight
    ]
    at_block = block_at // blk
    at_gru, at_qkv, at_char, at_out, at_up = (at_block + i for i in (0, 2, 5, 6, 7))
    layout = [0, table_at, small_at] + [i * blk for i in (at_gru, at_qkv, at_char, at_out, at_up)]
    at_table, at_down = table_at // table_rows, 0
    first = pack(arrays, layout, pack_rows, width)
    third = pack(
        [conv_weight[k] for k in range(3)], [k * 4 * blk for k in range(3)], 12 * blk, width
    )
    first = lax.all_gather(first, "seq", axis=0)
    third = lax.all_gather(third, "seq", axis=0)
    vectors = (
        first[:, small_at : small_at + 10, :blk].astype(F32).transpose(1, 0, 2).reshape(10, width)
    )
    bias_up = first[:, small_at + 10, :share].astype(F32).reshape(1, -1)
    norms = vectors

    rows = hidden.reshape(total, width)
    words = word_lengths.reshape(seqs, toks)
    ends = jnp.cumsum(words, axis=1)
    starts = ends - words
    lens = words.astype(F32)[..., None]

    qkv = qkv_call(rows, first, at_qkv, seqs, count)
    qkv = lax.all_to_all(qkv, "seq", 0, 0, tiled=True)
    z, c, block_totals = gates_call(group_ids, char_ids, first, at_gru, at_table, vectors)
    gathered = [block_totals] + [
        lax.ppermute(block_totals, "seq", [(i, i ^ mask) for i in range(count)])
        for mask in range(1, count)
    ]
    step = (1 << 19) // (count * toks)
    mixture, totals = attend_call(qkv, 2 * step)
    mixture = lax.all_to_all(mixture, "seq", 0, 0, tiled=True)
    gathered = collect(me_one, gathered)
    prior, pooled, proj, proj_low = states_call(
        me_one, z, c, gathered, starts[..., None], ends[..., None], lens, first, at_char, 2
    )
    mix_t, normal0, rstd0, normed, active, slope, normal1, rstd1, f_low = ffn_call(
        mixture, rows, first, at_out, at_up, at_down, bias_up, norms, seqs
    )

    def edges(left, right):
        joined = [v.reshape(seqs, toks, width) for v in (left, right)]
        return (
            jnp.concatenate([v[:, :1] for v in joined], -1),
            jnp.concatenate([v[:, -1:] for v in joined], -1),
        )

    begin, end = edges(f_low, proj_low)
    low, high = neighbours(begin, end)
    other = [swap(v, "seq", 0) for v in (f_low, proj_low)]
    tok_out, char_out, d_tok, d_char, d_merged, sums23, begin, end, *other = conv_call(
        f_low, proj_low, normal1, proj, norms, low, high, third,
        tok_grad.reshape(total, width), char_grad.reshape(total, width), seqs, other,
    )

    joined_edges = [low, high, swap(low, "seq", 0), swap(high, "seq", 0)]
    low, high = neighbours(begin, end)
    other_dm = swap(d_merged, "seq", 0)

    def onward(state, first_link):
        for link in range(first_link + 1, bits):
            ((values,), _) = together([split(state)])
            state = send_links(paired(values), link)
        return state

    def columns_of(begin, blocks, out):
        return [
            (begin + j * blk, blk, out, (slice(None), slice(j * width, (j + 1) * width)))
            for j in range(blocks)
        ]

    everything = (slice(None), slice(None))
    double = 2 * blk
    batch_bits = lax.axis_size("batch").bit_length() - 1
    unit = 8 * lax.axis_size("batch")
    height = max(2 * blk + table_rows, 3 * blk + SMALL_ROWS)
    height += -height % unit
    d_proj, d_ffn, sums1 = conv_back_call(
        d_merged, low, high, third, d_tok, d_char, normal1, rstd1, norms, seqs
    )
    conv_state = conv_weight_call(
        order, (f_low, proj_low), other, d_merged, other_dm, joined_edges, count
    )
    conv_state = send_links(conv_state, 1)
    ds, back_totals = states_back_call(
        d_proj, first, at_char, lens, starts[:, None, :], ends[:, None, :], z
    )
    send, keep, d_bias_up, d_attn, sums0, d_mix = ffn_back_call(
        slot, order, d_ffn, active, slope, normed, normal0, rstd0, norms, first, at_out, at_up,
        at_down, back_totals, mix_t, pooled, d_proj, seqs,
    )
    d_mix = lax.all_to_all(d_mix, "seq", 0, 0, tiled=True)
    ffn_came = [swap(piece, "seq", 0) for piece in send]
    conv_state = onward(conv_state, 1)
    ffn_state = fold(keep, ffn_came)
    ffn_state = send_links(ffn_state, 1)
    d_qkv = attend_back_call(qkv, d_mix, totals, step)
    PLACED.clear()
    d_qkv = lax.all_to_all(d_qkv, "seq", 0, 0, tiled=True)
    ((halves,), _) = together([cross(place, conv_state)])
    conv_run = Steps(
        across_halves(
            place, *halves,
            [
                (
                    r * double, double, 0,
                    (r // 2, slice(None), slice(r % 2 * width, (r % 2 + 1) * width)),
                )
                for r in range(6)
            ],
            [(3, double, 2 * width)],
        )
    )
    sums, d_bias = gates_back_call(
        me_one, group_ids, z, c, prior, ds, gathered, d_mix, char_ids,
        count * table_rows // NCHAR, 2,
    )
    ffn_state = onward(ffn_state, 1)
    for _ in range(1, batch_bits):
        advance(conv_run)
    rest_send, rest_keep = rest_call(order, first, at_table, at_gru, sums, height)
    hidden_grad, qkv_send, qkv_keep = qkv_back_call(
        order, d_qkv, rows, first, at_qkv, d_attn,
        [sums0, sums1, sums23, d_bias, d_bias_up], seqs, height,
    )
    PLACED.clear()
    (halves, (held,)), (rest_send, qkv_send) = together(
        [cross(place, ffn_state), conv_run.plan], [rest_send, qkv_send]
    )
    conv_run.resume([held])
    ffn_run = Steps(
        across_halves(
            place, *halves,
            [
                (0, share, 0, everything),
                *columns_of(share, 4, 1),
                (share + 4 * blk, blk, 2, everything),
                (share + 5 * blk, blk, 3, everything),
            ],
            [(share, width), (blk, 4 * width), (blk, width), (blk, width)], True,
        )
    )
    rest_came, qkv_came = (swap(send, "seq", 0) for send in (rest_send, qkv_send))
    ((values,), _) = together([split([[rest_keep, rest_came], [qkv_keep, qkv_came]])])
    last_run = Steps(
        across_direct(
            place, me_one, send_links(paired(values), 1),
            [
                *columns_of(0, 2, 0),
                (2 * blk, table_rows, 1, everything),
                *columns_of(height, 3, 2),
            ],
            height + 3 * blk,
            [
                (blk, 2 * width), (table_rows, width), (blk, 3 * width),
                (4, blk), (4, blk), (1, blk), (1, blk), (1, share),
            ],
        )
    )
    advance(conv_run, ffn_run, last_run)
    advance(last_run)
    while conv_run.plan or ffn_run.plan or last_run.plan:
        advance(conv_run, ffn_run, last_run)
    (conv_grad,) = conv_run.result
    down_grad, up_grad, out_grad, char_grad_w = ffn_run.result
    gru_grad, table_grad, qkv_grad, *small_grads = last_run.result
    d_gain, d_shift = (v.T for v in small_grads[:2])
    d_gate_b, d_cand_b, d_ffn_b = (v.reshape(-1) for v in small_grads[2:])
    shape_out = (seqs, toks, width)
    return (
        tok_out.reshape(shape_out),
        char_out.reshape(shape_out),
        hidden_grad.reshape(shape_out),
        qkv_grad,
        out_grad,
        up_grad,
        d_ffn_b,
        down_grad,
        gru_grad,
        d_gate_b,
        d_cand_b,
        char_grad_w,
        conv_grad,
        table_grad,
        d_gain,
        d_shift,
    )


def solution(mesh):
    rows, columns = P("seq", None), P("batch", "seq", None)
    return jax.shard_map(
        local,
        mesh=mesh,
        in_specs=(
            columns, P("batch", "seq"), P("batch"), columns, rows, rows, rows, P("seq"), rows,
            rows, P("seq"), P("seq"), rows, P(None, "seq", None), rows, rows, rows, columns,
            columns,
        ),
        out_specs=(
            columns, columns, columns, rows, rows, rows, P("seq"), rows, rows, P("seq"), P("seq"),
            rows, P(None, "seq", None), rows, rows, rows,
        ),
        check_vma=False,
    )
```

```python
import functools
import math

import jax
import jax.numpy as jnp
from jax import lax
from jax.experimental import pallas as pl
from jax.experimental.pallas import tpu as pltpu
from jax.sharding import PartitionSpec as P

HEADS = 12
NCHAR = 256
NORM_EPS = 1e-06
LANES = 128
SMALL_ROWS = 16
RIDE = 32
SCALE = 1000
F32 = jnp.float32
BF16 = jnp.bfloat16
VMEM_BYTES = 44 << 20
VMEM_MARGIN = 9 << 20


def dot(left, right, left_dim, right_dim):
    return lax.dot_general(
        left, right, (((left_dim,), (right_dim,)), ((), ())), preferred_element_type=F32
    )


def padded_bytes(dims, dtype):
    size = jnp.dtype(dtype).itemsize
    dims = (1, 1, *dims)
    rows = -(-dims[-2] * size // 32) * 32
    lanes = -(-dims[-1] // LANES) * LANES
    return math.prod(dims[:-2]) * rows * lanes


def params(grid_rank, blocks, scratch):
    need = sum(2 * padded_bytes(spec.block_shape, value.dtype) for spec, value in blocks)
    need += sum(padded_bytes(ref.shape, ref.dtype) for ref in scratch)
    return pltpu.CompilerParams(
        dimension_semantics=("arbitrary",) * grid_rank,
        vmem_limit_bytes=min(VMEM_BYTES, need + VMEM_MARGIN),
    )


def shape(dims, dtype):
    return jax.ShapeDtypeStruct(dims, dtype)


def stored(dims, dtype):
    return pltpu.HBM(dims, dtype) if PLACED else shape(dims, dtype)


def whole(dims):
    return pl.BlockSpec(dims, lambda *_: (0,) * len(dims))


def cost(flops, nbytes):
    return pl.CostEstimate(flops=int(flops) * SCALE, bytes_accessed=int(nbytes) * SCALE, transcendentals=0)


NEAR = []
LATEST = []
PLACED = []
TOKEN = jax.ShapeDtypeStruct((8, LANES), F32)


def launch(
    body, grid, prefetch, inputs, in_specs, out_specs, out_shape, scratch, price, name, carry=()
):
    deps = [pltpu.with_memory_space_constraint(v, pltpu.HBM) for v in LATEST]
    single = not isinstance(out_shape, (list, tuple))
    outs = [out_shape] if single else list(out_shape)
    specs = [out_specs] if single else list(out_specs)
    lead = len(prefetch) + len(inputs)
    extra = len(carry) + len(deps)
    anywhere = pl.BlockSpec(memory_space=pl.ANY)

    def kernel(*refs):
        own = refs[lead + extra :]
        body(*refs[:lead], *own[: len(outs)], *own[len(outs) + len(carry) + 1 :])

    inputs = [
        v
        if not PLACED or v.size < 1 << 16 or any(v is near for near in NEAR)
        else pltpu.with_memory_space_constraint(v, pltpu.HBM)
        for v in inputs
    ]
    results = pl.pallas_call(
        kernel,
        grid_spec=pltpu.PrefetchScalarGridSpec(
            num_scalar_prefetch=len(prefetch),
            grid=grid,
            in_specs=list(in_specs) + [anywhere] * extra,
            out_specs=specs + [anywhere] * (len(carry) + 1),
            scratch_shapes=scratch,
        ),
        out_shape=outs + [stored(v.shape, v.dtype) for v in (*carry, TOKEN)],
        input_output_aliases={lead + i: len(outs) + i for i in range(len(carry))},
        compiler_params=params(
            len(grid), [*zip(in_specs, inputs), *zip(specs, outs)], scratch
        ),
        cost_estimate=price,
        name=name,
    )(*prefetch, *inputs, *carry, *deps)
    NEAR.extend(v for v, out in zip(results, outs) if isinstance(out, jax.ShapeDtypeStruct))
    *results, LATEST[:] = *results[:-1], results[-1:]
    return results[0] if len(results) == 1 else results


def plan(body, grid, prefetch, inputs, in_specs, out_specs, out_shape, scratch, price, name):
    listed = isinstance(out_shape, (list, tuple))
    outs = (list(out_specs), list(out_shape)) if listed else ([out_specs], [out_shape])
    return body, grid, prefetch, inputs, in_specs, *outs, scratch, price, name


def together(plans, carry=()):
    bodies, grids, prefetch, inputs, in_specs, out_specs, outs, scratch, prices, names = zip(*plans)
    assert len(set(grids)) == 1
    groups = (prefetch, inputs, outs, scratch)

    def body(*refs):
        own = [[] for _ in plans]
        for group in groups:
            for refs_of, part in zip(own, group):
                refs_of.extend(refs[: len(part)])
                refs = refs[len(part) :]
        for one, refs_of in zip(bodies, own):
            one(*refs_of)

    def flat(parts):
        return [v for part in parts for v in part]

    price = pl.CostEstimate(
        flops=sum(v.flops for v in prices),
        bytes_accessed=sum(v.bytes_accessed for v in prices),
        transcendentals=0,
    )
    results = launch(
        body, grids[0], flat(prefetch), flat(inputs), flat(in_specs), flat(out_specs), flat(outs),
        flat(scratch), price, "_".join(names), carry,
    )
    results = list(results) if isinstance(results, (list, tuple)) else [results]
    found = []
    for part in outs:
        found.append(results[: len(part)])
        results = results[len(part) :]
    return found, results


class Steps:
    def __init__(self, plans):
        self.plans, self.result = plans, None
        self.plan = next(plans)

    def resume(self, values):
        try:
            self.plan = self.plans.send(values)
        except StopIteration as end:
            self.plan, self.result = None, end.value


def advance(*runs, carry=()):
    live = [run for run in runs if run.plan]
    found, carried = together([run.plan for run in live], carry)
    for run, values in zip(live, found):
        run.resume(values)
    return carried


def flat_block(ref):
    block = ref[...]
    return block.reshape(block.shape[0] * block.shape[1], block.shape[2])


def norm_forward(values):
    center = values - jnp.mean(values, -1, keepdims=True)
    rstd = lax.rsqrt(jnp.mean(center * center, -1, keepdims=True) + NORM_EPS)
    return center * rstd, rstd


def norm_backward(normal, rstd, gain, gradient):
    scaled = gradient * gain
    first = jnp.mean(scaled, -1, keepdims=True)
    second = jnp.mean(scaled * normal, -1, keepdims=True)
    return rstd * (scaled - first - normal * second)


def column_sum(values):
    return jnp.sum(values, 0, keepdims=True)


def gelu_parts(values):
    size = jnp.abs(values) * 0.7071067811865476
    bell = jnp.exp(-size * size)
    t = 1.0 / (1.0 + 0.3275911 * size)
    series = t * (
        0.254829592
        + t * (-0.284496736 + t * (1.421413741 + t * (-1.453152027 + t * 1.061405429)))
    )
    tail = 0.5 * series * bell
    phi_sum = jnp.where(values < 0, tail, 1.0 - tail)
    return values * phi_sum, phi_sum + values * (bell * 0.3989422804014327)


def qkv_kernel(seqs, toks, per, x_ref, w_ref, o_ref):
    acc = dot(x_ref[...], flat_block(w_ref), 1, 0)
    turned = acc.T.astype(BF16)
    width = turned.shape[0] // HEADS
    for s in range(seqs):
        for h in range(HEADS):
            pair = s * HEADS + h
            o_ref[pair // per, pair % per, 0] = turned[
                h * width : (h + 1) * width, s * toks : (s + 1) * toks
            ]


def qkv_call(rows, packed, base, seqs, count):
    total, width = rows.shape
    toks = total // seqs
    per = seqs * HEADS // count
    head = width // HEADS
    blk = width // count
    return launch(
        functools.partial(qkv_kernel, seqs, toks, per),
        (3,),
        [],
        [rows, packed],
        [ whole(rows.shape), pl.BlockSpec((count, blk, width), lambda j: (0, base + j, 0)), ],
        pl.BlockSpec((count, per, 1, head, toks), lambda j: (0, 0, j, 0, 0)),
        stored((count, per, 3, head, toks), BF16),
        [],
        cost(6 * total * width * width, 6 * width * width + 8 * total * width),
        "qkv",
    )


def spread(ref, index):
    return jnp.concatenate([ref[(i, *index)] for i in range(ref.shape[0])], axis=1)


def attend_kernel(step, scale, x_ref, o_ref, total_ref):
    queries = spread(x_ref, (0, 0)) * scale
    keys = spread(x_ref, (0, 1)).T
    values = spread(x_ref, (0, 2))
    toks = x_ref.shape[-1]
    for begin in range(0, queries.shape[1], step):
        scores = dot(keys, queries[:, begin : begin + step], 1, 0)
        highest = jnp.max(scores, 0, keepdims=True)
        expo = jnp.exp(scores - highest)
        totals = jnp.sum(expo, 0, keepdims=True)
        mixture = (dot(values, expo.astype(BF16), 1, 0) / totals).astype(BF16)
        total_ref[0, :, begin : begin + step] = highest + jnp.log(totals)
        for at in range(0, step, toks):
            o_ref[(begin + at) // toks, 0] = mixture[:, at : at + toks]


def attend_call(qkv, step):
    count, per, _, head, toks = qkv.shape
    length = count * toks
    scale = head**-0.5
    return launch(
        functools.partial(attend_kernel, step, scale),
        (per,),
        [],
        [qkv],
        [pl.BlockSpec((count, 1, 3, head, toks), lambda p: (0, p, 0, 0, 0))],
        [ pl.BlockSpec((count, 1, head, toks), lambda p: (0, p, 0, 0)), pl.BlockSpec((1, 1, length), lambda p: (p, 0, 0)), ],
        [stored((count, per, head, toks), BF16), shape((per, 1, length), F32)],
        [],
        cost(16 * per * length * length * head, 8 * per * length * head),
        "attend",
    )


def attend_back_kernel(step, scale, x_ref, g_ref, total_ref, o_ref):
    queries = spread(x_ref, (0, 0)) * scale
    keys_t = spread(x_ref, (0, 1))
    keys = keys_t.T
    values = spread(x_ref, (0, 2)).T
    grads = spread(g_ref, ())
    toks = x_ref.shape[-1]
    length = queries.shape[1]
    d_keys = jnp.zeros(queries.shape, F32)
    d_values = jnp.zeros(queries.shape, F32)
    for begin in range(0, length, step):
        query = queries[:, begin : begin + step]
        grad = grads[:, begin : begin + step]
        scores = dot(keys, query, 1, 0)
        probability = jnp.exp(scores - total_ref[0, :, begin : begin + step])
        d_prob = dot(values, grad, 1, 0)
        centered = jnp.sum(probability * d_prob, 0, keepdims=True)
        d_scores = (probability * (d_prob - centered)).astype(BF16)
        d_values += dot(grad, probability.astype(BF16), 1, 1)
        d_keys += dot(query, d_scores, 1, 1)
        d_query = (dot(keys_t, d_scores, 1, 0) * scale).astype(BF16)
        for at in range(0, step, toks):
            o_ref[(begin + at) // toks, 0, 0] = d_query[:, at : at + toks]
    d_keys = d_keys.astype(BF16)
    d_values = d_values.astype(BF16)
    for i in range(length // toks):
        o_ref[i, 0, 1] = d_keys[:, i * toks : (i + 1) * toks]
        o_ref[i, 0, 2] = d_values[:, i * toks : (i + 1) * toks]


def attend_back_call(qkv, grads, totals, step):
    count, per, _, head, toks = qkv.shape
    length = count * toks
    scale = head**-0.5
    return launch(
        functools.partial(attend_back_kernel, step, scale),
        (per,),
        [],
        [qkv, grads, totals],
        [ pl.BlockSpec((count, 1, 3, head, toks), lambda p: (0, p, 0, 0, 0)), pl.BlockSpec((count, head, toks), lambda p: (0, p, 0)), pl.BlockSpec((1, 1, length), lambda p: (p, 0, 0)), ],
        pl.BlockSpec((count, 1, 3, head, toks), lambda p: (0, p, 0, 0, 0)),
        stored(qkv.shape, BF16),
        [],
        cost(40 * per * length * length * head, 14 * per * length * head),
        "attend_back",
    )


def ffn_kernel(
    seqs,
    o_ref,
    x_ref,
    w_out_ref,
    w_up_ref,
    w_down_ref,
    bias_ref,
    norms_ref,
    mix_ref,
    normal0_ref,
    rstd0_ref,
    a_ref,
    g_ref,
    slope_ref,
    normal1_ref,
    rstd1_ref,
    f_ref,
    acc_ref,
):
    j = pl.program_id(0)
    per = o_ref.shape[1]
    head, toks = o_ref.shape[2:]

    @pl.when(j == 0)
    def _():
        for s in range(seqs):
            for h in range(HEADS):
                pair = s * HEADS + h
                mix_ref[h * head : (h + 1) * head, s * toks : (s + 1) * toks] = o_ref[
                    pair // per, pair % per
                ]
        attended = dot(mix_ref[...].T, flat_block(w_out_ref), 1, 0)
        normal, rstd = norm_forward(x_ref[...].astype(F32) + attended)
        normal0_ref[...] = normal
        rstd0_ref[...] = rstd
        normed = normal * norms_ref[0:1] + norms_ref[4:5]
        a_ref[...] = normed.astype(BF16)
        acc_ref[...] = normed

    up = dot(a_ref[...], flat_block(w_up_ref), 1, 0) + bias_ref[...]
    active, slope = gelu_parts(up)
    active = active.astype(BF16)
    g_ref[...] = active
    slope_ref[...] = slope.astype(BF16)
    acc_ref[...] += dot(active, flat_block(w_down_ref), 1, 0)

    @pl.when(j == pl.num_programs(0) - 1)
    def _():
        normal, rstd = norm_forward(acc_ref[...])
        normal1_ref[...] = normal
        rstd1_ref[...] = rstd
        f_ref[...] = (normal * norms_ref[1:2] + norms_ref[5:6]).astype(BF16)


def ffn_call(mixture, rows, packed, at_out, at_up, at_down, bias, norms, seqs):
    count, per, head, toks = mixture.shape
    total, width = rows.shape
    hidden = bias.shape[1]
    chunks = hidden // width
    blk = width // count
    owners = count // chunks
    return launch(
        functools.partial(ffn_kernel, seqs),
        (chunks,),
        [],
        [mixture, rows, packed, packed, packed, bias, norms],
        [ whole(mixture.shape), whole(rows.shape), pl.BlockSpec((count, blk, width), lambda j: (0, at_out, 0)), pl.BlockSpec((count, blk, width), lambda j: (0, at_up + j, 0)), pl.BlockSpec((owners, hidden // count, width), lambda j: (j, at_down, 0)), pl.BlockSpec((1, width), lambda j: (0, j)), whole(norms.shape), ],
        [ whole((width, total)), whole((total, width)), whole((total, 1)), whole((total, width)), pl.BlockSpec((total, width), lambda j: (0, j)), pl.BlockSpec((total, width), lambda j: (0, j)), whole((total, width)), whole((total, 1)), whole((total, width)), ],
        [ stored((width, total), BF16), stored((total, width), F32), stored((total, 1), F32), stored((total, width), BF16), stored((total, hidden), BF16), stored((total, hidden), BF16), shape((total, width), F32), shape((total, 1), F32), shape((total, width), BF16)],
        [pltpu.VMEM((total, width), F32)],
        cost( 2 * total * width * (width + 2 * hidden), 4 * hidden * width + 10 * total * hidden ),
        "ffn",
    )


def ffn_back_kernel(
    seqs,
    slot_ref,
    order_ref,
    d_ref,
    g_ref,
    slope_ref,
    a_ref,
    normal_ref,
    rstd_ref,
    norms_ref,
    w_out_ref,
    w_up_ref,
    w_down_ref,
    total_ref,
    mix_ref,
    pooled_ref,
    d_proj_ref,
    *refs,
):
    j = pl.program_id(0)
    count, blk, width = w_up_ref.shape
    owners, share, _ = w_down_ref.shape
    half = count // 2
    send_refs, refs = refs[:half], refs[half:]
    keep_ref, bias_ref, d_attn_ref, sums_ref, d_mix_ref = refs[:5]
    db_ref, at_ref, acc_ref, part_ref, down_ref = refs[5:]

    @pl.when(j == 0)
    def _():
        db_ref[...] = d_ref[...].astype(BF16)
        at_ref[...] = a_ref[...].T
        acc_ref[...] = d_ref[...]

    part_ref[...] = dot(g_ref[...].T, db_ref[...], 1, 0)
    for i in range(owners):
        slot = slot_ref[j * owners + i]
        down_ref[slot] = part_ref[i * share : (i + 1) * share, :].astype(BF16)

    d_up = (dot(db_ref[...], flat_block(w_down_ref), 1, 1) * slope_ref[...].astype(F32)).astype(BF16)
    bias_ref[...] = column_sum(d_up.astype(F32))
    part_ref[...] = dot(at_ref[...], d_up, 1, 0)
    place = pl.ds(pl.multiple_of(share + j * blk, 16), blk)
    for pos in range(count):
        piece = part_ref[pl.ds(pl.multiple_of(order_ref[pos] * blk, 16), blk), :].astype(BF16)
        if pos < half:
            keep_ref[pos, place, :] = piece
        else:
            send_refs[pos - half][place, :] = piece
    acc_ref[...] += dot(d_up, flat_block(w_up_ref), 1, 1)

    @pl.when(j == pl.num_programs(0) - 1)
    def _():
        for pos in range(half):
            keep_ref[pos, 0:share, :] = down_ref[pos]
            send_refs[pos][0:share, :] = down_ref[half + pos]
        gradient = acc_ref[...]
        normal = normal_ref[...]
        sums_ref[0:1, :] = column_sum(gradient * normal)
        sums_ref[1:2, :] = column_sum(gradient)
        d_sum = norm_backward(normal, rstd_ref[...], norms_ref[0:1], gradient)
        d_attn_ref[...] = d_sum
        low = d_sum.astype(BF16)

        def put(row):
            for pos in range(count):
                start = pl.multiple_of(order_ref[pos] * blk, 16)
                piece = part_ref[pl.ds(start, blk), :].astype(BF16)
                if pos < half:
                    keep_ref[pos, row : row + blk, :] = piece
                else:
                    send_refs[pos - half][row : row + blk, :] = piece

        base = keep_ref.shape[1] - 2 * blk
        part_ref[...] = dot(mix_ref[...], low, 1, 0)
        put(base)
        part_ref[...] = dot(pooled_ref[...].T, d_proj_ref[...], 1, 0)
        put(base + blk)
        turned = dot(flat_block(w_out_ref), low, 1, 1).astype(BF16)
        per = seqs * HEADS // count
        head, toks = width // HEADS, d_mix_ref.shape[2]
        for s in range(seqs):
            for h in range(HEADS):
                pair = s * HEADS + h
                row = pair % per * head
                d_mix_ref[pair // per, row : row + head] = turned[
                    h * head : (h + 1) * head, s * toks : (s + 1) * toks
                ]
        rest = jnp.concatenate([total_ref[j] for j in range(total_ref.shape[0])], 0)
        rest = jnp.concatenate([rest, jnp.zeros((RIDE - rest.shape[0], LANES), F32)], 0)
        for part in range(3):
            low = rest.astype(BF16)
            rest = rest - low.astype(F32)
            row = per * head + part * RIDE
            for device in range(count):
                d_mix_ref[device, row : row + RIDE] = low


def ffn_back_call(
    slot, order, d_ffn, active, slope, normed, normal, rstd, norms, packed, at_out, at_up, at_down, totals, mixture, pooled, d_proj, seqs):
    total, width = d_ffn.shape
    hidden = active.shape[1]
    count = packed.shape[0]
    chunks = hidden // width
    blk = width // count
    share = hidden // count
    owners = count // chunks
    per = seqs * HEADS // count
    head = width // HEADS
    toks = total // seqs
    rows_out = share + (chunks + 2) * blk
    wide = pl.BlockSpec((total, width), lambda j, *_: (0, j))
    results = launch(
        functools.partial(ffn_back_kernel, seqs),
        (chunks,),
        [slot, order],
        [d_ffn, active, slope, normed, normal, rstd, norms, packed, packed, packed, totals, mixture, pooled, d_proj],
        [ whole(d_ffn.shape), wide, wide, whole(normed.shape), whole(normal.shape), whole(rstd.shape), whole(norms.shape), pl.BlockSpec((count, blk, width), lambda j, *_: (0, at_out, 0)), pl.BlockSpec((count, blk, width), lambda j, *_: (0, at_up + j, 0)), pl.BlockSpec((owners, share, width), lambda j, *_: (j, at_down, 0)), whole(totals.shape), whole(mixture.shape), whole(pooled.shape), whole(d_proj.shape), ],
        [ *[whole((rows_out, width))] * (count // 2), whole((count // 2, rows_out, width)), pl.BlockSpec((1, width), lambda j, *_: (0, j)), whole((total, width)), whole((2, width)), whole((count, per * head + 3 * RIDE, toks)), ],
        [ *[stored((rows_out, width), BF16)] * (count // 2), stored((count // 2, rows_out, width), BF16), stored((1, hidden), F32), stored((total, width), F32), stored((2, width), F32), stored((count, per * head + 3 * RIDE, toks), BF16), ],
        [ pltpu.VMEM((total, width), BF16), pltpu.VMEM((width, total), BF16), pltpu.VMEM((total, width), F32), pltpu.VMEM((width, width), F32), pltpu.VMEM((count, share, width), BF16), ],
        cost( 8 * total * width * hidden + 2 * total * width * width, 8 * hidden * width + 10 * total * hidden, ),
        "ffn_back",
    )
    return results[: count // 2], *results[count // 2 :]


def gates_kernel(
    seqs, groups_ref, ids_ref, back_ids_ref, table_ref, w_fwd_ref, w_rev_ref, bias_ref,
    z_ref, c_ref, totals_ref,
):
    s = pl.program_id(0)
    steps = ids_ref.shape[1]
    rows = 2 * seqs
    table = flat_block(table_ref)
    vocabulary = lax.broadcasted_iota(jnp.int32, (steps, NCHAR), 1)
    chunks = z_ref.shape[0]
    half = chunks * LANES
    for direction, (source, weight) in enumerate(((ids_ref, w_fwd_ref), (back_ids_ref, w_rev_ref))):
        onehot = jnp.where(source[0] == vocabulary, 1.0, 0.0).astype(BF16)
        embedded = dot(onehot, table, 1, 0).astype(BF16)
        gate_input = dot(embedded, flat_block(weight), 1, 0)
        own = slice(direction * half, (direction + 1) * half)
        update = jax.nn.sigmoid(gate_input[:, :half] + bias_ref[8:9, own])
        candidate = jnp.tanh(gate_input[:, half:] + bias_ref[9:10, own])
        place = pl.ds(s + direction * seqs, steps, stride=rows)
        for j in range(chunks):
            z_ref[j, place, :] = update[:, j * LANES : (j + 1) * LANES]
            c_ref[j, place, :] = candidate[:, j * LANES : (j + 1) * LANES]

    @pl.when(s == pl.num_programs(0) - 1)
    def _():
        def one(t, carry):
            states, products = carry
            place = pl.ds(pl.multiple_of(t * rows, rows), rows)
            new_states, new_products = [], []
            for j in range(chunks):
                update = z_ref[j, place, :]
                decay = 1.0 - update
                new_states.append(decay * states[j] + update * c_ref[j, place, :])
                new_products.append(products[j] * decay)
            return tuple(new_states), tuple(new_products)

        zero = jnp.zeros((rows, LANES), F32)
        states, products = lax.fori_loop(
            0, steps, one, ((zero,) * chunks, (zero + 1.0,) * chunks), unroll=8
        )
        for j in range(chunks):
            totals_ref[0, j] = products[j]
            totals_ref[1, j] = states[j]


def gates_call(groups, ids, packed, at_gru, at_table, bias):
    seqs, steps = ids.shape
    count, _, width = packed.shape
    blk = width // count
    table_rows = 4 * NCHAR // count
    per_group = NCHAR // table_rows
    chunks = width // 2 // LANES
    laid = (chunks, steps * 2 * seqs, LANES)
    return launch(
        functools.partial(gates_kernel, seqs),
        (seqs,),
        [groups],
        [ids[..., None], ids[:, ::-1, None], packed, packed, packed, bias],
        [ pl.BlockSpec((1, steps, 1), lambda s, g: (s, 0, 0)), pl.BlockSpec((1, steps, 1), lambda s, g: (s, 0, 0)), pl.BlockSpec((per_group, table_rows, width), lambda s, g: (g[s], at_table, 0)), pl.BlockSpec((count, blk, width), lambda s, g: (0, at_gru, 0)), pl.BlockSpec((count, blk, width), lambda s, g: (0, at_gru + 1, 0)), whole(bias.shape), ],
        [whole(laid), whole(laid), whole((2, chunks, 2 * seqs, LANES))],
        [stored(laid, F32), stored(laid, F32), stored((2, chunks, 2 * seqs, LANES), F32)],
        [],
        cost( 2 * seqs * steps * width * (2 * NCHAR + 2 * width), 16 * seqs * steps * width ),
        "gates",
    )


def entry_state(me, totals, products, rows, seqs, forward):
    count, chunks = products.shape[0], products.shape[1]
    first = lax.broadcasted_iota(jnp.int32, (rows, LANES), 0) < seqs
    result = []
    for j in range(chunks):
        state = jnp.zeros((rows, LANES), F32)
        for lap in range(count):
            up, down = lap, count - 1 - lap
            one, other = (up, down) if forward else (down, up)
            product = jnp.where(first, products[one, j], products[other, j])
            total = jnp.where(first, totals[one, j], totals[other, j])
            up_in, down_in = (up < me).astype(F32), (down > me).astype(F32)
            ahead = jnp.where(first, up_in, down_in) if forward else jnp.where(first, down_in, up_in)
            state = jnp.where(ahead > 0.5, product * state + total, state)
        result.append(state)
    return result


def states_kernel(
    seqs, me_ref, z_ref, c_ref, all_ref, starts_ref, ends_ref, lens_ref, w_ref,
    prior_ref, pooled_ref, proj_ref, proj_low_ref, hold_ref, state_ref, acc_ref,
):
    i = pl.program_id(0)
    last = pl.num_programs(0) - 1
    rows = 2 * seqs
    chunks = z_ref.shape[0]
    span = z_ref.shape[1] // rows
    toks = starts_ref.shape[1]
    half = chunks * LANES

    @pl.when(i == 0)
    def _():
        entry = entry_state(me_ref[0], all_ref[:, 1], all_ref[:, 0], rows, seqs, True)
        for j in range(chunks):
            state_ref[j] = entry[j]
        acc_ref[...] = jnp.zeros_like(acc_ref)

    def one(t, states):
        place = pl.ds(pl.multiple_of(t * rows, rows), rows)
        result = []
        for j in range(chunks):
            prior_ref[j, place, :] = states[j]
            update = z_ref[j, place, :]
            state = (1.0 - update) * states[j] + update * c_ref[j, place, :]
            hold_ref[j, place, :] = state
            result.append(state)
        return tuple(result)

    states = lax.fori_loop(0, span, one, tuple(state_ref[j] for j in range(chunks)), unroll=8)
    for j in range(chunks):
        state_ref[j] = states[j]
    count = lax.broadcasted_iota(jnp.int32, (toks, span), 1) + i * span
    for direction in range(2):
        place_of = count if direction == 0 else (last + 1) * span - 1 - count
        for s in range(seqs):
            member = jnp.where(
                (place_of >= starts_ref[s]) & (place_of < ends_ref[s]), 1.0, 0.0
            ).astype(BF16)
            held = jnp.concatenate(
                [
                    hold_ref[j, pl.ds(s + direction * seqs, span, stride=rows), :]
                    for j in range(chunks)
                ],
                axis=1,
            ).astype(BF16)
            acc_ref[s * toks : (s + 1) * toks, direction * half : (direction + 1) * half] += dot(
                member, held, 1, 0
            )

    @pl.when(i == last)
    def _():
        for s in range(seqs):
            rows_of = slice(s * toks, (s + 1) * toks)
            pooled_ref[rows_of, :] = (acc_ref[rows_of, :] / lens_ref[s]).astype(BF16)
        proj = dot(pooled_ref[...], flat_block(w_ref), 1, 0)
        proj_ref[...] = proj
        proj_low_ref[...] = proj.astype(BF16)


def collect_kernel(me_ref, *refs):
    for mask, ref in enumerate(refs[:-1]):
        refs[-1][me_ref[0] ^ mask] = ref[...]


def collect(me, parts):
    out = (len(parts), *parts[0].shape)
    return launch(
        collect_kernel,
        (1,),
        [me],
        parts,
        [whole(v.shape) for v in parts],
        whole(out),
        shape(out, parts[0].dtype),
        [],
        cost(0, 8 * len(parts) * parts[0].size),
        "collect",
    )


def states_call(me, z, c, gathered, starts, ends, lens, packed, at_char, parts):
    chunks, length, _ = z.shape
    seqs, toks, _ = starts.shape
    count, _, width = packed.shape
    blk = width // count
    span = length // parts
    total = seqs * toks
    stream = pl.BlockSpec((chunks, span, LANES), lambda i, *_: (0, i, 0))
    return launch(
        functools.partial(states_kernel, seqs),
        (parts,),
        [me],
        [z, c, gathered, starts, ends, lens, packed],
        [ stream, stream, whole(gathered.shape), whole(starts.shape), whole(ends.shape), whole(lens.shape), pl.BlockSpec((count, blk, width), lambda i, *_: (0, at_char, 0)), ],
        [stream] + [whole((total, width))] * 3,
        [stored(z.shape, F32), stored((total, width), BF16), stored((total, width), F32), shape((total, width), BF16), ],
        [ pltpu.VMEM((chunks, span, LANES), F32), pltpu.VMEM((chunks, 2 * seqs, LANES), F32), pltpu.VMEM((total, width), F32), ],
        cost(2 * total * width * (width + length // 8), 12 * chunks * length * LANES),
        "states",
    )


def states_back_kernel(
    seqs, d_ref, w_ref, lens_ref, starts_ref, ends_ref, z_ref, ds_ref, total_ref,
):
    rows = 2 * seqs
    chunks = z_ref.shape[0]
    steps = z_ref.shape[1] // rows
    toks = starts_ref.shape[2]
    half = chunks * LANES
    d_pooled = dot(d_ref[...], flat_block(w_ref), 1, 1)
    count = lax.broadcasted_iota(jnp.int32, (steps, toks), 0)
    for s in range(seqs):
        d_summed = (d_pooled[s * toks : (s + 1) * toks] / lens_ref[s]).astype(BF16)
        for direction in range(2):
            place_of = count if direction == 0 else steps - 1 - count
            member = jnp.where(
                (place_of >= starts_ref[s]) & (place_of < ends_ref[s]), 1.0, 0.0
            ).astype(BF16)
            d_states = dot(member, d_summed[:, direction * half : (direction + 1) * half], 1, 0)
            for j in range(chunks):
                ds_ref[j, pl.ds(s + direction * seqs, steps, stride=rows), :] = d_states[
                    :, j * LANES : (j + 1) * LANES
                ]

    def one(lap, carried):
        place = pl.ds(pl.multiple_of((steps - 1 - lap) * rows, rows), rows)
        return tuple(
            (1.0 - z_ref[j, place, :]) * (ds_ref[j, place, :] + carried[j]) for j in range(chunks)
        )

    zero = jnp.zeros((rows, LANES), F32)
    carried = lax.fori_loop(0, steps, one, (zero,) * chunks, unroll=8)
    for j in range(chunks):
        total_ref[j] = carried[j]


def states_back_call(d_proj, packed, at_char, lens, starts, ends, z):
    chunks, length, _ = z.shape
    seqs = starts.shape[0]
    count, _, width = packed.shape
    blk = width // count
    return launch(
        functools.partial(states_back_kernel, seqs),
        (1,),
        [],
        [d_proj, packed, lens, starts, ends, z],
        [ whole(d_proj.shape), pl.BlockSpec((count, blk, width), lambda i: (0, at_char, 0)), whole(lens.shape), whole(starts.shape), whole(ends.shape), whole(z.shape), ],
        [whole(z.shape), whole((chunks, 2 * seqs, LANES))],
        [stored(z.shape, F32), shape((chunks, 2 * seqs, LANES), F32)],
        [],
        cost( 2 * d_proj.shape[0] * width * (width + length // 8), 8 * chunks * length * LANES ),
        "states_back",
    )


def gates_back_kernel(
    seqs, me_ref, groups_ref, z_ref, c_ref, prior_ref, ds_ref, all_ref, back_ref, ids_ref,
    back_ids_ref, s_ref, bias_ref, du_ref, dc_ref, carried_ref, acc_ref,
):
    i = pl.program_id(0)
    rows = 2 * seqs
    chunks = z_ref.shape[0]
    span = z_ref.shape[1] // rows
    half = chunks * LANES

    @pl.when(i == 0)
    def _():
        parts = back_ref[...].astype(F32)
        summed = parts[:, :RIDE] + parts[:, RIDE : 2 * RIDE] + parts[:, 2 * RIDE :]
        totals = summed[:, : chunks * rows].reshape(-1, chunks, rows, LANES)
        entry = entry_state(me_ref[0], totals, all_ref[:, 0], rows, seqs, False)
        for j in range(chunks):
            carried_ref[j] = entry[j]
        acc_ref[...] = jnp.zeros_like(acc_ref)

    def one(lap, carried):
        place = pl.ds(pl.multiple_of((span - 1 - lap) * rows, rows), rows)
        result = []
        for j in range(chunks):
            update = z_ref[j, place, :]
            candidate = c_ref[j, place, :]
            total = ds_ref[j, place, :] + carried[j]
            decay = 1.0 - update
            gated = total * update
            du_ref[j, place, :] = gated * decay * (candidate - prior_ref[j, place, :])
            dc_ref[j, place, :] = gated * (1.0 - candidate * candidate)
            result.append(decay * total)
        return tuple(result)

    carried = lax.fori_loop(0, span, one, tuple(carried_ref[j] for j in range(chunks)), unroll=8)
    for j in range(chunks):
        carried_ref[j] = carried[j]
    vocabulary = lax.broadcasted_iota(jnp.int32, (NCHAR, span), 0)
    for direction in range(2):
        source = ids_ref if direction == 0 else back_ids_ref
        for s in range(seqs):
            place = pl.ds(s + direction * seqs, span, stride=rows)
            gradient = jnp.concatenate(
                [part[j, place, :] for part in (du_ref, dc_ref) for j in range(chunks)], axis=1
            ).astype(BF16)
            onehot = jnp.where(source[s] == vocabulary, 1.0, 0.0).astype(BF16)
            acc_ref[groups_ref[s], :, direction * 2 * half : (direction + 1) * 2 * half] += dot(
                onehot, gradient, 1, 0
            )

    @pl.when(i == pl.num_programs(0) - 1)
    def _():
        total = jnp.zeros((1, 4 * half), F32)
        for g in range(acc_ref.shape[0]):
            total += column_sum(acc_ref[g])
            s_ref[g] = acc_ref[g].astype(BF16)
        bias_ref[...] = total


def gates_back_call(me, groups, z, c, prior, ds, gathered, gathered_back, ids, n_groups, parts):
    chunks, length, _ = z.shape
    seqs, steps = ids.shape
    span = length // parts
    width = 2 * chunks * LANES
    stream = pl.BlockSpec((chunks, span, LANES), lambda i, *_: (0, parts - 1 - i, 0))
    lanes = pl.BlockSpec((seqs, 1, steps // parts), lambda i, *_: (0, 0, parts - 1 - i))
    return launch(
        functools.partial(gates_back_kernel, seqs),
        (parts,),
        [me, groups],
        [z, c, prior, ds, gathered, gathered_back, ids[:, None, :], ids[:, None, ::-1]],
        [stream] * 4 + [whole(gathered.shape), pl.BlockSpec((gathered_back.shape[0], 3 * RIDE, LANES), lambda i, *_: (0, gathered_back.shape[1] // (3 * RIDE) - 1, 0)), lanes, lanes],
        [whole((n_groups, NCHAR, 2 * width)), whole((1, 2 * width))],
        [shape((n_groups, NCHAR, 2 * width), BF16), shape((1, 2 * width), F32)],
        [ pltpu.VMEM((chunks, span, LANES), F32), pltpu.VMEM((chunks, span, LANES), F32), pltpu.VMEM((chunks, 2 * seqs, LANES), F32), pltpu.VMEM((n_groups, NCHAR, 2 * width), F32), ],
        cost(4 * seqs * steps * NCHAR * width, 16 * chunks * length * LANES),
        "gates_back",
    )


def shifted(values, toks, low, high):
    total = values.shape[0]
    row = lax.broadcasted_iota(jnp.int32, (total, 1), 0)
    before = pltpu.roll(values, 1, 0)
    after = pltpu.roll(values, total - 1, 0)
    for s in range(total // toks):
        before = jnp.where(row == s * toks, low[s], before)
        after = jnp.where(row == (s + 1) * toks - 1, high[s], after)
    return before.astype(BF16), after.astype(BF16)


def conv_kernel(
    toks, f_ref, p_ref, normal_ref, proj_ref, norms_ref, low_ref, high_ref, w_ref, tok_g_ref,
    char_g_ref, tok_ref, char_ref, d_tok_ref, d_char_ref, dm_ref, sums_ref, begin_ref, end_ref,
    acc_ref, x_ref,
):
    half, k = pl.program_id(0), pl.program_id(1)
    width = f_ref.shape[1]

    @pl.when((half == 0) & (k == 0))
    def _():
        for part, source in enumerate((f_ref, p_ref)):
            columns = slice(part * width, (part + 1) * width)
            before, after = shifted(
                source[...].astype(F32),
                toks,
                low_ref[:, :, columns].astype(F32),
                high_ref[:, :, columns].astype(F32),
            )
            x_ref[0, :, columns] = before
            x_ref[1, :, columns] = source[...]
            x_ref[2, :, columns] = after

    product = dot(x_ref[k], flat_block(w_ref), 1, 0)

    @pl.when(k == 0)
    def _():
        acc_ref[...] = product

    @pl.when(k > 0)
    def _():
        acc_ref[...] += product

    def finish(which, base, grad_ref, out_ref, d_ref):
        normal, rstd = norm_forward(base + acc_ref[...])
        gain = norms_ref[2 + which : 3 + which]
        out_ref[...] = normal * gain + norms_ref[6 + which : 7 + which]
        gradient = grad_ref[...].astype(F32)
        sums_ref[0, 0:1, :] = column_sum(gradient * normal)
        sums_ref[0, 1:2, :] = column_sum(gradient)
        d_sum = norm_backward(normal, rstd, gain, gradient)
        d_ref[...] = d_sum
        low_sum = d_sum.astype(BF16)
        dm_ref[...] = low_sum
        for s in range(begin_ref.shape[0]):
            begin_ref[s] = low_sum[s * toks : s * toks + 1]
            end_ref[s] = low_sum[(s + 1) * toks - 1 : (s + 1) * toks]

    @pl.when((half == 0) & (k == 2))
    def _():
        finish(
            0, normal_ref[...] * norms_ref[1:2] + norms_ref[5:6], tok_g_ref, tok_ref, d_tok_ref
        )

    @pl.when((half == 1) & (k == 2))
    def _():
        finish(1, proj_ref[...], char_g_ref, char_ref, d_char_ref)


def conv_call(f_low, proj_low, normal1, proj, norms, low, high, packed, tok_grad, char_grad, seqs, carry):
    total, width = f_low.shape
    count = packed.shape[0]
    blk = 2 * width // count
    rows = (total, width)
    return launch(
        functools.partial(conv_kernel, total // seqs),
        (2, 3),
        [],
        [f_low, proj_low, normal1, proj, norms, low, high, packed, tok_grad, char_grad],
        [ whole(rows), whole(rows), whole(rows), whole(rows), whole(norms.shape), whole(low.shape), whole(high.shape), pl.BlockSpec((count, blk, width), lambda h, k: (0, 2 * k + h, 0)), whole(rows), whole(rows), ],
        [ whole(rows), whole(rows), whole(rows), whole(rows), pl.BlockSpec(rows, lambda h, k: (0, h)), pl.BlockSpec((1, 2, width), lambda h, k: (h, 0, 0)), pl.BlockSpec((seqs, 1, width), lambda h, k: (0, 0, h)), pl.BlockSpec((seqs, 1, width), lambda h, k: (0, 0, h)), ],
        [ stored(rows, F32), stored(rows, F32), shape(rows, F32), shape(rows, F32), shape((total, 2 * width), BF16), shape((2, 2, width), F32), shape((seqs, 1, 2 * width), BF16), shape((seqs, 1, 2 * width), BF16), ],
        [pltpu.VMEM(rows, F32), pltpu.VMEM((3, total, 2 * width), BF16)],
        cost(24 * total * width * width, 24 * width * width + 40 * total * width),
        "conv",
        carry,
    )


def place_blocks(part_ref, order_ref, send_ref, keep_ref, blk, row=0):
    count = part_ref.shape[0] // blk
    for pos in range(count):
        start = pl.multiple_of(order_ref[pos] * blk, 16)
        piece = part_ref[pl.ds(start, blk), :].astype(BF16)
        if pos < count // 2:
            keep_ref[pos, row : row + blk, :] = piece
        else:
            send_ref[pos - count // 2, row : row + blk, :] = piece


def conv_weight_kernel(
    toks, order_ref, f_ref, p_ref, other_f_ref, other_p_ref, dm_ref, other_dm_ref, low_ref,
    high_ref, other_low_ref, other_high_ref, keep_a_ref, sent_a_ref, keep_b_ref, sent_b_ref,
    turned_ref, whole_ref, part_ref,
):
    k, half = pl.program_id(0), pl.program_id(1)
    total, width = f_ref.shape
    pieces = 2 * keep_a_ref.shape[0]
    blk = keep_a_ref.shape[1]

    @pl.when((k == 0) & (half == 0))
    def _():
        edges = ((low_ref[...], high_ref[...]), (other_low_ref[...], other_high_ref[...]))
        pairs = ((f_ref, p_ref), (other_f_ref, other_p_ref))
        for core, (pair, (low, high)) in enumerate(zip(pairs, edges)):
            for part, source in enumerate(pair):
                columns = slice(part * width, (part + 1) * width)
                middle = source[...]
                before, after = shifted(
                    middle.astype(F32),
                    toks,
                    low[:, :, columns].astype(F32),
                    high[:, :, columns].astype(F32),
                )
                for at, value in enumerate((before, middle, after)):
                    whole_ref[at, columns, :] = value.T
            for pos in range(pieces):
                start = pl.multiple_of(order_ref[pos] * blk, 16)
                for at in range(3):
                    turned_ref[
                        at, pos * blk : (pos + 1) * blk, core * total : (core + 1) * total
                    ] = whole_ref[at, pl.ds(start, blk), :]

    turned = turned_ref[k]
    part_ref[...] = dot(turned[:, :total], dm_ref[...], 1, 0) + dot(
        turned[:, total:], other_dm_ref[...], 1, 0
    )

    def put(keep_ref, sent_ref, kept, sent):
        for index, (one, other) in enumerate(zip(kept, sent)):
            keep_ref[index] = part_ref[one * blk : (one + 1) * blk, :].astype(BF16)
            sent_ref[index] = part_ref[other * blk : (other + 1) * blk, :].astype(BF16)

    at = 2 * k + half

    @pl.when(at < 3)
    def _():
        put(keep_a_ref, sent_a_ref, range(pieces // 2), range(pieces // 2, pieces))

    @pl.when(at >= 3)
    def _():
        put(keep_b_ref, sent_b_ref, range(0, pieces, 2), range(1, pieces, 2))


def conv_weight_call(order, own, other, dm, other_dm, edges, count):
    total, width = own[0].shape
    toks = total // edges[0].shape[0]
    blk = 2 * width // count
    out = (count // 4, 3 * blk, width)
    first = pl.BlockSpec((count // 4, blk, width), lambda k, h, *_: (0, jnp.minimum(2 * k + h, 2), 0))
    second = pl.BlockSpec(
        (count // 4, blk, width), lambda k, h, *_: (0, jnp.maximum(2 * k + h - 3, 0), 0)
    )
    columns = pl.BlockSpec((total, width), lambda k, h, *_: (0, h))
    plain = [*own, *other]
    keep_a, sent_a, keep_b, sent_b = launch(
        functools.partial(conv_weight_kernel, toks),
        (3, 2),
        [order],
        [*plain, dm, other_dm, *edges],
        [*[whole(v.shape) for v in plain], columns, columns, *[whole(v.shape) for v in edges]],
        [first, first, second, second],
        [stored(out, BF16)] * 4,
        [
            pltpu.VMEM((3, width, 2 * total), BF16),
            pltpu.VMEM((3, 2 * width, total), BF16),
            pltpu.VMEM((width, width), F32),
        ],
        cost(24 * total * width * width, 12 * width * width),
        "conv_weight",
    )
    return [[keep_a, sent_a], [keep_b, sent_b]]


def conv_back_kernel(
    toks, dm_ref, low_ref, high_ref, w_ref, d_tok_ref, d_char_ref, normal_ref, rstd_ref,
    norms_ref, d_proj_ref, d_ffn_ref, sums_ref, shift_ref, acc_ref,
):
    k, half = pl.program_id(0), pl.program_id(1)
    width = d_tok_ref.shape[1]

    @pl.when((half == 0) & (k == 0))
    def _():
        for part in range(2):
            columns = slice(part * width, (part + 1) * width)
            source = dm_ref[:, columns]
            before, after = shifted(
                source.astype(F32),
                toks,
                low_ref[:, :, columns].astype(F32),
                high_ref[:, :, columns].astype(F32),
            )
            shift_ref[part] = after
            shift_ref[2 + part] = source
            shift_ref[4 + part] = before

    product = dot(shift_ref[2 * k + half], flat_block(w_ref), 1, 1)

    @pl.when((k == 0) & (half == 0))
    def _():
        acc_ref[...] = product

    @pl.when((k > 0) | (half > 0))
    def _():
        acc_ref[...] += product

    @pl.when((k == 2) & (half == 1))
    def _():
        d_proj_ref[...] = (d_char_ref[...] + acc_ref[:, width:]).astype(BF16)
        gradient = d_tok_ref[...] + acc_ref[:, :width]
        normal = normal_ref[...]
        sums_ref[0:1, :] = column_sum(gradient * normal)
        sums_ref[1:2, :] = column_sum(gradient)
        d_ffn_ref[...] = norm_backward(normal, rstd_ref[...], norms_ref[1:2], gradient)


def conv_back_call(d_merged, low, high, packed, d_tok, d_char, normal1, rstd1, norms, seqs):
    total, width = d_tok.shape
    count = packed.shape[0]
    blk = 2 * width // count
    rows = (total, width)
    return launch(
        functools.partial(conv_back_kernel, total // seqs),
        (3, 2),
        [],
        [d_merged, low, high, packed, d_tok, d_char, normal1, rstd1, norms],
        [ whole(d_merged.shape), whole(low.shape), whole(high.shape), pl.BlockSpec((count, blk, width), lambda k, h: (0, 2 * k + h, 0)), whole(rows), whole(rows), whole(rows), whole(rstd1.shape), whole(norms.shape), ],
        [whole(rows), whole(rows), whole((2, width))],
        [shape(rows, BF16), shape(rows, F32), shape((2, width), F32)],
        [ pltpu.VMEM((6, total, width), BF16), pltpu.VMEM((total, 2 * width), F32), ],
        cost(24 * total * width * width, 24 * width * width + 20 * total * width),
        "conv_back",
    )


def rest_kernel(
    order_ref, table_ref, s_ref, w0_ref, w1_ref, send_ref, keep_ref, part_ref,
):
    count, blk, width = w0_ref.shape
    rows = part_ref.shape[0]
    turned = flat_block(table_ref).T
    sums = s_ref[...].reshape(rows, 2 * width)
    for part in range(2):
        part_ref[0:width, :] = dot(turned, sums[:, part * width : (part + 1) * width], 1, 0)
        place_blocks(part_ref.at[0:width], order_ref, send_ref, keep_ref, blk, part * blk)
    part_ref[...] = dot(sums[:, :width], flat_block(w0_ref), 1, 1) + dot(
        sums[:, width:], flat_block(w1_ref), 1, 1
    )
    place_blocks(part_ref, order_ref, send_ref, keep_ref, rows // count, 2 * blk)


def rest_call(order, packed, at_table, at_gru, sums, height):
    count, _, width = packed.shape
    blk = width // count
    rows = sums.shape[0] * sums.shape[1]
    table_rows = rows // count
    out = (count // 2, height, width)
    return launch(
        rest_kernel,
        (1,),
        [order],
        [packed, sums, packed, packed],
        [
            pl.BlockSpec((count, table_rows, width), lambda i, *_: (0, at_table, 0)),
            whole(sums.shape),
            pl.BlockSpec((count, blk, width), lambda i, *_: (0, at_gru, 0)),
            pl.BlockSpec((count, blk, width), lambda i, *_: (0, at_gru + 1, 0)),
        ],
        [whole(out), whole(out)],
        [stored(out, BF16), stored(out, BF16)],
        [pltpu.VMEM((rows, width), F32)],
        cost(8 * rows * width * width, 20 * width * width),
        "rest",
    )


def qkv_back_kernel(
    seqs, order_ref, d_ref, x_ref, w_ref, d_attn_ref,
    sums0_ref, sums1_ref, sums23_ref, bias_ref, bias_up_ref, out_ref, send_ref, keep_ref, xt_ref,
    dt_ref, part_ref, small_ref,
):
    j = pl.program_id(0)
    per = d_ref.shape[1]
    head, toks = d_ref.shape[3:]
    pieces, _, width = send_ref.shape
    blk = width // (2 * pieces)
    half = width // 2

    def put(row):
        for pos in range(2 * pieces):
            start = pl.multiple_of(order_ref[pos] * blk, 16)
            piece = part_ref[pl.ds(start, blk), :].astype(BF16)
            if pos < pieces:
                keep_ref[pos, row, :] = piece
            else:
                send_ref[pos - pieces, row, :] = piece

    @pl.when(j == 0)
    def _():
        xt_ref[...] = x_ref[...].T
        out_ref[...] = d_attn_ref[...]
        small_ref[...] = jnp.zeros_like(small_ref)
        for row, ref in enumerate((sums0_ref, sums1_ref)):
            small_ref[row : row + 1] = ref[0:1]
            small_ref[4 + row : 5 + row] = ref[1:2]
        for which in range(2):
            small_ref[2 + which : 3 + which] = sums23_ref[which, 0:1]
            small_ref[6 + which : 7 + which] = sums23_ref[which, 1:2]
        for part in range(2):
            own = slice(part * half, (part + 1) * half)
            small_ref[8:9, own] = bias_ref[:, part * width : part * width + half]
            small_ref[9:10, own] = bias_ref[:, part * width + half : (part + 1) * width]
        for part in range(bias_up_ref.shape[1] // width):
            small_ref[10 + part : 11 + part] = bias_up_ref[:, part * width : (part + 1) * width]
        small = small_ref[...].astype(BF16)
        for pos in range(pieces):
            keep_ref[pos, 3 * blk : 3 * blk + SMALL_ROWS, :] = small
            send_ref[pos, 3 * blk : 3 * blk + SMALL_ROWS, :] = small

    for s in range(seqs):
        for h in range(HEADS):
            pair = s * HEADS + h
            dt_ref[h * head : (h + 1) * head, s * toks : (s + 1) * toks] = d_ref[
                pair // per, pair % per, 0
            ]
    gradient = dt_ref[...].T
    part_ref[...] = dot(xt_ref[...], gradient, 1, 0)
    put(pl.ds(pl.multiple_of(j * blk, 16), blk))
    out_ref[...] += dot(gradient, flat_block(w_ref), 1, 1)


def qkv_back_call(
    order, d_qkv, rows, packed, base, d_attn, small, seqs, height
):
    count, per, _, head, toks = d_qkv.shape
    total, width = rows.shape
    blk = width // count
    out = (count // 2, height, width)
    rest = [d_attn, *small]
    return launch(
        functools.partial(qkv_back_kernel, seqs),
        (3,),
        [order],
        [d_qkv, rows, packed, *rest],
        [
            pl.BlockSpec((count, per, 1, head, toks), lambda j, *_: (0, 0, j, 0, 0)),
            whole(rows.shape),
            pl.BlockSpec((count, blk, width), lambda j, *_: (0, base + j, 0)),
            *[whole(v.shape) for v in rest],
        ],
        [whole((total, width)), whole(out), whole(out)],
        [stored((total, width), F32), stored(out, BF16), stored(out, BF16)],
        [
            pltpu.VMEM((width, total), BF16),
            pltpu.VMEM((width, total), BF16),
            pltpu.VMEM((width, width), F32),
            pltpu.VMEM((SMALL_ROWS, width), F32),
        ],
        cost(16 * total * width * width, 20 * width * width + 16 * total * width),
        "qkv_back",
    )


def pack_kernel(layout, *refs):
    ins, out_ref = refs[:-1], refs[-1]
    at = 0
    out_ref[...] = jnp.zeros_like(out_ref)
    width = out_ref.shape[1]
    for ref, row in zip(ins, layout):
        height, columns = ref.shape
        if columns < width:
            out_ref[row : row + height, :columns] = ref[...]
        else:
            for block in range(columns // width):
                out_ref[row + block * height : row + (block + 1) * height, :] = ref[
                    :, block * width : (block + 1) * width
                ]


def pack(arrays, layout, rows, width):
    return launch(
        functools.partial(pack_kernel, layout),
        (1,),
        [],
        arrays,
        [whole(v.shape) for v in arrays],
        whole((rows, width)),
        shape((rows, width), BF16),
        [],
        cost(0, 4 * rows * width),
        "pack",
    )


def swap(value, axis, bit):
    size = lax.axis_size(axis)
    return lax.ppermute(value, axis, [(i, i ^ (1 << bit)) for i in range(size)])


def add_low(kept, arrived):
    return (kept.astype(F32) + arrived.astype(F32)).astype(BF16)


def fold_kernel(keep_top, keep_bottom, came_top, came_bottom, ka_ref, sa_ref, kb_ref, sb_ref):
    half = ka_ref.shape[0]
    for index in range(half):
        ka_ref[index] = add_low(keep_top[index], came_top[index])
        sa_ref[index] = add_low(keep_top[half + index], came_top[half + index])
        kb_ref[index] = add_low(keep_bottom[2 * index], came_bottom[2 * index])
        sb_ref[index] = add_low(keep_bottom[2 * index + 1], came_bottom[2 * index + 1])


def tiles(rows):
    return 3 if PLACED and rows % 48 == 0 else 1


def fold_pieces_kernel(keep_top, keep_bottom, *refs):
    pieces = keep_top.shape[0]
    top, bottom, outs = refs[:pieces], refs[pieces : 2 * pieces], refs[2 * pieces :]
    ka_ref, sa_ref, kb_ref, sb_ref = outs
    half = pieces // 2
    for index in range(half):
        ka_ref[index] = add_low(keep_top[index], top[index][...])
        sa_ref[index] = add_low(keep_top[half + index], top[half + index][...])
        kb_ref[index] = add_low(keep_bottom[2 * index], bottom[2 * index][...])
        sb_ref[index] = add_low(keep_bottom[2 * index + 1], bottom[2 * index + 1][...])


def fold(keep, arrived):
    pieces, rows, width = keep.shape
    steps = tiles(rows // 2)
    tile = rows // 2 // steps
    top = pl.BlockSpec((pieces, tile, width), lambda i: (0, i, 0))
    bottom = pl.BlockSpec((pieces, tile, width), lambda i: (0, steps + i, 0))
    one_top = pl.BlockSpec((tile, width), lambda i: (i, 0))
    one_bottom = pl.BlockSpec((tile, width), lambda i: (steps + i, 0))
    ka, sa, kb, sb = launch(
        fold_pieces_kernel,
        (steps,),
        [],
        [keep, keep, *arrived, *arrived],
        [top, bottom] + [one_top] * pieces + [one_bottom] * pieces,
        [pl.BlockSpec((pieces // 2, tile, width), lambda i: (0, i, 0))] * 4,
        [stored((pieces // 2, rows // 2, width), BF16)] * 4,
        [],
        cost(pieces * rows * width, 6 * pieces * rows * width),
        "fold",
    )
    return [[ka, sa], [kb, sb]]


def send_links(state, step):
    bits = lax.axis_size("seq").bit_length() - 1
    return [
        [kept, swap(sent, "seq", bit)] for (kept, sent), bit in zip(state, (step, bits - step))
    ]


def split(state):
    pieces, rows, width = state[0][0].shape
    steps = tiles(rows)
    spec = pl.BlockSpec((pieces, rows // steps, width), lambda i, *_: (0, i, 0))
    out = pl.BlockSpec((pieces // 2, rows // steps, width), lambda i, *_: (0, i, 0))
    return plan(
        fold_kernel,
        (steps,),
        [],
        [state[0][0], state[1][0], state[0][1], state[1][1]],
        [spec] * 4,
        [out] * 4,
        [stored((pieces // 2, rows, width), BF16)] * 4,
        [],
        cost(pieces * rows * width, 12 * pieces * rows * width),
        "split",
    )


def paired(values):
    ka, sa, kb, sb = values
    return [[ka, sa], [kb, sb]]


def cross_kernel(place_ref, ka_ref, kb_ref, ca_ref, cb_ref, kept_ref, sent_ref):
    high = (place_ref[0] & 1) == 1
    first = add_low(ka_ref[0], ca_ref[0])
    second = add_low(kb_ref[0], cb_ref[0])
    kept_ref[...] = jnp.where(high, second, first)
    sent_ref[...] = jnp.where(high, first, second)


def cross(place, state):
    _, rows, width = state[0][0].shape
    steps = tiles(rows)
    spec = pl.BlockSpec((1, rows // steps, width), lambda i, *_: (0, i, 0))
    return plan(
        cross_kernel,
        (steps,),
        [place],
        [state[0][0], state[1][0], state[0][1], state[1][1]],
        [spec] * 4,
        [pl.BlockSpec((rows // steps, width), lambda i, *_: (i, 0))] * 2,
        [stored((rows, width), BF16)] * 2,
        [],
        cost(rows * width, 12 * rows * width),
        "cross",
    )


def halve_kernel(bit, place_ref, kept_ref, came_ref, next_ref, sent_ref):
    high = ((place_ref[0] >> bit) & 1) == 1
    rows = next_ref.shape[0]
    first = add_low(kept_ref[:rows], came_ref[:rows])
    second = add_low(kept_ref[rows:], came_ref[rows:])
    next_ref[...] = jnp.where(high, second, first)
    sent_ref[...] = jnp.where(high, first, second)


def halve(place, bit, kept, came):
    rows, width = kept.shape
    return plan(
        functools.partial(halve_kernel, bit),
        (1,),
        [place],
        [kept, came],
        [whole(kept.shape)] * 2,
        [whole((rows // 2, width))] * 2,
        [stored((rows // 2, width), BF16)] * 2,
        [],
        cost(rows * width, 6 * rows * width),
        "halve",
    )


def add_kernel(kept_ref, came_ref, out_ref):
    out_ref[...] = add_low(kept_ref[...], came_ref[...])


def add(kept, came):
    return plan(
        add_kernel,
        (1,),
        [],
        [kept, came],
        [whole(kept.shape)] * 2,
        whole(kept.shape),
        stored(kept.shape, BF16),
        [],
        cost(kept.size, 6 * kept.size),
        "add",
    )


def assemble_kernel(bit, place_ref, held_ref, came_ref, out_ref):
    high = ((place_ref[0] >> bit) & 1) == 1
    rows = held_ref.shape[0]
    held, came = held_ref[...], came_ref[...]
    out_ref[:rows] = jnp.where(high, came, held)
    out_ref[rows:] = jnp.where(high, held, came)


def assemble(place, bit, held, came):
    rows, width = held.shape
    return plan(
        functools.partial(assemble_kernel, bit),
        (1,),
        [place],
        [held, came],
        [whole(held.shape)] * 2,
        whole((2 * rows, width)),
        stored((2 * rows, width), BF16),
        [],
        cost(rows * width, 8 * rows * width),
        "assemble",
    )


def finish_kernel(layout, place_ref, held_ref, came_ref, *out_refs):
    high = (place_ref[0] & 1) == 1
    rows = held_ref.shape[0]
    for begin, size, out, index in layout:
        part = slice(begin % rows, begin % rows + size)
        held, came = held_ref[part].astype(F32), came_ref[part].astype(F32)
        out_refs[out][index] = jnp.where(high == (begin < rows), came, held)


def cut(layout, rows):
    for begin, size, out, index in layout:
        edges = [begin, begin + size]
        if begin < rows < begin + size:
            edges.insert(1, rows)
        for low, high in zip(edges, edges[1:]):
            yield low, high - low, out, index[:-2] + (slice(low - begin, high - begin), index[-1])


def finish(place, held, came, layout, outs):
    layout = list(cut(layout, held.shape[0]))
    return plan(
        functools.partial(finish_kernel, layout),
        (1,),
        [place],
        [held, came],
        [whole(held.shape)] * 2,
        [whole(dims) for dims in outs],
        [stored(dims, F32) for dims in outs],
        [],
        cost(held.size, 16 * held.size),
        "finish",
    )


def across_halves(place, kept, sent, layout, outs, merged=False):
    bits = lax.axis_size("batch").bit_length() - 1
    came = swap(sent, "batch", 0)
    halved = bits - 1 if merged else bits
    for bit in range(1, halved):
        kept, sent = yield halve(place, bit, kept, came)
        came = swap(sent, "batch", bit)
    (held,) = yield add(kept, came)
    for bit in range(halved, bits):
        (held,) = yield add(held, swap(held, "batch", bit))
    for bit in reversed(range(halved)):
        came = swap(held, "batch", bit)
        if bit:
            (held,) = yield assemble(place, bit, held, came)
    return (yield finish(place, held, came, layout, outs))


def deal_kernel(place_ref, ka_ref, kb_ref, ca_ref, cb_ref, *refs):
    outs, sum_ref = refs[:-1], refs[-1]
    rows, part = ka_ref.shape[1], outs[0].shape[0]
    sum_ref[:rows] = add_low(ka_ref[0], ca_ref[0])
    sum_ref[rows:] = add_low(kb_ref[0], cb_ref[0])
    for mask, out_ref in enumerate(outs):
        start = pl.multiple_of((place_ref[0] ^ mask) * part, 16)
        out_ref[...] = sum_ref[pl.ds(start, part), :]


def total_kernel(*refs):
    total = refs[0][...].astype(F32)
    for ref in refs[1:-1]:
        total += ref[...].astype(F32)
    refs[-1][...] = total.astype(BF16)


def spread_kernel(layout, small_at, parts, place_ref, me_ref, *refs):
    ins, outs, all_ref = refs[:parts], refs[parts:-1], refs[-1]
    rows = ins[0].shape[0]
    for mask, ref in enumerate(ins):
        start = pl.multiple_of((place_ref[0] ^ mask) * rows, 16)
        all_ref[pl.ds(start, rows), :] = ref[...]
    for begin, size, out, index in layout:
        outs[out][index] = all_ref[begin : begin + size].astype(F32)
    blk, share = outs[-5].shape[1], outs[-1].shape[1]
    small = all_ref[small_at : small_at + SMALL_ROWS].astype(F32)
    width = small.shape[1]
    me = me_ref[0]
    mine = pltpu.roll(small, lax.rem(width - me * blk, width), 1)[:, :blk]
    outs[-5][...] = mine[0:4]
    outs[-4][...] = mine[4:8]
    outs[-3][...] = mine[8:9]
    outs[-2][...] = mine[9:10]
    spot = me * share
    turned = pltpu.roll(small, lax.rem(width - lax.rem(spot, width), width), 1)[:, :share]
    row = lax.broadcasted_iota(jnp.int32, turned.shape, 0)
    outs[-1][...] = column_sum(jnp.where(row == 10 + lax.div(spot, width), turned, 0.0))


def across_direct(place, me, state, layout, small_at, outs):
    for link in range(2, lax.axis_size("seq").bit_length() - 1):
        state = send_links(paired((yield split(state))), link)
    parts = lax.axis_size("batch")
    _, rows, width = state[0][0].shape
    part = (2 * rows // parts, width)
    ends = [(mask, [(i, i ^ mask) for i in range(parts)]) for mask in range(1, parts)]
    pieces = yield plan(
        deal_kernel,
        (1,),
        [place],
        [state[0][0], state[1][0], state[0][1], state[1][1]],
        [whole(state[0][0].shape)] * 4,
        [whole(part)] * parts,
        [stored(part, BF16)] * parts,
        [pltpu.VMEM((2 * rows, width), BF16)],
        cost(rows * width, 12 * rows * width),
        "deal",
    )
    came = [lax.ppermute(pieces[mask], "batch", pairs) for mask, pairs in ends]
    (held,) = yield plan(
        total_kernel,
        (1,),
        [],
        [pieces[0], *came],
        [whole(part)] * parts,
        [whole(part)],
        [stored(part, BF16)],
        [],
        cost(rows * width, 5 * rows * width),
        "total",
    )
    came = [lax.ppermute(held, "batch", pairs) for _, pairs in ends]
    return (
        yield plan(
            functools.partial(spread_kernel, layout, small_at, parts),
            (1,),
            [place, me],
            [held, *came],
            [whole(part)] * parts,
            [whole(dims) for dims in outs],
            [stored(dims, F32) for dims in outs],
            [pltpu.VMEM((2 * rows, width), BF16)],
            cost(rows * width, 12 * rows * width),
            "spread",
        )
    )


def neighbours(first, last):
    count = lax.axis_size("seq")
    up = [(i, i + 1) for i in range(count - 1)]
    down = [(target, source) for source, target in up]
    return lax.ppermute(last, "seq", up), lax.ppermute(first, "seq", down)


def local(
    hidden, char_ids, group_ids, word_lengths, qkv_weight, out_weight, up_weight, ffn_bias,
    down_weight, gru_weight, gate_bias, candidate_bias, char_weight, conv_weight, char_table,
    norm_gain, norm_shift, tok_grad, char_grad,
):
    count = lax.axis_size("seq")
    bits = count.bit_length() - 1
    me = lax.axis_index("seq").astype(jnp.int32)
    seqs, toks, width = hidden.shape
    total = seqs * toks
    half = width // 2
    blk = width // count
    share = ffn_bias.shape[0]
    table_rows = char_table.shape[0]
    chars = char_ids.shape[1]
    reverse = [int(format(i, f"0{bits}b")[::-1], 2) for i in range(count)]
    order = jnp.asarray(reverse, jnp.int32) ^ me
    slot = sum(
        (((jnp.arange(count, dtype=jnp.int32) ^ me) >> b) & 1) << (bits - 1 - b) for b in range(bits)
    )
    me_one = me.reshape(1)

    place = lax.axis_index("batch").astype(jnp.int32).reshape(1)
    LATEST.clear()
    PLACED[:] = [True]
    NEAR.clear()

    table_at = share
    small_at = table_at + table_rows
    block_at = small_at + 16
    block_at += -block_at % blk
    pack_rows = block_at + 11 * blk
    small = jnp.concatenate(
        [norm_gain.T, norm_shift.T, gate_bias[None], candidate_bias[None]], 0
    )
    small = jnp.pad(small, ((0, 6), (0, width - blk)))
    small = small.at[10, :share].set(ffn_bias)
    arrays = [
        down_weight, char_table, small, gru_weight, qkv_weight, char_weight, out_weight, up_weight
    ]
    at_block = block_at // blk
    at_gru, at_qkv, at_char, at_out, at_up = (at_block + i for i in (0, 2, 5, 6, 7))
    layout = [0, table_at, small_at] + [i * blk for i in (at_gru, at_qkv, at_char, at_out, at_up)]
    at_table, at_down = table_at // table_rows, 0
    first = pack(arrays, layout, pack_rows, width)
    third = pack(
        [conv_weight[k] for k in range(3)], [k * 4 * blk for k in range(3)], 12 * blk, width
    )
    first = lax.all_gather(first, "seq", axis=0)
    third = lax.all_gather(third, "seq", axis=0)
    vectors = (
        first[:, small_at : small_at + 10, :blk].astype(F32).transpose(1, 0, 2).reshape(10, width)
    )
    bias_up = first[:, small_at + 10, :share].astype(F32).reshape(1, -1)
    norms = vectors

    rows = hidden.reshape(total, width)
    words = word_lengths.reshape(seqs, toks)
    ends = jnp.cumsum(words, axis=1)
    starts = ends - words
    lens = words.astype(F32)[..., None]

    qkv = qkv_call(rows, first, at_qkv, seqs, count)
    qkv = lax.all_to_all(qkv, "seq", 0, 0, tiled=True)
    z, c, block_totals = gates_call(group_ids, char_ids, first, at_gru, at_table, vectors)
    gathered = [block_totals] + [
        lax.ppermute(block_totals, "seq", [(i, i ^ mask) for i in range(count)])
        for mask in range(1, count)
    ]
    step = (1 << 19) // (count * toks)
    mixture, totals = attend_call(qkv, 2 * step)
    mixture = lax.all_to_all(mixture, "seq", 0, 0, tiled=True)
    gathered = collect(me_one, gathered)
    prior, pooled, proj, proj_low = states_call(
        me_one, z, c, gathered, starts[..., None], ends[..., None], lens, first, at_char, 2
    )
    mix_t, normal0, rstd0, normed, active, slope, normal1, rstd1, f_low = ffn_call(
        mixture, rows, first, at_out, at_up, at_down, bias_up, norms, seqs
    )

    def edges(left, right):
        joined = [v.reshape(seqs, toks, width) for v in (left, right)]
        return (
            jnp.concatenate([v[:, :1] for v in joined], -1),
            jnp.concatenate([v[:, -1:] for v in joined], -1),
        )

    begin, end = edges(f_low, proj_low)
    low, high = neighbours(begin, end)
    other = [swap(v, "seq", 0) for v in (f_low, proj_low)]
    tok_out, char_out, d_tok, d_char, d_merged, sums23, begin, end, *other = conv_call(
        f_low, proj_low, normal1, proj, norms, low, high, third,
        tok_grad.reshape(total, width), char_grad.reshape(total, width), seqs, other,
    )

    joined_edges = [low, high, swap(low, "seq", 0), swap(high, "seq", 0)]
    low, high = neighbours(begin, end)
    other_dm = swap(d_merged, "seq", 0)

    def onward(state, first_link):
        for link in range(first_link + 1, bits):
            ((values,), _) = together([split(state)])
            state = send_links(paired(values), link)
        return state

    def columns_of(begin, blocks, out):
        return [
            (begin + j * blk, blk, out, (slice(None), slice(j * width, (j + 1) * width)))
            for j in range(blocks)
        ]

    everything = (slice(None), slice(None))
    double = 2 * blk
    batch_bits = lax.axis_size("batch").bit_length() - 1
    unit = 8 * lax.axis_size("batch")
    height = max(2 * blk + table_rows, 3 * blk + SMALL_ROWS)
    height += -height % unit
    d_proj, d_ffn, sums1 = conv_back_call(
        d_merged, low, high, third, d_tok, d_char, normal1, rstd1, norms, seqs
    )
    conv_state = conv_weight_call(
        order, (f_low, proj_low), other, d_merged, other_dm, joined_edges, count
    )
    conv_state = send_links(conv_state, 1)
    ds, back_totals = states_back_call(
        d_proj, first, at_char, lens, starts[:, None, :], ends[:, None, :], z
    )
    send, keep, d_bias_up, d_attn, sums0, d_mix = ffn_back_call(
        slot, order, d_ffn, active, slope, normed, normal0, rstd0, norms, first, at_out, at_up,
        at_down, back_totals, mix_t, pooled, d_proj, seqs,
    )
    d_mix = lax.all_to_all(d_mix, "seq", 0, 0, tiled=True)
    ffn_came = [swap(piece, "seq", 0) for piece in send]
    conv_state = onward(conv_state, 1)
    ffn_state = fold(keep, ffn_came)
    ffn_state = send_links(ffn_state, 1)
    d_qkv = attend_back_call(qkv, d_mix, totals, step)
    PLACED.clear()
    d_qkv = lax.all_to_all(d_qkv, "seq", 0, 0, tiled=True)
    ((halves,), _) = together([cross(place, conv_state)])
    conv_run = Steps(
        across_halves(
            place, *halves,
            [
                (
                    r * double, double, 0,
                    (r // 2, slice(None), slice(r % 2 * width, (r % 2 + 1) * width)),
                )
                for r in range(6)
            ],
            [(3, double, 2 * width)],
        )
    )
    sums, d_bias = gates_back_call(
        me_one, group_ids, z, c, prior, ds, gathered, d_mix, char_ids,
        count * table_rows // NCHAR, 2,
    )
    ffn_state = onward(ffn_state, 1)
    for _ in range(1, batch_bits):
        advance(conv_run)
    rest_send, rest_keep = rest_call(order, first, at_table, at_gru, sums, height)
    hidden_grad, qkv_send, qkv_keep = qkv_back_call(
        order, d_qkv, rows, first, at_qkv, d_attn,
        [sums0, sums1, sums23, d_bias, d_bias_up], seqs, height,
    )
    PLACED.clear()
    (halves, (held,)), (rest_send, qkv_send) = together(
        [cross(place, ffn_state), conv_run.plan], [rest_send, qkv_send]
    )
    conv_run.resume([held])
    ffn_run = Steps(
        across_halves(
            place, *halves,
            [
                (0, share, 0, everything),
                *columns_of(share, 4, 1),
                (share + 4 * blk, blk, 2, everything),
                (share + 5 * blk, blk, 3, everything),
            ],
            [(share, width), (blk, 4 * width), (blk, width), (blk, width)], True,
        )
    )
    rest_came, qkv_came = (swap(send, "seq", 0) for send in (rest_send, qkv_send))
    ((values,), _) = together([split([[rest_keep, rest_came], [qkv_keep, qkv_came]])])
    last_run = Steps(
        across_direct(
            place, me_one, send_links(paired(values), 1),
            [
                *columns_of(0, 2, 0),
                (2 * blk, table_rows, 1, everything),
                *columns_of(height, 3, 2),
            ],
            height + 3 * blk,
            [
                (blk, 2 * width), (table_rows, width), (blk, 3 * width),
                (4, blk), (4, blk), (1, blk), (1, blk), (1, share),
            ],
        )
    )
    advance(conv_run, ffn_run, last_run)
    advance(last_run)
    while conv_run.plan or ffn_run.plan or last_run.plan:
        advance(conv_run, ffn_run, last_run)
    (conv_grad,) = conv_run.result
    down_grad, up_grad, out_grad, char_grad_w = ffn_run.result
    gru_grad, table_grad, qkv_grad, *small_grads = last_run.result
    d_gain, d_shift = (v.T for v in small_grads[:2])
    d_gate_b, d_cand_b, d_ffn_b = (v.reshape(-1) for v in small_grads[2:])
    shape_out = (seqs, toks, width)
    return (
        tok_out.reshape(shape_out),
        char_out.reshape(shape_out),
        hidden_grad.reshape(shape_out),
        qkv_grad,
        out_grad,
        up_grad,
        d_ffn_b,
        down_grad,
        gru_grad,
        d_gate_b,
        d_cand_b,
        char_grad_w,
        conv_grad,
        table_grad,
        d_gain,
        d_shift,
    )


def solution(mesh):
    rows, columns = P("seq", None), P("batch", "seq", None)
    return jax.shard_map(
        local,
        mesh=mesh,
        in_specs=(
            columns, P("batch", "seq"), P("batch"), columns, rows, rows, rows, P("seq"), rows,
            rows, P("seq"), P("seq"), rows, P(None, "seq", None), rows, rows, rows, columns,
            columns,
        ),
        out_specs=(
            columns, columns, columns, rows, rows, rows, P("seq"), rows, rows, P("seq"), P("seq"),
            rows, P(None, "seq", None), rows, rows, rows,
        ),
        check_vma=False,
    )
```
